512 devices in a mesh: space: 32 (over x, z_lo, core), vel: 16 (over z_hi, y).
Axes of the slice: x: 4, y: 4, z: 16 (z_hi: 4, z_lo: 4; z = z_hi * 4 + z_lo), core: 2. Of those that a mesh axis runs over, the one named last changes fastest.
Arguments:
- distribution: float32 [512, 48, 2304], P('space', 'vel'), may hold values from 0 to 5.4, as said below
- freestream: float32 [48, 2304], P('vel'), may hold values from 0 to 3, as said below
- face_area: float32 [3, 6, 512], P(None, None, 'space'), may hold values from -2.5 to 2.5
- cell_volume: float32 [512], P('space'), may hold values from 1 to 3
- neighbours: int32 [6, 512], P(None, 'space'), may hold values from 0 to 23
- wall_flags: int32 [6, 512], P(None, 'space'), may hold values 0 or 1
- send_cells: int32 [2, 128], P(None, 'space'), may hold values from 0 to 15, as said below
Outputs:
- new_distribution: float32 [512, 48, 2304], P('space', 'vel')
The draws below stay inside these ranges and needn't reach their ends.
Inputs may be any that keep to these rules, and one draw needn't show every extreme that they name: `distribution`: smooth in no direction; nonnegative, with a positive sum over velocities in every cell. `freestream`: nonnegative. `send_cells`: a local cell index of the sending block; distinct within each row of one block. `neighbours`: rows below 16 are the block's own cells, then 4 rows from the block below, then 4 from the block above; unused where the face is a wall.
All inputs are finite; a program needn't handle non-finite values. No bound on the sum of `wall_flags` on one device may be relied on, other than what follows from the above.
Results may differ from the reference program's by a relative error of at most 0.0003.
Values sent between devices are 32-bit elements; how exact they have to be, the bound alone decides.
A program may use at most 64 MiB of HBM per device.

```python
import math
import jax
import jax.numpy as jnp
from jax import lax

NV = 48
FPC = 6
SUBSTEPS = 2
CELLS_DEV = 16
HALO = 4
GRID_SITE_COUNT = 512


def velocity_line():
    return (jnp.arange(NV).astype(jnp.float32) - (NV - 1) / 2.0) * 0.25


def draw_distribution(key, part):
    key = jax.random.fold_in(key, 3)
    random_subseeds = jax.random.split(key, 4)
    rough_low, rough_high, drift_bound = (0.5, 1.5, 1.5)
    particle_concentration = jnp.exp(jax.random.uniform(random_subseeds[0], (GRID_SITE_COUNT, 1, 1), jnp.float32, math.log(0.3), math.log(3.0)))
    drift_vec = jax.random.uniform(random_subseeds[1], (3, GRID_SITE_COUNT, 1, 1), jnp.float32, -drift_bound, drift_bound)
    kinetic_heat_level = jnp.exp(jax.random.uniform(random_subseeds[2], (GRID_SITE_COUNT, 1, 1), jnp.float32, math.log(0.5), math.log(1.5)))
    line = velocity_line()
    grid_x = line[None, :, None]
    grid_y = jnp.repeat(line, NV)[None, None, :]
    grid_z = jnp.tile(line, NV)[None, None, :]
    heat_velocity_width = (grid_x - drift_vec[0]) ** 2 + (grid_y - drift_vec[1]) ** 2 + (grid_z - drift_vec[2]) ** 2
    boundary_jaggedness = jax.random.uniform(random_subseeds[3], (GRID_SITE_COUNT, NV, NV * NV), jnp.float32, rough_low, rough_high)
    return particle_concentration * jnp.exp(-heat_velocity_width / (2.0 * kinetic_heat_level)) * boundary_jaggedness


def draw_freestream(key, part):
    key = jax.random.fold_in(key, 5)
    random_subseeds = jax.random.split(key, 4)
    rough_low, rough_high = (0.8, 1.2)
    speed = jax.random.uniform(random_subseeds[0], (), jnp.float32, 2.5, 3.5)
    kinetic_heat_level = jax.random.uniform(random_subseeds[1], (), jnp.float32, 0.3, 0.6)
    ripple_height = jax.random.uniform(random_subseeds[2], (), jnp.float32, 1.0, 2.0)
    line = velocity_line()
    grid_x = line[:, None]
    grid_y = jnp.repeat(line, NV)[None, :]
    grid_z = jnp.tile(line, NV)[None, :]
    heat_velocity_width = (grid_x - speed) ** 2 + grid_y ** 2 + grid_z ** 2
    boundary_jaggedness = jax.random.uniform(random_subseeds[3], (NV, NV * NV), jnp.float32, rough_low, rough_high)
    return ripple_height * jnp.exp(-heat_velocity_width / (2.0 * kinetic_heat_level)) * boundary_jaggedness


def draw_send_cells(key, part):
    key = jax.random.fold_in(key, 7)
    blocks = GRID_SITE_COUNT // CELLS_DEV
    positions = jnp.arange(CELLS_DEV, dtype=jnp.int32)

    def one_list(side_row, block_id):
        subkey = jax.random.fold_in(jax.random.fold_in(key, side_row + 17), block_id)
        scores = jax.random.randint(subkey, (CELLS_DEV,), 0, 4096, dtype=jnp.int32) * CELLS_DEV + positions
        forced = (block_id == 0) & ((positions == CELLS_DEV - 1) | (positions == 0) & (side_row == 0))
        scores = jnp.where(forced, scores + 2 ** 24, scores)
        return lax.top_k(scores, HALO)[1].astype(jnp.int32)
    block_ids = jnp.arange(blocks, dtype=jnp.int32)

    def per_row(side_row):
        return jax.vmap(lambda block_id: one_list(side_row, block_id))(block_ids)
    listing = jax.vmap(per_row)(jnp.arange(2, dtype=jnp.int32))
    return listing.reshape(2, blocks * HALO)


def with_ends(entries, own_key, least, largest):
    index_at = [jax.random.randint(jax.random.fold_in(own_key, axis), (), 0, length) for axis, length in enumerate(entries.shape)]
    widest = entries.shape.index(max(entries.shape))
    next_to = index_at[:widest] + [(index_at[widest] + 1) % entries.shape[widest]] + index_at[widest + 1:]
    return entries.at[tuple(index_at)].set(least).at[tuple(next_to)].set(largest)


def block_levels(key, extent, pieces, least, largest):
    def one(dim, parts):
        draws = jax.random.uniform(jax.random.fold_in(jax.random.fold_in(key, 6), dim), (parts,), jnp.float32, least / len(pieces), largest / len(pieces))
        return jnp.repeat(jnp.exp(draws), extent[dim] // parts).reshape((-1,) + (1,) * (len(extent) - dim - 1))

    loudness = one(*pieces[0])
    for cut in pieces[1:]:
        loudness = loudness * one(*cut)
    return loudness


def centred(rng, shape, scale, most, pieces=(), kind=jnp.bfloat16):
    level = block_levels(rng, shape, pieces, -0.22, 0.18) if pieces else 1.0
    drawn = jax.random.normal(rng, shape, jnp.float32) * scale * level
    return jnp.minimum(jnp.maximum(drawn, -most), most).astype(kind)


def setup_inputs(seed: int = 0) -> dict:
    streams_of = jax.random.split(jax.random.key(seed), 8)
    distribution = draw_distribution(jax.random.fold_in(streams_of[7], 71), 0)
    freestream = draw_freestream(jax.random.fold_in(streams_of[7], 71), 0)
    face_area = centred(streams_of[2], (3, FPC, GRID_SITE_COUNT), 1.0, 2.5, ((2, 32),), jnp.float32)
    cell_volume = jnp.clip(jnp.exp(math.log(3.0) - 1.0986123 * jax.random.uniform(streams_of[3], (GRID_SITE_COUNT,), jnp.float32) ** block_levels(streams_of[3], (GRID_SITE_COUNT,), ((0, 32),), -0.2, 0.2)), 1.0, 3.0)
    neighbours = with_ends(jax.random.randint(streams_of[4], (FPC, GRID_SITE_COUNT), 0, CELLS_DEV + 2 * HALO), jax.random.fold_in(streams_of[4], 1), 0, (CELLS_DEV + 2 * HALO) - 1).astype(jnp.int32)
    wall_flags = with_ends((jax.random.randint(streams_of[5], (FPC, GRID_SITE_COUNT), 0, 6) < 1).astype(jnp.int32), jax.random.fold_in(streams_of[5], 1), 0, 1)
    send_cells = draw_send_cells(jax.random.fold_in(streams_of[7], 71), 0)
    return dict(distribution=distribution, freestream=freestream, face_area=face_area, cell_volume=cell_volume, neighbours=neighbours, wall_flags=wall_flags, send_cells=send_cells)


GRID_STEP = 0.25
TIME_STEP = 0.02
WALL_TEMP = 1.0
COLLISION_SCALE = 0.002
MU_POWER_LAW = 0.81
ANISO_MIX_WEIGHT = 0.5


def grid_axis(points, first_point):
    return ((jnp.arange(points) + first_point).astype(jnp.float32) - (NV - 1) / 2.0) * GRID_STEP


def plane_axes():
    grid_line = grid_axis(NV, 0)
    return jnp.repeat(grid_line, NV), jnp.tile(grid_line, NV)


def moment_weights(plane_vel, grid_y, grid_z):
    unity_grid = jnp.ones((plane_vel.shape[0], grid_y.shape[0]), jnp.float32)
    vel_x = plane_vel[:, None] * unity_grid
    vel_y = grid_y[None, :] * unity_grid
    vel_z = grid_z[None, :] * unity_grid
    return jnp.stack([unity_grid, vel_x, vel_y, vel_z, vel_x * vel_x, vel_y * vel_y, vel_z * vel_z,
                      vel_x * vel_y, vel_x * vel_z, vel_y * vel_z])


def moment_sums(values, weights):
    return jnp.einsum("cxj,mxj->mc", values, weights, precision=lax.Precision.HIGHEST)


def per_cell(values):
    return values[:, None, None]


def shift_flat(values, offset):
    filler = jnp.zeros(values.shape[:-1] + (abs(offset),), values.dtype)
    if offset > 0:
        return jnp.concatenate([values[..., offset:], filler], axis=-1)
    return jnp.concatenate([filler, values[..., :offset]], axis=-1)


def fp_update(padded, plane_ext, grid_y, grid_z, moments_sum):
    flat_size = padded.shape[-1]
    z_index = jnp.arange(flat_size) % NV
    keep_up = (z_index < NV - 1).astype(padded.dtype)
    keep_down = (z_index > 0).astype(padded.dtype)

    def along_y(values, offset):
        return shift_flat(values, offset * NV)

    def along_z(values, offset):
        return shift_flat(values, offset) * (keep_up if offset > 0 else keep_down)

    mass_sum = moments_sum[0]
    particle_concentration = GRID_STEP ** 3 * mass_sum
    mean_x = moments_sum[1] / mass_sum
    mean_y = moments_sum[2] / mass_sum
    mean_z = moments_sum[3] / mass_sum
    second_moment_horizontal = moments_sum[4] / mass_sum - mean_x * mean_x
    second_moment_lateral = moments_sum[5] / mass_sum - mean_y * mean_y
    second_moment_vertical = moments_sum[6] / mass_sum - mean_z * mean_z
    cov_xy = moments_sum[7] / mass_sum - mean_x * mean_y
    cov_xz = moments_sum[8] / mass_sum - mean_x * mean_z
    cov_yz = moments_sum[9] / mass_sum - mean_y * mean_z
    kinetic_heat_level = (second_moment_horizontal + second_moment_lateral + second_moment_vertical) / 3.0
    collision_frequency = COLLISION_SCALE * particle_concentration * kinetic_heat_level ** (1.0 - MU_POWER_LAW)
    centre = padded[:, 1:-1]
    next_plane = padded[:, 2:]
    prev_plane = padded[:, :-2]
    drift_x = (plane_ext[2:][None, :, None] - per_cell(mean_x)) * next_plane \
        - (plane_ext[:-2][None, :, None] - per_cell(mean_x)) * prev_plane
    flow_y = (grid_y[None, None, :] - per_cell(mean_y)) * centre
    drift_y = along_y(flow_y, 1) - along_y(flow_y, -1)
    flow_z = (grid_z[None, None, :] - per_cell(mean_z)) * centre
    drift_z = along_z(flow_z, 1) - along_z(flow_z, -1)
    drift = (drift_x + drift_y + drift_z) / (2.0 * GRID_STEP)
    doubled = 2.0 * centre
    second_xx = next_plane - doubled + prev_plane
    up_y = along_y(centre, 1)
    down_y = along_y(centre, -1)
    second_yy = up_y + down_y - doubled
    second_zz = along_z(centre, 1) + along_z(centre, -1) - doubled
    second_xy = (along_y(next_plane, 1) - along_y(next_plane, -1) - along_y(prev_plane, 1) + along_y(prev_plane, -1)) / 4.0
    second_xz = (along_z(next_plane, 1) - along_z(next_plane, -1) - along_z(prev_plane, 1) + along_z(prev_plane, -1)) / 4.0
    second_yz = (along_z(up_y, 1) - along_z(up_y, -1) - along_z(down_y, 1) + along_z(down_y, -1)) / 4.0
    spherical_share = (1.0 - ANISO_MIX_WEIGHT) * kinetic_heat_level
    diffusion = per_cell(spherical_share + ANISO_MIX_WEIGHT * second_moment_horizontal) * second_xx \
        + per_cell(spherical_share + ANISO_MIX_WEIGHT * second_moment_lateral) * second_yy \
        + per_cell(spherical_share + ANISO_MIX_WEIGHT * second_moment_vertical) * second_zz \
        + 2.0 * ANISO_MIX_WEIGHT * (per_cell(cov_xy) * second_xy + per_cell(cov_xz) * second_xz + per_cell(cov_yz) * second_yz)
    return centre + per_cell(collision_frequency) * (drift + diffusion / (GRID_STEP * GRID_STEP))


def reference(distribution, freestream, face_area, cell_volume, neighbours, wall_flags, send_cells):
    blocks = GRID_SITE_COUNT // CELLS_DEV
    grid_y, grid_z = plane_axes()
    plane_vel = grid_axis(NV, 0)
    plane_ext = grid_axis(NV + 2, -1)
    weights = moment_weights(plane_vel, grid_y, grid_z)
    maxwell = jnp.exp(-(plane_vel[:, None] ** 2 + grid_y[None, :] ** 2 + grid_z[None, :] ** 2) / (2.0 * WALL_TEMP))
    far_field = jnp.broadcast_to(freestream, (HALO, NV, NV * NV))

    def sent(block_id, side_row):
        clipped = jnp.clip(block_id, 0, blocks - 1).astype(jnp.int32)
        picked = lax.dynamic_slice_in_dim(send_cells[side_row], clipped * HALO, HALO, 0)
        source = lax.dynamic_slice_in_dim(distribution, clipped * CELLS_DEV, CELLS_DEV, 0)
        return source[picked]

    def one_block(block_id):
        start = (block_id * CELLS_DEV).astype(jnp.int32)
        local = lax.dynamic_slice_in_dim(distribution, start, CELLS_DEV, 0)
        below_rows = jnp.where(block_id == 0, far_field, sent(block_id - 1, 1))
        above_rows = jnp.where(block_id == blocks - 1, far_field, sent(block_id + 1, 0))
        extended = jnp.concatenate([local, below_rows, above_rows], axis=0)
        block_area = lax.dynamic_slice_in_dim(face_area, start, CELLS_DEV, 2)
        block_volume = lax.dynamic_slice_in_dim(cell_volume, start, CELLS_DEV, 0)
        block_neighbours = lax.dynamic_slice_in_dim(neighbours, start, CELLS_DEV, 1)
        block_wall = lax.dynamic_slice_in_dim(wall_flags, start, CELLS_DEV, 1)
        flux_sum = jnp.zeros_like(local)
        for face_slot in range(FPC):
            normal_vel = per_cell(block_area[0, face_slot]) * plane_vel[None, :, None] \
                + per_cell(block_area[1, face_slot]) * grid_y[None, None, :] \
                + per_cell(block_area[2, face_slot]) * grid_z[None, None, :]
            out_flux = jnp.sum(jnp.maximum(normal_vel, 0.0) * local, axis=(1, 2)) * GRID_STEP ** 3
            in_flux = jnp.sum(jnp.maximum(-normal_vel, 0.0) * maxwell[None], axis=(1, 2)) * GRID_STEP ** 3
            wall_in = per_cell(out_flux / in_flux) * maxwell[None]
            upwind_side = jnp.where(per_cell(block_wall[face_slot]) == 1, wall_in, extended[block_neighbours[face_slot]])
            flux_sum = flux_sum + jnp.maximum(normal_vel, 0.0) * local + jnp.minimum(normal_vel, 0.0) * upwind_side
        moved = local - TIME_STEP * flux_sum / per_cell(block_volume)
        for substep in range(SUBSTEPS):
            moments_sum = moment_sums(moved, weights)
            padded = jnp.pad(moved, ((0, 0), (1, 1), (0, 0)))
            moved = fp_update(padded, plane_ext, grid_y, grid_z, moments_sum)
        return moved

    result = lax.map(one_block, jnp.arange(blocks))
    return result.reshape(GRID_SITE_COUNT, NV, NV * NV)
```

```python
import functools

import jax
import jax.numpy as jnp
from jax import lax
from jax.experimental import pallas as pl
from jax.experimental.pallas import tpu as pltpu
from jax.sharding import PartitionSpec as P

NV = 48
FLAT = NV * NV
STEP = 0.25
DT = 0.02
RATE = 0.002
FACES = 6
HALO = 4
CELLS = 16
PLANES = 3
MARGIN = 128
WIDE = FLAT + 2 * MARGIN
VELS = 16
MESH = pl.DeviceIdType.MESH
F32 = jnp.float32
BF16 = jnp.bfloat16


def split2(x):
    hi = x.astype(BF16)
    return hi, (x - hi.astype(F32)).astype(BF16)


def split3(x):
    hi = x.astype(BF16)
    r = x - hi.astype(F32)
    mid = r.astype(BF16)
    return hi, mid, (r - mid.astype(F32)).astype(BF16)


def lane_sums(acc):
    ones = jnp.ones((16, 128), BF16)
    total = None
    for part in split3(acc):
        term = lax.dot_general(ones, part, (((1,), (1,)), ((), ())), preferred_element_type=F32)
        total = term if total is None else total + term
    return total[0:1]


def spread(row, sel):
    k = row.shape[1]
    lane = lax.broadcasted_iota(jnp.int32, (CELLS, k), 1)
    cell = lax.broadcasted_iota(jnp.int32, (CELLS, k), 0)
    own = jnp.where((lane & (CELLS - 1)) == cell, jnp.broadcast_to(row, (CELLS, k)), 0.0)
    stacked = jnp.concatenate(split3(own), axis=0)
    out = jnp.dot(stacked, sel, preferred_element_type=F32)
    return out[0:16] + out[16:32] + out[32:48]


def rep(x, n):
    return jnp.concatenate([x] * n, axis=1)


def kernel(
    dist, free, area, vol, nb, wall, send, out,
    distv, hs, hr, fa, fb, fc, yt, zt, mt, prm, sb, lhs, sel, fsend, frecv, msend, mrecv,
    in_sem, out_sem, h_ssem, h_rsem, f_ssem, f_rsem, m_ssem, m_rsem, p_ssem, p_rsem,
):
    space = lax.axis_index("space")
    vel = lax.axis_index("vel")
    blocks = lax.axis_size("space")
    has_below, has_above = space > 0, space < blocks - 1
    has_left, has_right = vel > 0, vel < VELS - 1

    loads = [pltpu.make_async_copy(dist.at[p], distv.at[p], in_sem.at[p]) for p in range(PLANES)]
    for copy in loads:
        copy.start()

    barrier = pltpu.get_barrier_semaphore()
    for d in range(1, VELS):
        pl.semaphore_signal(barrier, 1, device_id=(space, lax.rem(vel + d, VELS)), device_id_type=MESH)

    @pl.when(has_below)
    def _():
        pl.semaphore_signal(barrier, 1, device_id=(space - 1, vel), device_id_type=MESH)

    @pl.when(has_above)
    def _():
        pl.semaphore_signal(barrier, 1, device_id=(space + 1, vel), device_id_type=MESH)

    flat = lax.broadcasted_iota(jnp.int32, (CELLS, FLAT), 1).astype(F32)
    row = jnp.floor((flat + 0.5) / NV)
    y = (row - (NV - 1) / 2.0) * STEP
    z = (flat - row * NV - (NV - 1) / 2.0) * STEP
    yt[...] = y
    zt[...] = z
    mt[...] = jnp.exp(-(y * y + z * z) / 2.0)
    krow = lax.broadcasted_iota(jnp.int32, (256, 1280), 0)
    kcol = lax.broadcasted_iota(jnp.int32, (256, 1280), 1)
    sel[...] = jnp.where((krow >> 4) == (kcol >> 7), 1.0, 0.0).astype(BF16)
    for buf in (fa, fb):
        for plane in range(PLANES + 2):
            buf[plane, :, 0:MARGIN] = jnp.zeros((CELLS, MARGIN), F32)
            buf[plane, :, MARGIN + FLAT :] = jnp.zeros((CELLS, MARGIN), F32)

    @pl.when(jnp.logical_not(has_left))
    def _():
        fa[0] = jnp.zeros((CELLS, WIDE), F32)
        fb[0] = jnp.zeros((CELLS, WIDE), F32)

    @pl.when(jnp.logical_not(has_right))
    def _():
        fa[PLANES + 1] = jnp.zeros((CELLS, WIDE), F32)
        fb[PLANES + 1] = jnp.zeros((CELLS, WIDE), F32)

    prm[...] = jnp.zeros((32, 128), F32)
    for i in range(3):
        prm[6 * i : 6 * i + 6, 0:CELLS] = area[i]
    prm[18:24, 0:CELLS] = nb[...].astype(F32)
    prm[24:30, 0:CELLS] = wall[...].astype(F32)
    prm[30:31, 0:CELLS] = DT / vol[...]
    cols = prm[...].T[0:CELLS]
    for r in range(31):
        sb[r] = jnp.broadcast_to(cols[:, r : r + 1], (CELLS, 128))

    for copy in loads:
        copy.wait()
    for p in range(PLANES):
        for side in range(2):
            for r in range(HALO):
                hs[side, p, r : r + 1, :] = distv[p, pl.ds(send[side, r], 1), :]

    peers = VELS - 1 + has_below.astype(jnp.int32) + has_above.astype(jnp.int32)
    pl.semaphore_wait(barrier, peers)

    def halo(side, target):
        return pltpu.make_async_remote_copy(
            src_ref=hs.at[side], dst_ref=hr.at[1 - side], send_sem=h_ssem.at[side], recv_sem=h_rsem.at[1 - side],
            device_id=(target, vel), device_id_type=MESH,
        )

    @pl.when(has_above)
    def _():
        halo(1, space + 1).start()

    @pl.when(has_below)
    def _():
        halo(0, space - 1).start()

    @pl.when(jnp.logical_not(has_below))
    def _():
        for p in range(PLANES):
            hr[0, p] = jnp.broadcast_to(free[p : p + 1, :], (HALO, FLAT))

    @pl.when(jnp.logical_not(has_above))
    def _():
        for p in range(PLANES):
            hr[1, p] = jnp.broadcast_to(free[p : p + 1, :], (HALO, FLAT))

    xs = [((vel * PLANES + p).astype(F32) - (NV - 1) / 2.0) * STEP for p in range(PLANES)]
    mx = [jnp.exp(jnp.full((CELLS, 128), -0.5, F32) * (x * x)) for x in xs]

    def gather_copy(src, dst, ssem, rsem, d):
        return pltpu.make_async_remote_copy(
            src_ref=src, dst_ref=dst.at[d], send_sem=ssem.at[d], recv_sem=rsem.at[d],
            device_id=(space, lax.rem(vel + d, VELS)), device_id_type=MESH,
        )

    def total(src, dst, ssem, rsem):
        acc = src[...]
        for d in range(1, VELS):
            gather_copy(src, dst, ssem, rsem, d).wait_recv()
            acc = acc + dst[d]
        return acc

    def flux_plane(p, carry):
        sx = [sb[s] * xs[p] for s in range(FACES)]

        def step(t, carry):
            off = pl.multiple_of(t * 256, 128)
            outs, ins = list(carry[:FACES]), list(carry[FACES:])
            for j in range(2):
                o = pl.ds(off + 128 * j, 128)
                dd, yy, zz = distv[p, :, o], yt[:, o], zt[:, o]
                mm = mt[:, o] * mx[p]
                for s in range(FACES):
                    w = jnp.maximum(sx[s] + sb[6 + s] * yy + sb[12 + s] * zz, 0.0)
                    outs[s] = outs[s] + w * dd
                    ins[s] = ins[s] + w * mm
            return tuple(outs + ins)

        return lax.fori_loop(0, FLAT // 256, step, carry)

    carry = tuple(jnp.zeros((CELLS, 128), F32) for _ in range(2 * FACES))
    for p in range(PLANES):
        carry = flux_plane(p, carry)
    fsend[0:1, 0:96] = lane_sums(jnp.concatenate(carry[:FACES], axis=0))
    fsend[0:1, 128:224] = lane_sums(jnp.concatenate(carry[FACES:], axis=0))
    fsend[0:1, 96:128] = jnp.zeros((1, 32), F32)
    fsend[0:1, 224:256] = jnp.ones((1, 32), F32)
    for d in range(1, VELS):
        gather_copy(fsend, frecv, f_ssem, f_rsem, d).start()
    flux = total(fsend, frecv, f_ssem, f_rsem)
    ratio = spread(flux[:, 0:128] / jnp.where(flux[:, 128:256] > 0.0, flux[:, 128:256], 1.0), sel[0:128, 0:768])

    lane = lax.broadcasted_iota(jnp.int32, (CELLS, 64), 1) & 31
    for s in range(FACES):
        r = ratio[:, 128 * s : 128 * s + 64]
        r_hi = r.astype(BF16).astype(F32)
        at_wall = jnp.where(lane == 24, r_hi, jnp.where(lane == 25, r - r_hi, 0.0))
        inside = jnp.where(lane.astype(F32) == sb[18 + s][:, 0:64], 1.0, 0.0)
        lhs[16 * s : 16 * s + 16, :] = jnp.where(sb[24 + s][:, 0:64] > 0.5, at_wall, inside).astype(BF16)

    @pl.when(has_below)
    def _():
        halo(1, space + 1).wait_recv()

    @pl.when(has_above)
    def _():
        halo(0, space - 1).wait_recv()

    zero6 = tuple(jnp.zeros((CELLS, 128), F32) for _ in range(6))

    def add_moments(acc, f, yy, zz):
        fy, fz = f * yy, f * zz
        return (acc[0] + f, acc[1] + fy, acc[2] + fz, acc[3] + fy * yy, acc[4] + fz * zz, acc[5] + fy * zz)

    def send_moments(k, sums):
        m0 = sums[0][0] + sums[1][0] + sums[2][0]
        wx = [sums[p][0] * xs[p] for p in range(PLANES)]
        m1 = wx[0] + wx[1] + wx[2]
        m4 = wx[0] * xs[0] + wx[1] * xs[1] + wx[2] * xs[2]

        def plain(i):
            return sums[0][i] + sums[1][i] + sums[2][i]

        def timesx(i):
            return sums[0][i] * xs[0] + sums[1][i] * xs[1] + sums[2][i] * xs[2]

        acc = [m0, m1, plain(1), plain(2), m4, plain(3), plain(4), timesx(1), timesx(2), plain(5)]
        msend[k, 0:1, 0:160] = lane_sums(jnp.concatenate(acc, axis=0))
        msend[k, 0:1, 160:256] = jnp.zeros((1, 96), F32)
        for d in range(1, VELS):
            gather_copy(msend.at[k], mrecv.at[k], m_ssem.at[k], m_rsem.at[k], d).start()

    def plane_copy(k, buf, right):
        src, dst = (PLANES, 0) if right else (1, PLANES + 1)
        lanes = pl.ds(MARGIN, FLAT)
        i = 1 if right else 0
        return pltpu.make_async_remote_copy(
            src_ref=buf.at[src, :, lanes], dst_ref=buf.at[dst, :, lanes],
            send_sem=p_ssem.at[k, i], recv_sem=p_rsem.at[k, i],
            device_id=(space, vel + 1 if right else vel - 1), device_id_type=MESH,
        )

    def send_plane(k, buf, right):
        @pl.when(has_right if right else has_left)
        def _():
            plane_copy(k, buf, right).start()

    def recv_planes(k, buf):
        @pl.when(has_left)
        def _():
            plane_copy(k, buf, True).wait_recv()

        @pl.when(has_right)
        def _():
            plane_copy(k, buf, False).wait_recv()

    def moved_plane(p):
        sx = [sb[s] * xs[p] for s in range(FACES)]
        scale = sb[30]

        def step(t, acc):
            off = pl.multiple_of(t * 256, 128)
            o = pl.ds(off, 256)
            mm = mt[0:8, o] * rep(mx[p][0:8], 2)
            ext = jnp.concatenate([distv[p, :, o], hr[0, p, :, o], hr[1, p, :, o], mm], axis=0)
            picked = jnp.dot(lhs[...], jnp.concatenate(split2(ext), axis=0), preferred_element_type=F32)
            for j in range(2):
                o = pl.ds(off + 128 * j, 128)
                dd, yy, zz = distv[p, :, o], yt[:, o], zt[:, o]
                out_sum, in_sum = None, None
                for s in range(FACES):
                    w = sx[s] + sb[6 + s] * yy + sb[12 + s] * zz
                    up = jnp.maximum(w, 0.0)
                    term = (w - up) * picked[16 * s : 16 * s + 16, 128 * j : 128 * j + 128]
                    out_sum = up if s == 0 else out_sum + up
                    in_sum = term if s == 0 else in_sum + term
                f = dd - scale * (out_sum * dd + in_sum)
                fa[p + 1, :, pl.ds(off + 128 * j + MARGIN, 128)] = f
                acc = add_moments(acc, f, yy, zz)
            return acc

        return lax.fori_loop(0, FLAT // 256, step, zero6)

    sums = [None] * PLANES
    sums[0] = moved_plane(0)
    send_plane(0, fa, False)
    sums[2] = moved_plane(2)
    send_plane(0, fa, True)
    sums[1] = moved_plane(1)
    send_moments(0, sums)

    def coefficients(k):
        row = total(msend.at[k], mrecv.at[k], m_ssem.at[k], m_rsem.at[k])
        allm = spread(row, sel[...])
        m = [allm[:, 128 * i : 128 * i + 128] for i in range(10)]
        inv = 1.0 / m[0]
        ux, uy, uz = m[1] * inv, m[2] * inv, m[3] * inv
        cxx, cyy, czz = m[4] * inv - ux * ux, m[5] * inv - uy * uy, m[6] * inv - uz * uz
        cxy, cxz, cyz = m[7] * inv - ux * uy, m[8] * inv - ux * uz, m[9] * inv - uy * uz
        theta = (cxx + cyy + czz) / 3.0
        a = (RATE * STEP**3) * m[0] * jnp.exp(0.19 * jnp.log(theta))
        lx, ly, lz = 0.5 * (theta + cxx), 0.5 * (theta + cyy), 0.5 * (theta + czz)
        return dict(
            ux=ux, a=a, k0=1.0 - 32.0 * a * (lx + ly + lz), lx=16.0 * a * lx,
            ys=a * (16.0 * ly + 0.5), a2=2.0 * a, a2uy=2.0 * a * uy, a2uz=2.0 * a * uz, zq=16.0 * a * lz,
            gxy=4.0 * a * cxy, gxz=4.0 * a * cxz, gyz=4.0 * a * cyz,
        )

    width = 384

    def relax_plane(src, dst, dst_off, p, c, moments):
        n = width // 128
        drift_n = c["a2"] * (xs[p] + STEP - c["ux"]) + c["lx"]
        drift_p = c["lx"] - c["a2"] * (xs[p] - STEP - c["ux"])
        kn, kp, k0 = rep(drift_n, n), rep(drift_p, n), rep(c["k0"], n)
        ys, a2, a2uy, a2uz, zq = (rep(c[q], n) for q in ("ys", "a2", "a2uy", "a2uz", "zq"))
        gxy, gxz, gyz = (rep(c[q], n) for q in ("gxy", "gxz", "gyz"))
        lanes = lax.broadcasted_iota(jnp.int32, (CELLS, width), 1)

        def step(t, acc):
            off = pl.multiple_of(t * width, 128)
            win = pl.ds(off, width + 2 * MARGIN)
            cen = pl.ds(off, width)
            cw, nw, pw = src[p + 1, :, win], src[p + 2, :, win], src[p, :, win]
            xw = nw - pw
            yy, zz = yt[:, cen], zt[:, cen]
            total_w = width + 2 * MARGIN

            def up(v):
                return pltpu.roll(v, total_w - NV, 1)[:, MARGIN : MARGIN + width]

            def down(v):
                return pltpu.roll(v, NV, 1)[:, MARGIN : MARGIN + width]

            cc, nn, pp = (v[:, MARGIN : MARGIN + width] for v in (cw, nw, pw))
            u, d = up(cw), down(cw)
            diff = u - d
            res = k0 * cc + kn * nn + kp * pp
            res = res + ys * (u + d) + (a2 * yy - a2uy) * diff + gxy * (up(xw) - down(xw))
            cross = gxz * (nn - pp) + gyz * diff
            zr = a2 * zz - a2uz
            plus = (zq + zr) * cc + cross
            minus = (zq - zr) * cc - cross
            edge = (NV - 1) / 2.0 * STEP
            res = res + jnp.where(zz < edge - 0.1, pltpu.roll(plus, width - 1, 1), 0.0)
            res = res + jnp.where(zz > 0.1 - edge, pltpu.roll(minus, 1, 1), 0.0)
            dst[dst_off + p, :, pl.ds(off + (MARGIN if dst_off else 0), width)] = res
            if moments:
                for j in range(n):
                    q = slice(128 * j, 128 * j + 128)
                    acc = add_moments(acc, res[:, q], yy[:, q], zz[:, q])
            return acc

        del lanes
        return lax.fori_loop(0, FLAT // width, step, zero6 if moments else 0)

    c = coefficients(0)
    recv_planes(0, fa)
    sums[0] = relax_plane(fa, fb, 1, 0, c, True)
    send_plane(1, fb, False)
    sums[2] = relax_plane(fa, fb, 1, 2, c, True)
    send_plane(1, fb, True)
    sums[1] = relax_plane(fa, fb, 1, 1, c, True)
    send_moments(1, sums)
    c = coefficients(1)
    relax_plane(fb, fc, 0, 1, c, False)
    recv_planes(1, fb)
    stores = [pltpu.make_async_copy(fc.at[p], out.at[p], out_sem.at[p]) for p in range(PLANES)]
    stores[1].start()
    for p in (0, 2):
        relax_plane(fb, fc, 0, p, c, False)
        stores[p].start()

    @pl.when(has_above)
    def _():
        halo(1, space + 1).wait_send()

    @pl.when(has_below)
    def _():
        halo(0, space - 1).wait_send()

    for d in range(1, VELS):
        gather_copy(fsend, frecv, f_ssem, f_rsem, d).wait_send()
        for k in range(2):
            gather_copy(msend.at[k], mrecv.at[k], m_ssem.at[k], m_rsem.at[k], d).wait_send()
    for k, buf in ((0, fa), (1, fb)):
        for right in (False, True):

            @pl.when(has_right if right else has_left)
            def _():
                plane_copy(k, buf, right).wait_send()

    for copy in stores:
        copy.wait()


def body(distribution, freestream, face_area, cell_volume, neighbours, wall_flags, send_cells):
    dma = pltpu.SemaphoreType.DMA
    vmem = pl.BlockSpec(memory_space=pltpu.VMEM)
    anyw = pl.BlockSpec(memory_space=pl.ANY)
    new = pl.pallas_call(
        kernel,
        out_shape=jax.ShapeDtypeStruct((PLANES, CELLS, FLAT), F32),
        in_specs=[anyw, vmem, vmem, vmem, vmem, vmem, pl.BlockSpec(memory_space=pltpu.SMEM)],
        out_specs=anyw,
        scratch_shapes=[
            pltpu.VMEM((PLANES, CELLS, FLAT), F32),
            pltpu.VMEM((2, PLANES, HALO, FLAT), F32),
            pltpu.VMEM((2, PLANES, HALO, FLAT), F32),
            pltpu.VMEM((PLANES + 2, CELLS, WIDE), F32),
            pltpu.VMEM((PLANES + 2, CELLS, WIDE), F32),
            pltpu.VMEM((PLANES, CELLS, FLAT), F32),
            pltpu.VMEM((CELLS, FLAT), F32),
            pltpu.VMEM((CELLS, FLAT), F32),
            pltpu.VMEM((CELLS, FLAT), F32),
            pltpu.VMEM((32, 128), F32),
            pltpu.VMEM((32, CELLS, 128), F32),
            pltpu.VMEM((96, 64), BF16),
            pltpu.VMEM((256, 1280), BF16),
            pltpu.VMEM((1, 256), F32),
            pltpu.VMEM((VELS, 1, 256), F32),
            pltpu.VMEM((2, 1, 256), F32),
            pltpu.VMEM((2, VELS, 1, 256), F32),
            dma((PLANES,)), dma((PLANES,)), dma((2,)), dma((2,)),
            dma((VELS,)), dma((VELS,)), dma((2, VELS)), dma((2, VELS)), dma((2, 2)), dma((2, 2)),
        ],
        compiler_params=pltpu.CompilerParams(
            collective_id=0, has_side_effects=True, vmem_limit_bytes=24 * 1024 * 1024
        ),
    )(
        jnp.transpose(distribution, (1, 0, 2)), freestream, face_area, cell_volume.reshape(1, CELLS), neighbours,
        wall_flags, send_cells,
    )
    return jnp.transpose(new, (1, 0, 2))


def solution(mesh):
    in_specs = (
        P("space", "vel", None),
        P("vel", None),
        P(None, None, "space"),
        P("space"),
        P(None, "space"),
        P(None, "space"),
        P(None, "space"),
    )
    out_specs = P("space", "vel", None)
    return jax.shard_map(body, mesh=mesh, in_specs=in_specs, out_specs=out_specs, check_vma=False)
```

```python
import functools

import jax
import jax.numpy as jnp
from jax import lax
from jax.experimental import pallas as pl
from jax.experimental.pallas import tpu as pltpu
from jax.sharding import PartitionSpec as P

NV = 48
FLAT = NV * NV
STEP = 0.25
DT = 0.02
RATE = 0.002
FACES = 6
HALO = 4
CELLS = 16
PLANES = 3
MARGIN = 128
WIDE = FLAT + 2 * MARGIN
VELS = 16
LANES = 4
PARTS = ((9, 13), (13, 16), (16, 18), (0, 9))
MESH = pl.DeviceIdType.MESH
F32 = jnp.float32
BF16 = jnp.bfloat16


def split2(x):
    hi = x.astype(BF16)
    return hi, (x - hi.astype(F32)).astype(BF16)


def split3(x):
    hi = x.astype(BF16)
    r = x - hi.astype(F32)
    mid = r.astype(BF16)
    return hi, mid, (r - mid.astype(F32)).astype(BF16)


def lane_sums(acc):
    ones = jnp.ones((16, 128), BF16)
    total = None
    for part in split3(acc):
        term = lax.dot_general(ones, part, (((1,), (1,)), ((), ())), preferred_element_type=F32)
        total = term if total is None else total + term
    return total[0:1]


def spread(row, sel):
    k = row.shape[1]
    lane = lax.broadcasted_iota(jnp.int32, (CELLS, k), 1)
    cell = lax.broadcasted_iota(jnp.int32, (CELLS, k), 0)
    own = jnp.where((lane & (CELLS - 1)) == cell, jnp.broadcast_to(row, (CELLS, k)), 0.0)
    stacked = jnp.concatenate(split3(own), axis=0)
    out = jnp.dot(stacked, sel, preferred_element_type=F32)
    return out[0:16] + out[16:32] + out[32:48]


def rep(x, n):
    return jnp.concatenate([x] * n, axis=1)


def kernel(
    dist, free_h, area_h, vol_h, nb_h, wall_h, send_h, out,
    free, area, vol, nb, wall, send, distv, hs, hr, fa, fb, fc, relay, yt, zt, mt, prm, sb, lhs, sel, fsend, frecv, msend, mrecv,
    in_sem, out_sem, h_ssem, h_rsem, f_ssem, f_rsem, m_ssem, m_rsem, p_ssem, p_rsem,
    s_sem, z_ssem, z_rsem, r_ssem, r_rsem,
):
    space = lax.axis_index("space")
    vel = lax.axis_index("vel")
    blocks = lax.axis_size("space")
    has_below, has_above = space > 0, space < blocks - 1
    has_left, has_right = vel > 0, vel < VELS - 1

    loads = [pltpu.make_async_copy(dist.at[p], distv.at[p], in_sem.at[p]) for p in range(PLANES)]
    small = [
        pltpu.make_async_copy(src, dst, s_sem.at[i])
        for i, (src, dst) in enumerate(
            ((area_h, area), (nb_h, nb), (wall_h, wall), (vol_h, vol), (send_h, send), (free_h, free))
        )
    ]
    for copy in small + loads:
        copy.start()

    barrier = pltpu.get_barrier_semaphore()
    for d in range(1, VELS):
        pl.semaphore_signal(barrier, 1, device_id=(space, lax.rem(vel + d, VELS)), device_id_type=MESH)

    @pl.when(has_below)
    def _():
        pl.semaphore_signal(barrier, 1, device_id=(space - 1, vel), device_id_type=MESH)

    @pl.when(has_above)
    def _():
        pl.semaphore_signal(barrier, 1, device_id=(space + 1, vel), device_id_type=MESH)

    flat = lax.broadcasted_iota(jnp.int32, (CELLS, FLAT), 1).astype(F32)
    row = jnp.floor((flat + 0.5) / NV)
    y = (row - (NV - 1) / 2.0) * STEP
    z = (flat - row * NV - (NV - 1) / 2.0) * STEP
    yt[...] = y
    zt[...] = z
    mt[...] = jnp.exp(-(y * y + z * z) / 2.0)
    krow = lax.broadcasted_iota(jnp.int32, (256, 1280), 0)
    kcol = lax.broadcasted_iota(jnp.int32, (256, 1280), 1)
    sel[...] = jnp.where((krow >> 4) == (kcol >> 7), 1.0, 0.0).astype(BF16)
    for buf in (fa, fb):
        for plane in range(PLANES + 2):
            buf[plane, :, 0:MARGIN] = jnp.zeros((CELLS, MARGIN), F32)
            buf[plane, :, MARGIN + FLAT :] = jnp.zeros((CELLS, MARGIN), F32)

    @pl.when(jnp.logical_not(has_left))
    def _():
        fa[0] = jnp.zeros((CELLS, WIDE), F32)
        fb[0] = jnp.zeros((CELLS, WIDE), F32)

    @pl.when(jnp.logical_not(has_right))
    def _():
        fa[PLANES + 1] = jnp.zeros((CELLS, WIDE), F32)
        fb[PLANES + 1] = jnp.zeros((CELLS, WIDE), F32)

    for copy in small:
        copy.wait()

    prm[...] = jnp.zeros((32, 128), F32)
    for i in range(3):
        prm[6 * i : 6 * i + 6, 0:CELLS] = area[i]
    prm[18:24, 0:CELLS] = nb[...].astype(F32)
    prm[24:30, 0:CELLS] = wall[...].astype(F32)
    prm[30:31, 0:CELLS] = DT / vol[...]
    cols = prm[...].T[0:CELLS]
    for r in range(31):
        sb[r] = jnp.broadcast_to(cols[:, r : r + 1], (CELLS, 128))

    for copy in loads:
        copy.wait()
    for p in range(PLANES):
        for side in range(2):
            for r in range(HALO):
                hs[side, p, r : r + 1, :] = distv[p, pl.ds(send[side, r], 1), :]

    xs = [((vel * PLANES + p).astype(F32) - (NV - 1) / 2.0) * STEP for p in range(PLANES)]
    mx = [jnp.exp(jnp.full((CELLS, 128), -0.5, F32) * (x * x)) for x in xs]

    def gather_copy(src, dst, ssem, rsem, d):
        return pltpu.make_async_remote_copy(
            src_ref=src, dst_ref=dst.at[d], send_sem=ssem.at[d], recv_sem=rsem.at[d],
            device_id=(space, lax.rem(vel + d, VELS)), device_id_type=MESH,
        )

    def total(src, dst, ssem, rsem):
        acc = src[...]
        for d in range(1, VELS):
            gather_copy(src, dst, ssem, rsem, d).wait_recv()
            acc = acc + dst[d]
        return acc

    def flux_plane(p, carry):
        sx = [sb[s] * xs[p] for s in range(FACES)]

        def step(t, carry):
            off = pl.multiple_of(t * 256, 128)
            outs, ins = list(carry[:FACES]), list(carry[FACES:])
            for j in range(2):
                o = pl.ds(off + 128 * j, 128)
                dd, yy, zz = distv[p, :, o], yt[:, o], zt[:, o]
                mm = mt[:, o] * mx[p]
                for s in range(FACES):
                    w = jnp.maximum(sx[s] + sb[6 + s] * yy + sb[12 + s] * zz, 0.0)
                    outs[s] = outs[s] + w * dd
                    ins[s] = ins[s] + w * mm
            return tuple(outs + ins)

        return lax.fori_loop(0, FLAT // 256, step, carry)

    carry = tuple(jnp.zeros((CELLS, 128), F32) for _ in range(2 * FACES))
    for p in range(PLANES):
        carry = flux_plane(p, carry)
    fsend[0:1, 0:96] = lane_sums(jnp.concatenate(carry[:FACES], axis=0))
    fsend[0:1, 128:224] = lane_sums(jnp.concatenate(carry[FACES:], axis=0))
    fsend[0:1, 96:128] = jnp.zeros((1, 32), F32)
    fsend[0:1, 224:256] = jnp.ones((1, 32), F32)
    peers = VELS - 1 + has_below.astype(jnp.int32) + has_above.astype(jnp.int32)
    pl.semaphore_wait(barrier, peers)

    def halo(side, target):
        return pltpu.make_async_remote_copy(
            src_ref=hs.at[side], dst_ref=hr.at[1 - side], send_sem=h_ssem.at[side], recv_sem=h_rsem.at[1 - side],
            device_id=(target, vel), device_id_type=MESH,
        )

    @pl.when(has_above)
    def _():
        halo(1, space + 1).start()

    @pl.when(has_below)
    def _():
        halo(0, space - 1).start()

    @pl.when(jnp.logical_not(has_below))
    def _():
        for p in range(PLANES):
            hr[0, p] = jnp.broadcast_to(free[p : p + 1, :], (HALO, FLAT))

    @pl.when(jnp.logical_not(has_above))
    def _():
        for p in range(PLANES):
            hr[1, p] = jnp.broadcast_to(free[p : p + 1, :], (HALO, FLAT))

    for d in range(1, VELS):
        gather_copy(fsend, frecv, f_ssem, f_rsem, d).start()
    flux = total(fsend, frecv, f_ssem, f_rsem)
    ratio = spread(flux[:, 0:128] / jnp.where(flux[:, 128:256] > 0.0, flux[:, 128:256], 1.0), sel[0:128, 0:768])

    lane = lax.broadcasted_iota(jnp.int32, (CELLS, 64), 1) & 31
    for s in range(FACES):
        r = ratio[:, 128 * s : 128 * s + 64]
        r_hi = r.astype(BF16).astype(F32)
        at_wall = jnp.where(lane == 24, r_hi, jnp.where(lane == 25, r - r_hi, 0.0))
        inside = jnp.where(lane.astype(F32) == sb[18 + s][:, 0:64], 1.0, 0.0)
        lhs[16 * s : 16 * s + 16, :] = jnp.where(sb[24 + s][:, 0:64] > 0.5, at_wall, inside).astype(BF16)

    @pl.when(has_below)
    def _():
        halo(1, space + 1).wait_recv()

    @pl.when(has_above)
    def _():
        halo(0, space - 1).wait_recv()

    zero6 = tuple(jnp.zeros((CELLS, 128), F32) for _ in range(6))

    def add_moments(acc, f, yy, zz):
        fy, fz = f * yy, f * zz
        return (acc[0] + f, acc[1] + fy, acc[2] + fz, acc[3] + fy * yy, acc[4] + fz * zz, acc[5] + fy * zz)

    def send_moments(k, sums):
        m0 = sums[0][0] + sums[1][0] + sums[2][0]
        wx = [sums[p][0] * xs[p] for p in range(PLANES)]
        m1 = wx[0] + wx[1] + wx[2]
        m4 = wx[0] * xs[0] + wx[1] * xs[1] + wx[2] * xs[2]

        def plain(i):
            return sums[0][i] + sums[1][i] + sums[2][i]

        def timesx(i):
            return sums[0][i] * xs[0] + sums[1][i] * xs[1] + sums[2][i] * xs[2]

        acc = [m0, m1, plain(1), plain(2), m4, plain(3), plain(4), timesx(1), timesx(2), plain(5)]
        msend[k, 0:1, 0:160] = lane_sums(jnp.concatenate(acc, axis=0))
        msend[k, 0:1, 160:256] = jnp.zeros((1, 96), F32)
        for d in range(1, VELS):
            gather_copy(msend.at[k], mrecv.at[k], m_ssem.at[k], m_rsem.at[k], d).start()

    y_at, z_at = lax.rem(vel, LANES), vel // LANES

    def sides(right):
        return (LANES - 1, 0, 1, z_at < LANES - 1) if right else (0, LANES - 1, -1, z_at > 0)

    def ends(right):
        return (PLANES, 0) if right else (1, PLANES + 1)

    def lanes_of(right, q):
        first, last = PARTS[q if right else LANES - 1 - q]
        return first, last - first

    def near_copy(k, buf, right):
        src, dst = ends(right)
        lanes = pl.ds(MARGIN, FLAT)
        i = 1 if right else 0
        return pltpu.make_async_remote_copy(
            src_ref=buf.at[src, :, lanes], dst_ref=buf.at[dst, :, lanes],
            send_sem=p_ssem.at[k, i], recv_sem=p_rsem.at[k, i],
            device_id=(space, vel + 1 if right else vel - 1), device_id_type=MESH,
        )

    def part_copy(k, buf, right, q):
        home, other, dz, _ = sides(right)
        src, dst = ends(right)
        first, count = lanes_of(right, q)
        lanes = pl.ds(MARGIN + 128 * first, 128 * count)
        i = 1 if right else 0
        if q == home:
            dst_ref, recv, to = buf.at[dst, :, lanes], z_rsem.at[k, i, q], (z_at + dz) * LANES + other
        else:
            dst_ref, recv, to = relay.at[k, i, :, pl.ds(0, 128 * count)], r_rsem.at[k, i], z_at * LANES + q
        return pltpu.make_async_remote_copy(
            src_ref=buf.at[src, :, lanes], dst_ref=dst_ref, send_sem=z_ssem.at[k, i, q], recv_sem=recv,
            device_id=(space, to), device_id_type=MESH,
        )

    def relay_copy(k, buf, right, q):
        home, other, dz, _ = sides(right)
        src, dst = ends(right)
        first, count = lanes_of(right, q)
        lanes = pl.ds(MARGIN + 128 * first, 128 * count)
        i = 1 if right else 0
        return pltpu.make_async_remote_copy(
            src_ref=relay.at[k, i, :, pl.ds(0, 128 * count)], dst_ref=buf.at[dst, :, lanes],
            send_sem=r_ssem.at[k, i], recv_sem=z_rsem.at[k, i, q],
            device_id=(space, (z_at + dz) * LANES + other), device_id_type=MESH,
        )

    def send_plane(k, buf, right):
        home, _, _, inner = sides(right)

        @pl.when(y_at != home)
        def _():
            near_copy(k, buf, right).start()

        @pl.when((y_at == home) & inner)
        def _():
            for q in range(LANES):
                part_copy(k, buf, right, q).start()

    def pass_on(k, buf):
        for right in (True, False):
            home, _, _, inner = sides(right)
            for q in range(LANES):
                if q != home:

                    @pl.when((y_at == q) & inner)
                    def _():
                        part_copy(k, buf, right, q).wait_recv()
                        relay_copy(k, buf, right, q).start()

    def recv_planes(k, buf):
        for right in (True, False):
            home, other, _, _ = sides(right)
            from_z = z_at > 0 if right else z_at < LANES - 1

            @pl.when(y_at != other)
            def _():
                near_copy(k, buf, right).wait_recv()

            @pl.when((y_at == other) & from_z)
            def _():
                for q in range(LANES):
                    if q == home:
                        part_copy(k, buf, right, q).wait_recv()
                    else:
                        relay_copy(k, buf, right, q).wait_recv()

    def end_planes(k, buf):
        for right in (True, False):
            home, _, _, inner = sides(right)

            @pl.when(y_at != home)
            def _():
                near_copy(k, buf, right).wait_send()

            @pl.when((y_at == home) & inner)
            def _():
                for q in range(LANES):
                    part_copy(k, buf, right, q).wait_send()

            for q in range(LANES):
                if q != home:

                    @pl.when((y_at == q) & inner)
                    def _():
                        relay_copy(k, buf, right, q).wait_send()

    def moved_plane(p):
        sx = [sb[s] * xs[p] for s in range(FACES)]
        scale = sb[30]

        def step(t, acc):
            off = pl.multiple_of(t * 256, 128)
            o = pl.ds(off, 256)
            mm = mt[0:8, o] * rep(mx[p][0:8], 2)
            ext = jnp.concatenate([distv[p, :, o], hr[0, p, :, o], hr[1, p, :, o], mm], axis=0)
            picked = jnp.dot(lhs[...], jnp.concatenate(split2(ext), axis=0), preferred_element_type=F32)
            for j in range(2):
                o = pl.ds(off + 128 * j, 128)
                dd, yy, zz = distv[p, :, o], yt[:, o], zt[:, o]
                out_sum, in_sum = None, None
                for s in range(FACES):
                    w = sx[s] + sb[6 + s] * yy + sb[12 + s] * zz
                    up = jnp.maximum(w, 0.0)
                    term = (w - up) * picked[16 * s : 16 * s + 16, 128 * j : 128 * j + 128]
                    out_sum = up if s == 0 else out_sum + up
                    in_sum = term if s == 0 else in_sum + term
                f = dd - scale * (out_sum * dd + in_sum)
                fa[p + 1, :, pl.ds(off + 128 * j + MARGIN, 128)] = f
                acc = add_moments(acc, f, yy, zz)
            return acc

        return lax.fori_loop(0, FLAT // 256, step, zero6, unroll=True)

    sums = [None] * PLANES
    sums[0] = moved_plane(0)
    send_plane(0, fa, False)
    sums[2] = moved_plane(2)
    send_plane(0, fa, True)
    sums[1] = moved_plane(1)
    send_moments(0, sums)
    pass_on(0, fa)

    def coefficients(k):
        row = total(msend.at[k], mrecv.at[k], m_ssem.at[k], m_rsem.at[k])
        allm = spread(row, sel[...])
        m = [allm[:, 128 * i : 128 * i + 128] for i in range(10)]
        inv = 1.0 / m[0]
        ux, uy, uz = m[1] * inv, m[2] * inv, m[3] * inv
        cxx, cyy, czz = m[4] * inv - ux * ux, m[5] * inv - uy * uy, m[6] * inv - uz * uz
        cxy, cxz, cyz = m[7] * inv - ux * uy, m[8] * inv - ux * uz, m[9] * inv - uy * uz
        theta = (cxx + cyy + czz) / 3.0
        a = (RATE * STEP**3) * m[0] * jnp.exp(0.19 * jnp.log(theta))
        lx, ly, lz = 0.5 * (theta + cxx), 0.5 * (theta + cyy), 0.5 * (theta + czz)
        return dict(
            ux=ux, a=a, k0=1.0 - 32.0 * a * (lx + ly + lz), lx=16.0 * a * lx,
            ys=a * (16.0 * ly + 0.5), a2=2.0 * a, a2uy=2.0 * a * uy, a2uz=2.0 * a * uz, zq=16.0 * a * lz,
            gxy=4.0 * a * cxy, gxz=4.0 * a * cxz, gyz=4.0 * a * cyz,
        )

    width = 768

    def relax_plane(src, dst, dst_off, p, c, moments):
        n = width // 128
        drift_n = c["a2"] * (xs[p] + STEP - c["ux"]) + c["lx"]
        drift_p = c["lx"] - c["a2"] * (xs[p] - STEP - c["ux"])
        kn, kp, k0 = rep(drift_n, n), rep(drift_p, n), rep(c["k0"], n)
        ys, a2, a2uy, a2uz, zq = (rep(c[q], n) for q in ("ys", "a2", "a2uy", "a2uz", "zq"))
        gxy, gxz, gyz = (rep(c[q], n) for q in ("gxy", "gxz", "gyz"))

        def step(t, acc):
            off = pl.multiple_of(t * width, 128)
            win = pl.ds(off, width + 2 * MARGIN)
            cen = pl.ds(off, width)
            cw, nw, pw = src[p + 1, :, win], src[p + 2, :, win], src[p, :, win]
            xw = nw - pw
            yy, zz = yt[:, cen], zt[:, cen]
            total_w = width + 2 * MARGIN

            def up(v):
                return pltpu.roll(v, total_w - NV, 1)[:, MARGIN : MARGIN + width]

            def down(v):
                return pltpu.roll(v, NV, 1)[:, MARGIN : MARGIN + width]

            cc, nn, pp = (v[:, MARGIN : MARGIN + width] for v in (cw, nw, pw))
            u, d = up(cw), down(cw)
            diff = u - d
            res = k0 * cc + kn * nn + kp * pp
            res = res + ys * (u + d) + (a2 * yy - a2uy) * diff + gxy * (up(xw) - down(xw))
            cross = gxz * (nn - pp) + gyz * diff
            zr = a2 * zz - a2uz
            plus = (zq + zr) * cc + cross
            minus = (zq - zr) * cc - cross
            edge = (NV - 1) / 2.0 * STEP
            res = res + jnp.where(zz < edge - 0.1, pltpu.roll(plus, width - 1, 1), 0.0)
            res = res + jnp.where(zz > 0.1 - edge, pltpu.roll(minus, 1, 1), 0.0)
            dst[dst_off + p, :, pl.ds(off + (MARGIN if dst_off else 0), width)] = res
            if moments:
                for j in range(n):
                    q = slice(128 * j, 128 * j + 128)
                    acc = add_moments(acc, res[:, q], yy[:, q], zz[:, q])
            return acc

        return lax.fori_loop(0, FLAT // width, step, zero6 if moments else 0, unroll=True)

    c = coefficients(0)
    recv_planes(0, fa)
    sums[0] = relax_plane(fa, fb, 1, 0, c, True)
    send_plane(1, fb, False)
    sums[2] = relax_plane(fa, fb, 1, 2, c, True)
    send_plane(1, fb, True)
    sums[1] = relax_plane(fa, fb, 1, 1, c, True)
    send_moments(1, sums)
    pass_on(1, fb)
    c = coefficients(1)
    relax_plane(fb, fc, 0, 1, c, False)
    recv_planes(1, fb)
    stores = [pltpu.make_async_copy(fc.at[p], out.at[p], out_sem.at[p]) for p in range(PLANES)]
    stores[1].start()
    for p in (0, 2):
        relax_plane(fb, fc, 0, p, c, False)
        stores[p].start()

    @pl.when(has_above)
    def _():
        halo(1, space + 1).wait_send()

    @pl.when(has_below)
    def _():
        halo(0, space - 1).wait_send()

    for d in range(1, VELS):
        gather_copy(fsend, frecv, f_ssem, f_rsem, d).wait_send()
        for k in range(2):
            gather_copy(msend.at[k], mrecv.at[k], m_ssem.at[k], m_rsem.at[k], d).wait_send()
    end_planes(0, fa)
    end_planes(1, fb)
    for copy in stores:
        copy.wait()


def body(distribution, freestream, face_area, cell_volume, neighbours, wall_flags, send_cells):
    dma = pltpu.SemaphoreType.DMA
    hbm = pl.BlockSpec(memory_space=pltpu.HBM)
    anyw = pl.BlockSpec(memory_space=pl.ANY)
    new = pl.pallas_call(
        kernel,
        out_shape=jax.ShapeDtypeStruct((PLANES, CELLS, FLAT), F32),
        in_specs=[hbm] * 7,
        out_specs=anyw,
        scratch_shapes=[
            pltpu.VMEM((PLANES, FLAT), F32),
            pltpu.VMEM((3, FACES, CELLS), F32),
            pltpu.VMEM((1, CELLS), F32),
            pltpu.VMEM((FACES, CELLS), jnp.int32),
            pltpu.VMEM((FACES, CELLS), jnp.int32),
            pltpu.SMEM((2, HALO), jnp.int32),
            pltpu.VMEM((PLANES, CELLS, FLAT), F32),
            pltpu.VMEM((2, PLANES, HALO, FLAT), F32),
            pltpu.VMEM((2, PLANES, HALO, FLAT), F32),
            pltpu.VMEM((PLANES + 2, CELLS, WIDE), F32),
            pltpu.VMEM((PLANES + 2, CELLS, WIDE), F32),
            pltpu.VMEM((PLANES, CELLS, FLAT), F32),
            pltpu.VMEM((2, 2, CELLS, 4 * 128), F32),
            pltpu.VMEM((CELLS, FLAT), F32),
            pltpu.VMEM((CELLS, FLAT), F32),
            pltpu.VMEM((CELLS, FLAT), F32),
            pltpu.VMEM((32, 128), F32),
            pltpu.VMEM((32, CELLS, 128), F32),
            pltpu.VMEM((96, 64), BF16),
            pltpu.VMEM((256, 1280), BF16),
            pltpu.VMEM((1, 256), F32),
            pltpu.VMEM((VELS, 1, 256), F32),
            pltpu.VMEM((2, 1, 256), F32),
            pltpu.VMEM((2, VELS, 1, 256), F32),
            dma((PLANES,)), dma((PLANES,)), dma((2,)), dma((2,)),
            dma((VELS,)), dma((VELS,)), dma((2, VELS)), dma((2, VELS)), dma((2, 2)), dma((2, 2)),
            dma((6,)), dma((2, 2, LANES)), dma((2, 2, LANES)), dma((2, 2)), dma((2, 2)),
        ],
        compiler_params=pltpu.CompilerParams(
            collective_id=0, has_side_effects=True, vmem_limit_bytes=63 * 1024 * 1024
        ),
    )(
        jnp.transpose(distribution, (1, 0, 2)), freestream, face_area, cell_volume.reshape(1, CELLS), neighbours,
        wall_flags, send_cells,
    )
    return jnp.transpose(new, (1, 0, 2))


def solution(mesh):
    in_specs = (
        P("space", "vel", None),
        P("vel", None),
        P(None, None, "space"),
        P("space"),
        P(None, "space"),
        P(None, "space"),
        P(None, "space"),
    )
    out_specs = P("space", "vel", None)
    return jax.shard_map(body, mesh=mesh, in_specs=in_specs, out_specs=out_specs, check_vma=False)
```

```python
import jax
import jax.numpy as jnp
import numpy as np
from jax import lax
from jax.experimental import pallas as pl
from jax.experimental.pallas import tpu as pltpu
from jax.sharding import PartitionSpec as P

NV = 48
FLAT = NV * NV
STEP = 0.25
DT = 0.02
RATE = 0.002
FACES = 6
HALO = 4
CELLS = 16
PLANES = 3
MARGIN = 128
WIDE = FLAT + 2 * MARGIN
VELS = 16
LANES = 4
PARTS = ((8, 12), (12, 15), (15, 18), (0, 8))
MESH = pl.DeviceIdType.MESH
F32 = jnp.float32
BF16 = jnp.bfloat16


PLANE_SUMS = 22
TIMES_X = (0, 1, 2, 6, 7, 9, 10, 12, 13, 15, 16, 18, 19, 20, 21)
TIMES_XX = (0, 6, 9, 12, 15, 18, 19, 20, 21)
X_FACE = tuple(range(18))
SENT = tuple(range(PLANE_SUMS)) + TIMES_X + TIMES_XX + X_FACE
AT_X, AT_XX, AT_FACE = 22, 37, 46
MOMENTS = (0, AT_X, 1, 2, AT_XX, 3, 4, AT_X + 1, AT_X + 2, 5)


def plane_sums(j, k):
    y, z = (j - (NV - 1) / 2.0) * STEP, (k - (NV - 1) / 2.0) * STEP
    one = np.ones_like(y)
    lo_y, hi_y, lo_z, hi_z = ((at == end).astype(np.float64) for at in (j, k) for end in (0, NV - 1))
    sums = [one, y, z, y * y, z * z, y * z]
    for face in (lo_y, hi_y):
        sums += [face, face * z, face * z * z]
    for face in (lo_z, hi_z):
        sums += [face, face * y, face * y * y]
    sums += [lo_y * lo_z, lo_y * hi_z, hi_y * lo_z, hi_y * hi_z]
    return np.stack(sums)


def two_parts(x):
    hi = x.astype(jnp.bfloat16)
    return hi, (x - hi.astype(np.float64)).astype(jnp.bfloat16)


def sum_weights():
    at = np.arange(FLAT)
    weights = plane_sums(at // NV, at % NV)[list(SENT)].T
    return np.concatenate(two_parts(weights), axis=1)


def stencil_moments():
    line = np.array([0, 1, 2, 17, 23, 30, 45, 46, 47])
    at = np.stack(np.meshgrid(line, line, line, indexing="ij")).reshape(3, -1)

    def velocity(index):
        return (index - (NV - 1) / 2.0) * STEP

    planes = plane_sums(at[1], at[2])
    x = velocity(at[0])
    basis = [planes[c] for c in range(PLANE_SUMS)] + [planes[c] * x for c in TIMES_X] + [planes[c] * x * x for c in TIMES_XX]
    for end in (0, NV - 1):
        basis += [planes[c] * (at[0] == end) for c in X_FACE]

    def polynomials(index):
        v = velocity(index)
        inside = np.all((index >= 0) & (index < NV), axis=0)
        vx, vy, vz = v
        return np.stack([np.ones_like(vx), vx, vy, vz, vx * vx, vy * vy, vz * vz, vx * vy, vx * vz, vy * vz]) * inside

    def moved(*steps):
        index = at.copy()
        for axis, step in steps:
            index[axis] += step
        return polynomials(index)

    v = velocity(at)
    first = [(moved((i, -1)) - moved((i, 1))) / (2 * STEP) for i in range(3)]
    terms = [sum(v[i] * first[i] for i in range(3))] + first
    terms += [(moved((i, -1)) - 2 * moved() + moved((i, 1))) / STEP**2 for i in range(3)]
    for i, j in ((0, 1), (0, 2), (1, 2)):
        corner = {(p, q): moved((i, p), (j, q)) for p in (-1, 1) for q in (-1, 1)}
        terms.append((corner[-1, -1] - corner[-1, 1] - corner[1, -1] + corner[1, 1]) / (2 * STEP**2))
    wanted = np.concatenate(terms)
    found = np.linalg.lstsq(np.stack(basis).T, wanted.T, rcond=None)[0]
    found = np.round(found * 1024) / 1024
    assert np.abs(np.stack(basis).T @ found - wanted.T).max() < 1e-6
    out = np.zeros((128, 100))
    out[: len(basis)] = found
    return out


def small_matrices():
    row = np.arange(128)[:, None]
    col = np.arange(1280)[None, :] // 128
    ratios = row // 16 == col[:, :768]
    moments = row == np.array(MOMENTS)[col]
    products = (row % 10 == col) & (row < 110)
    stencil = np.zeros((128, 128))
    stencil[:, :100] = stencil_moments()
    for m, lane in enumerate(MOMENTS):
        stencil[lane, 100 + m] = 1.0
    plain = [a.astype(jnp.bfloat16) for a in (ratios, moments, products)]
    whole = np.concatenate(plain + list(two_parts(stencil)), axis=1)
    return np.concatenate(np.split(whole, whole.shape[1] // 128, axis=1), axis=0)


def split2(x):
    hi = x.astype(BF16)
    return hi, (x - hi.astype(F32)).astype(BF16)


def split3(x):
    hi = x.astype(BF16)
    r = x - hi.astype(F32)
    mid = r.astype(BF16)
    return hi, mid, (r - mid.astype(F32)).astype(BF16)


def lane_sums(acc):
    ones = jnp.ones((16, 128), BF16)
    total = None
    for part in split3(acc):
        term = lax.dot_general(ones, part, (((1,), (1,)), ((), ())), preferred_element_type=F32)
        total = term if total is None else total + term
    return total[0:1]


def times(x, matrix):
    out = jnp.dot(jnp.concatenate(split3(x), axis=0), matrix, preferred_element_type=F32)
    return out[0:16] + out[16:32] + out[32:48]


def spread(row, matrix):
    lane = lax.broadcasted_iota(jnp.int32, (CELLS, 128), 1)
    cell = lax.broadcasted_iota(jnp.int32, (CELLS, 128), 0)
    own = jnp.where((lane & (CELLS - 1)) == cell, jnp.broadcast_to(row, (CELLS, 128)), 0.0)
    return times(own, matrix)


def columns(matrix, first, count):
    return jnp.concatenate([matrix[128 * i : 128 * i + 128, :] for i in range(first, first + count)], axis=1)


def rep(x, n):
    return jnp.concatenate([x] * n, axis=1)


def kernel(
    dist, free_h, area_h, vol_h, nb_h, wall_h, send_h, wts_h, mat_h, out,
    free, area, vol, nb, wall, send, distv, hs, hr, wts, mat, pb, fa, wb, fb, fc, relay,
    yt, zt, mt, prm, sb, lhs, fsend, frecv, mrecv,
    in_sem, out_sem, h_ssem, h_rsem, f_ssem, f_rsem, m_ssem, m_rsem, p_ssem, p_rsem,
    s_sem, z_ssem, z_rsem, r_ssem, r_rsem,
):
    space = lax.axis_index("space")
    vel = lax.axis_index("vel")
    blocks = lax.axis_size("space")
    has_below, has_above = space > 0, space < blocks - 1
    has_left, has_right = vel > 0, vel < VELS - 1

    loads = [pltpu.make_async_copy(dist.at[p], distv.at[p], in_sem.at[p]) for p in range(PLANES)]
    small = [
        pltpu.make_async_copy(src, dst, s_sem.at[i])
        for i, (src, dst) in enumerate(
            ((area_h, area), (nb_h, nb), (wall_h, wall), (vol_h, vol), (send_h, send), (free_h, free))
        )
    ]
    late = [
        pltpu.make_async_copy(src, dst, s_sem.at[6 + i]) for i, (src, dst) in enumerate(((wts_h, wts), (mat_h, mat)))
    ]
    for copy in small + loads + late:
        copy.start()

    barrier = pltpu.get_barrier_semaphore()
    for d in range(1, VELS):
        pl.semaphore_signal(barrier, 1, device_id=(space, lax.rem(vel + d, VELS)), device_id_type=MESH)

    @pl.when(has_below)
    def _():
        pl.semaphore_signal(barrier, 1, device_id=(space - 1, vel), device_id_type=MESH)

    @pl.when(has_above)
    def _():
        pl.semaphore_signal(barrier, 1, device_id=(space + 1, vel), device_id_type=MESH)

    flat = lax.broadcasted_iota(jnp.int32, (CELLS, FLAT), 1).astype(F32)
    row = jnp.floor((flat + 0.5) / NV)
    y = (row - (NV - 1) / 2.0) * STEP
    z = (flat - row * NV - (NV - 1) / 2.0) * STEP
    yt[...] = y
    zt[...] = z
    mt[...] = jnp.exp(-(y * y + z * z) / 2.0)
    for buf, count in ((fa, PLANES + 4), (fb, PLANES + 2)):
        for plane in range(count):
            buf[plane, :, 0:MARGIN] = jnp.zeros((CELLS, MARGIN), F32)
            buf[plane, :, MARGIN + FLAT :] = jnp.zeros((CELLS, MARGIN), F32)

    @pl.when(jnp.logical_not(has_left))
    def _():
        for plane in (fa.at[0], fa.at[1], fb.at[0]):
            plane[...] = jnp.zeros((CELLS, WIDE), F32)

    @pl.when(jnp.logical_not(has_right))
    def _():
        for plane in (fa.at[PLANES + 2], fa.at[PLANES + 3], fb.at[PLANES + 1]):
            plane[...] = jnp.zeros((CELLS, WIDE), F32)

    for copy in small:
        copy.wait()

    prm[...] = jnp.zeros((32, 128), F32)
    for i in range(3):
        prm[6 * i : 6 * i + 6, 0:CELLS] = area[i]
    prm[18:24, 0:CELLS] = nb[...].astype(F32)
    prm[24:30, 0:CELLS] = wall[...].astype(F32)
    prm[30:31, 0:CELLS] = DT / vol[...]
    cols = prm[...].T[0:CELLS]
    for r in range(31):
        sb[r] = jnp.broadcast_to(cols[:, r : r + 1], (CELLS, 128))
    lane = lax.broadcasted_iota(jnp.int32, (CELLS, 64), 1) & 31
    for s in range(FACES):
        inside = (lane.astype(F32) == sb[18 + s][:, 0:64]) & (sb[24 + s][:, 0:64] < 0.5)
        lhs[16 * s : 16 * s + 16, :] = jnp.where(inside, 1.0, 0.0).astype(BF16)

    for copy in loads:
        copy.wait()
    for p in range(PLANES):
        for side in range(2):
            for r in range(HALO):
                hs[side, p, r : r + 1, :] = distv[p, pl.ds(send[side, r], 1), :]

    xs = {p: ((vel * PLANES + p).astype(F32) - (NV - 1) / 2.0) * STEP for p in range(-2, PLANES + 2)}
    mx = {p: jnp.exp(jnp.full((CELLS, 128), -0.5, F32) * (x * x)) for p, x in xs.items()}

    def gather_copy(src, dst, ssem, rsem, d):
        return pltpu.make_async_remote_copy(
            src_ref=src, dst_ref=dst.at[d], send_sem=ssem.at[d], recv_sem=rsem.at[d],
            device_id=(space, lax.rem(vel + d, VELS)), device_id_type=MESH,
        )

    def total(src, dst, ssem, rsem):
        acc = src[...]
        for d in range(1, VELS):
            gather_copy(src, dst, ssem, rsem, d).wait_recv()
            acc = acc + dst[d]
        return acc

    def flux_plane(p, carry):
        sx = [sb[s] * xs[p] for s in range(FACES)]

        def step(t, carry):
            off = pl.multiple_of(t * 256, 128)
            outs, ins = list(carry[:FACES]), list(carry[FACES:])
            for j in range(2):
                o = pl.ds(off + 128 * j, 128)
                dd, yy, zz = distv[p, :, o], yt[:, o], zt[:, o]
                mm = mt[:, o] * mx[p]
                for s in range(FACES):
                    w = jnp.maximum(sx[s] + sb[6 + s] * yy + sb[12 + s] * zz, 0.0)
                    outs[s] = outs[s] + w * dd
                    ins[s] = ins[s] + w * mm
            return tuple(outs + ins)

        return lax.fori_loop(0, FLAT // 256, step, carry)

    carry = tuple(jnp.zeros((CELLS, 128), F32) for _ in range(2 * FACES))
    for p in range(PLANES):
        carry = flux_plane(p, carry)
    fsend[0:1, 0:96] = lane_sums(jnp.concatenate(carry[:FACES], axis=0))
    fsend[0:1, 128:224] = lane_sums(jnp.concatenate(carry[FACES:], axis=0))
    fsend[0:1, 96:128] = jnp.zeros((1, 32), F32)
    fsend[0:1, 224:256] = jnp.ones((1, 32), F32)
    peers = VELS - 1 + has_below.astype(jnp.int32) + has_above.astype(jnp.int32)
    pl.semaphore_wait(barrier, peers)

    def halo(side, target):
        return pltpu.make_async_remote_copy(
            src_ref=hs.at[side], dst_ref=hr.at[1 - side], send_sem=h_ssem.at[side], recv_sem=h_rsem.at[1 - side],
            device_id=(target, vel), device_id_type=MESH,
        )

    @pl.when(has_above)
    def _():
        halo(1, space + 1).start()

    @pl.when(has_below)
    def _():
        halo(0, space - 1).start()

    @pl.when(jnp.logical_not(has_below))
    def _():
        for p in range(PLANES):
            hr[0, p] = jnp.broadcast_to(free[p : p + 1, :], (HALO, FLAT))

    @pl.when(jnp.logical_not(has_above))
    def _():
        for p in range(PLANES):
            hr[1, p] = jnp.broadcast_to(free[p : p + 1, :], (HALO, FLAT))

    for d in range(1, VELS):
        gather_copy(fsend, frecv, f_ssem, f_rsem, d).start()
    @pl.when(has_below)
    def _():
        halo(1, space + 1).wait_recv()

    @pl.when(has_above)
    def _():
        halo(0, space - 1).wait_recv()

    y_at, z_at = lax.rem(vel, LANES), vel // LANES

    def sides(right):
        return (LANES - 1, 0, 1, z_at < LANES - 1) if right else (0, LANES - 1, -1, z_at > 0)

    def ends(right):
        return (pl.ds(1, 2), pl.ds(0, 2)) if right else (pl.ds(0, 2), pl.ds(PLANES + 2, 2))

    def lanes_of(right, q):
        first, last = PARTS[q if right else LANES - 1 - q]
        return first, last - first

    def near_copy(right):
        src, dst = ends(right)
        i = 1 if right else 0
        return pltpu.make_async_remote_copy(
            src_ref=pb.at[src], dst_ref=fa.at[dst, :, pl.ds(MARGIN, FLAT)], send_sem=p_ssem.at[i], recv_sem=p_rsem.at[i],
            device_id=(space, vel + 1 if right else vel - 1), device_id_type=MESH,
        )

    def part_copy(right, q):
        home, other, dz, _ = sides(right)
        src, dst = ends(right)
        first, count = lanes_of(right, q)
        lanes, wide = pl.ds(128 * first, 128 * count), pl.ds(MARGIN + 128 * first, 128 * count)
        i = 1 if right else 0
        if q == home:
            dst_ref, recv, to = fa.at[dst, :, wide], z_rsem.at[i, q], (z_at + dz) * LANES + other
        else:
            dst_ref, recv, to = relay.at[i, :, :, pl.ds(0, 128 * count)], r_rsem.at[i], z_at * LANES + q
        return pltpu.make_async_remote_copy(
            src_ref=pb.at[src, :, lanes], dst_ref=dst_ref, send_sem=z_ssem.at[i, q], recv_sem=recv,
            device_id=(space, to), device_id_type=MESH,
        )

    def relay_copy(right, q):
        home, other, dz, _ = sides(right)
        src, dst = ends(right)
        first, count = lanes_of(right, q)
        lanes, wide = pl.ds(128 * first, 128 * count), pl.ds(MARGIN + 128 * first, 128 * count)
        i = 1 if right else 0
        return pltpu.make_async_remote_copy(
            src_ref=relay.at[i, :, :, pl.ds(0, 128 * count)], dst_ref=fa.at[dst, :, wide],
            send_sem=r_ssem.at[i], recv_sem=z_rsem.at[i, q],
            device_id=(space, (z_at + dz) * LANES + other), device_id_type=MESH,
        )

    def send_plane(right):
        home, _, _, inner = sides(right)

        @pl.when(y_at != home)
        def _():
            near_copy(right).start()

        @pl.when((y_at == home) & inner)
        def _():
            for q in range(LANES):
                part_copy(right, q).start()

    def pass_on():
        for right in (True, False):
            home, _, _, inner = sides(right)
            for q in range(LANES):
                if q != home:

                    @pl.when((y_at == q) & inner)
                    def _():
                        part_copy(right, q).wait_recv()
                        relay_copy(right, q).start()

    def recv_planes():
        for right in (True, False):
            home, other, _, _ = sides(right)
            from_z = z_at > 0 if right else z_at < LANES - 1

            @pl.when(y_at != other)
            def _():
                near_copy(right).wait_recv()

            @pl.when((y_at == other) & from_z)
            def _():
                for q in range(LANES):
                    if q == home:
                        part_copy(right, q).wait_recv()
                    else:
                        relay_copy(right, q).wait_recv()

    def end_planes():
        for right in (True, False):
            home, _, _, inner = sides(right)

            @pl.when(y_at != home)
            def _():
                near_copy(right).wait_send()

            @pl.when((y_at == home) & inner)
            def _():
                for q in range(LANES):
                    part_copy(right, q).wait_send()

            for q in range(LANES):
                if q != home:

                    @pl.when((y_at == q) & inner)
                    def _():
                        relay_copy(right, q).wait_send()

    def flow_plane(p):
        sx = [sb[s] * xs[p] for s in range(FACES)]
        scale = sb[30]

        def step(t, acc):
            off = pl.multiple_of(t * 256, 128)
            o = pl.ds(off, 256)
            ext = jnp.concatenate([distv[p, :, o], hr[0, p, :, o], hr[1, p, :, o], jnp.zeros((8, 256), F32)], axis=0)
            picked = jnp.dot(lhs[...], jnp.concatenate(split2(ext), axis=0), preferred_element_type=F32)
            for j in range(2):
                o = pl.ds(off + 128 * j, 128)
                dd, yy, zz = distv[p, :, o], yt[:, o], zt[:, o]
                out_sum, in_sum = None, None
                for s in range(FACES):
                    w = sx[s] + sb[6 + s] * yy + sb[12 + s] * zz
                    up = jnp.maximum(w, 0.0)
                    term = (w - up) * picked[16 * s : 16 * s + 16, 128 * j : 128 * j + 128]
                    out_sum = up if s == 0 else out_sum + up
                    in_sum = term if s == 0 else in_sum + term
                pb[p, :, o] = dd - scale * (out_sum * dd + in_sum)
            return acc

        lax.fori_loop(0, FLAT // 256, step, 0, unroll=True)

    flow_plane(1)
    flow_plane(0)
    send_plane(False)
    flow_plane(2)
    send_plane(True)

    for copy in late:
        copy.wait()

    flux = total(fsend, frecv, f_ssem, f_rsem)
    ratio = spread(flux[:, 0:128] / jnp.where(flux[:, 128:256] > 0.0, flux[:, 128:256], 1.0), columns(mat, 0, 6))
    for s in range(FACES):
        sb[18 + s] = jnp.where(sb[24 + s] > 0.5, -sb[30] * ratio[:, 128 * s : 128 * s + 128], 0.0)

    def wall_planes(off, planes):
        o = pl.ds(off, 128)
        yy, zz, mm = yt[:, o], zt[:, o], mt[:, o]
        sums = [None] * len(planes)
        for s in range(FACES):
            along = sb[6 + s] * yy + sb[12 + s] * zz
            for i, p in enumerate(planes):
                term = jnp.minimum(sb[s] * xs[p] + along, 0.0) * sb[18 + s]
                sums[i] = term if s == 0 else sums[i] + term
        return [sums[i] * (mm * mx[p]) for i, p in enumerate(planes)]

    def add_walls(t, acc):
        off = pl.multiple_of(t * 256, 128)
        halves = []
        for j in range(2):
            walls = wall_planes(off + 128 * j, range(PLANES))
            now = [pb[p, :, pl.ds(off + 128 * j, 128)] + walls[p] for p in range(PLANES)]
            for p in range(PLANES):
                fa[p + 2, :, pl.ds(off + 128 * j + MARGIN, 128)] = now[p]
            halves.append(jnp.concatenate(now, axis=0))
        parts = jnp.concatenate(split3(jnp.concatenate(halves, axis=1)), axis=0)
        return acc + jnp.dot(parts, wts[pl.ds(off, 256), :], preferred_element_type=F32)

    rows = PLANES * CELLS
    acc = lax.fori_loop(0, FLAT // 256, add_walls, jnp.zeros((3 * rows, 128), F32), unroll=True)
    acc = acc[0:rows] + acc[rows : 2 * rows] + acc[2 * rows :]
    acc = acc + pltpu.roll(acc, 64, 1)
    lane = lax.broadcasted_iota(jnp.int32, (CELLS, 128), 1) & 63
    sent = None
    for p in range(PLANES):
        face = 0.0
        if p == 0:
            face = jnp.where(has_left, 0.0, 1.0)
        if p == PLANES - 1:
            face = jnp.where(has_right, 0.0, 1.0)
        weight = jnp.where(
            lane < AT_X, 1.0, jnp.where(lane < AT_XX, xs[p], jnp.where(lane < AT_FACE, xs[p] * xs[p], face))
        )
        term = weight * acc[CELLS * p : CELLS * p + CELLS]
        sent = term if p == 0 else sent + term
    low = lax.broadcasted_iota(jnp.int32, (8, 128), 1) < 64
    mrecv[0] = jnp.where(low, sent[0:8], sent[8:16])
    for d in range(1, VELS):
        gather_copy(mrecv.at[0], mrecv, m_ssem, m_rsem, d).start()

    halo_planes = (-2, -1, PLANES, PLANES + 1)

    def halo_walls(t, acc):
        off = pl.multiple_of(t * 128, 128)
        walls = wall_planes(off, halo_planes)
        for i in range(4):
            wb[i, :, pl.ds(off, 128)] = walls[i]
        return acc

    pass_on()
    lax.fori_loop(0, FLAT // 128, halo_walls, 0, unroll=3)

    for d in range(1, VELS):
        gather_copy(mrecv.at[0], mrecv, m_ssem, m_rsem, d).wait_recv()
    packed = mrecv[0]
    for d in range(1, VELS):
        packed = packed + mrecv[d]

    def unpack(x):
        return jnp.concatenate([x, pltpu.roll(x, 64, 1)], axis=0)

    lane = lax.broadcasted_iota(jnp.int32, (CELLS, 128), 1)
    on_face = (lane >= AT_FACE) & (lane < 64)
    least = unpack(mrecv[vel])
    largest = unpack(mrecv[lax.rem(vel + 1, VELS)])
    sums = jnp.where(lane < AT_FACE, unpack(packed), jnp.where(on_face, least, 0.0))
    sums = sums + pltpu.roll(jnp.where(on_face, largest, 0.0), len(X_FACE), 1)

    def coefficients(allm):
        m = [allm[:, 128 * i : 128 * i + 128] for i in range(10)]
        inv = 1.0 / m[0]
        ux, uy, uz = m[1] * inv, m[2] * inv, m[3] * inv
        cxx, cyy, czz = m[4] * inv - ux * ux, m[5] * inv - uy * uy, m[6] * inv - uz * uz
        cxy, cxz, cyz = m[7] * inv - ux * uy, m[8] * inv - ux * uz, m[9] * inv - uy * uz
        theta = (cxx + cyy + czz) / 3.0
        a = (RATE * STEP**3) * m[0] * jnp.exp(0.19 * jnp.log(theta))
        lx, ly, lz = 0.5 * (theta + cxx), 0.5 * (theta + cyy), 0.5 * (theta + czz)
        terms = (a, -a * ux, -a * uy, -a * uz, a * lx, a * ly, a * lz, 0.5 * a * cxy, 0.5 * a * cxz, 0.5 * a * cyz)
        return terms, dict(
            ux=ux, a=a, k0=1.0 - 32.0 * a * (lx + ly + lz), lx=16.0 * a * lx,
            ys=a * (16.0 * ly + 0.5), a2=2.0 * a, a2uy=2.0 * a * uy, a2uz=2.0 * a * uz, zq=16.0 * a * lz,
            gxy=4.0 * a * cxy, gxz=4.0 * a * cxz, gyz=4.0 * a * cyz,
        )

    terms, c1 = coefficients(times(sums, columns(mat, 6, 10)))
    factor = jnp.where(lane < 110, 1.0, 0.0)
    for t in range(10):
        factor = jnp.where((lane >= 10 * t) & (lane < 10 * t + 10), terms[t], factor)
    stencil = times(sums, columns(mat, 26, 2))
    _, c2 = coefficients(times(factor * (stencil[:, 0:128] + stencil[:, 128:256]), columns(mat, 16, 10)))

    width = 768

    def relax_plane(src, at, dst, dst_at, p, c):
        n = width // 128
        margin = MARGIN if dst.shape[-1] == WIDE else 0
        drift_n = c["a2"] * (xs[p] + STEP - c["ux"]) + c["lx"]
        drift_p = c["lx"] - c["a2"] * (xs[p] - STEP - c["ux"])
        kn, kp, k0 = rep(drift_n, n), rep(drift_p, n), rep(c["k0"], n)
        ys, a2, a2uy, a2uz, zq = (rep(c[q], n) for q in ("ys", "a2", "a2uy", "a2uz", "zq"))
        gxy, gxz, gyz = (rep(c[q], n) for q in ("gxy", "gxz", "gyz"))

        def step(t, acc):
            off = pl.multiple_of(t * width, 128)
            win = pl.ds(off, width + 2 * MARGIN)
            cen = pl.ds(off, width)
            cw, nw, pw = src[at, :, win], src[at + 1, :, win], src[at - 1, :, win]
            xw = nw - pw
            yy, zz = yt[:, cen], zt[:, cen]
            total_w = width + 2 * MARGIN

            def up(v):
                return pltpu.roll(v, total_w - NV, 1)[:, MARGIN : MARGIN + width]

            def down(v):
                return pltpu.roll(v, NV, 1)[:, MARGIN : MARGIN + width]

            cc, nn, pp = (v[:, MARGIN : MARGIN + width] for v in (cw, nw, pw))
            u, d = up(cw), down(cw)
            diff = u - d
            res = k0 * cc + kn * nn + kp * pp
            res = res + ys * (u + d) + (a2 * yy - a2uy) * diff + gxy * (up(xw) - down(xw))
            cross = gxz * (nn - pp) + gyz * diff
            zr = a2 * zz - a2uz
            plus = (zq + zr) * cc + cross
            minus = (zq - zr) * cc - cross
            edge = (NV - 1) / 2.0 * STEP
            res = res + jnp.where(zz < edge - 0.1, pltpu.roll(plus, width - 1, 1), 0.0)
            res = res + jnp.where(zz > 0.1 - edge, pltpu.roll(minus, 1, 1), 0.0)
            dst[dst_at, :, pl.ds(off + margin, width)] = res
            return acc

        lax.fori_loop(0, FLAT // width, step, 0, unroll=True)

    relax_plane(fa, 3, fb, 2, 1, c1)
    recv_planes()

    @pl.when(has_left)
    def _():
        for i in range(2):
            fa[i, :, MARGIN : MARGIN + FLAT] = fa[i, :, MARGIN : MARGIN + FLAT] + wb[i]
        relax_plane(fa, 1, fb, 0, -1, c1)

    @pl.when(has_right)
    def _():
        for i in range(2):
            plane = PLANES + 2 + i
            fa[plane, :, MARGIN : MARGIN + FLAT] = fa[plane, :, MARGIN : MARGIN + FLAT] + wb[2 + i]
        relax_plane(fa, PLANES + 2, fb, PLANES + 1, PLANES, c1)

    relax_plane(fa, 2, fb, 1, 0, c1)
    relax_plane(fa, 4, fb, 3, 2, c1)
    stores = [pltpu.make_async_copy(fc.at[p], out.at[p], out_sem.at[p]) for p in range(PLANES)]
    for p in range(PLANES):
        relax_plane(fb, p + 1, fc, p, p, c2)
        stores[p].start()

    @pl.when(has_above)
    def _():
        halo(1, space + 1).wait_send()

    @pl.when(has_below)
    def _():
        halo(0, space - 1).wait_send()

    for d in range(1, VELS):
        gather_copy(fsend, frecv, f_ssem, f_rsem, d).wait_send()
        gather_copy(mrecv.at[0], mrecv, m_ssem, m_rsem, d).wait_send()
    end_planes()
    for copy in stores:
        copy.wait()


def body(distribution, freestream, face_area, cell_volume, neighbours, wall_flags, send_cells):
    dma = pltpu.SemaphoreType.DMA
    hbm = pl.BlockSpec(memory_space=pltpu.HBM)
    anyw = pl.BlockSpec(memory_space=pl.ANY)
    new = pl.pallas_call(
        kernel,
        out_shape=jax.ShapeDtypeStruct((PLANES, CELLS, FLAT), F32),
        in_specs=[hbm] * 9,
        out_specs=anyw,
        scratch_shapes=[
            pltpu.VMEM((PLANES, FLAT), F32),
            pltpu.VMEM((3, FACES, CELLS), F32),
            pltpu.VMEM((1, CELLS), F32),
            pltpu.VMEM((FACES, CELLS), jnp.int32),
            pltpu.VMEM((FACES, CELLS), jnp.int32),
            pltpu.SMEM((2, HALO), jnp.int32),
            pltpu.VMEM((PLANES, CELLS, FLAT), F32),
            pltpu.VMEM((2, PLANES, HALO, FLAT), F32),
            pltpu.VMEM((2, PLANES, HALO, FLAT), F32),
            pltpu.VMEM((FLAT, 128), BF16),
            pltpu.VMEM((28 * 128, 128), BF16),
            pltpu.VMEM((PLANES, CELLS, FLAT), F32),
            pltpu.VMEM((PLANES + 4, CELLS, WIDE), F32),
            pltpu.VMEM((4, CELLS, FLAT), F32),
            pltpu.VMEM((PLANES + 2, CELLS, WIDE), F32),
            pltpu.VMEM((PLANES, CELLS, FLAT), F32),
            pltpu.VMEM((2, 2, CELLS, 4 * 128), F32),
            pltpu.VMEM((CELLS, FLAT), F32),
            pltpu.VMEM((CELLS, FLAT), F32),
            pltpu.VMEM((CELLS, FLAT), F32),
            pltpu.VMEM((32, 128), F32),
            pltpu.VMEM((32, CELLS, 128), F32),
            pltpu.VMEM((96, 64), BF16),
            pltpu.VMEM((1, 256), F32),
            pltpu.VMEM((VELS, 1, 256), F32),
            pltpu.VMEM((VELS, 8, 128), F32),
            dma((PLANES,)), dma((PLANES,)), dma((2,)), dma((2,)),
            dma((VELS,)), dma((VELS,)), dma((VELS,)), dma((VELS,)), dma((2,)), dma((2,)),
            dma((8,)), dma((2, LANES)), dma((2, LANES)), dma((2,)), dma((2,)),
        ],
        compiler_params=pltpu.CompilerParams(
            collective_id=0, has_side_effects=True, vmem_limit_bytes=63 * 1024 * 1024
        ),
    )(
        jnp.transpose(distribution, (1, 0, 2)), freestream, face_area, cell_volume.reshape(1, CELLS), neighbours,
        wall_flags, send_cells, jnp.asarray(sum_weights()), jnp.asarray(small_matrices()),
    )
    return jnp.transpose(new, (1, 0, 2))


def solution(mesh):
    in_specs = (
        P("space", "vel", None),
        P("vel", None),
        P(None, None, "space"),
        P("space"),
        P(None, "space"),
        P(None, "space"),
        P(None, "space"),
    )
    out_specs = P("space", "vel", None)
    return jax.shard_map(body, mesh=mesh, in_specs=in_specs, out_specs=out_specs, check_vma=False)
```

```python
import jax
import jax.numpy as jnp
import numpy as np
from jax import lax
from jax.experimental import pallas as pl
from jax.experimental.pallas import tpu as pltpu
from jax.sharding import PartitionSpec as P

NV = 48
FLAT = NV * NV
STEP = 0.25
DT = 0.02
RATE = 0.002
FACES = 6
HALO = 4
CELLS = 16
PLANES = 3
MARGIN = 128
WIDE = FLAT + 2 * MARGIN
VELS = 16
WALL_ROWS = FACES * PLANES * CELLS
LANES = 4
PARTS = ((8, 12), (12, 15), (15, 18), (0, 8))
MESH = pl.DeviceIdType.MESH
F32 = jnp.float32
BF16 = jnp.bfloat16


PLANE_SUMS = 22
TIMES_X = (0, 1, 2, 6, 7, 9, 10, 12, 13, 15, 16, 18, 19, 20, 21)
TIMES_XX = (0, 6, 9, 12, 15, 18, 19, 20, 21)
X_FACE = tuple(range(18))
SENT = tuple(range(PLANE_SUMS)) + TIMES_X + TIMES_XX + X_FACE
AT_X, AT_XX, AT_FACE = 22, 37, 46
MOMENTS = (0, AT_X, 1, 2, AT_XX, 3, 4, AT_X + 1, AT_X + 2, 5)


def plane_sums(j, k):
    y, z = (j - (NV - 1) / 2.0) * STEP, (k - (NV - 1) / 2.0) * STEP
    one = np.ones_like(y)
    lo_y, hi_y, lo_z, hi_z = ((at == end).astype(np.float64) for at in (j, k) for end in (0, NV - 1))
    sums = [one, y, z, y * y, z * z, y * z]
    for face in (lo_y, hi_y):
        sums += [face, face * z, face * z * z]
    for face in (lo_z, hi_z):
        sums += [face, face * y, face * y * y]
    sums += [lo_y * lo_z, lo_y * hi_z, hi_y * lo_z, hi_y * hi_z]
    return np.stack(sums)


def two_parts(x):
    hi = x.astype(jnp.bfloat16)
    return hi, (x - hi.astype(np.float64)).astype(jnp.bfloat16)


def sum_weights():
    at = np.arange(FLAT)
    weights = plane_sums(at // NV, at % NV)[list(SENT)].T
    return np.concatenate(two_parts(weights), axis=1)


def stencil_moments():
    line = np.array([0, 1, 2, 17, 23, 30, 45, 46, 47])
    at = np.stack(np.meshgrid(line, line, line, indexing="ij")).reshape(3, -1)

    def velocity(index):
        return (index - (NV - 1) / 2.0) * STEP

    planes = plane_sums(at[1], at[2])
    x = velocity(at[0])
    basis = [planes[c] for c in range(PLANE_SUMS)] + [planes[c] * x for c in TIMES_X] + [planes[c] * x * x for c in TIMES_XX]
    for end in (0, NV - 1):
        basis += [planes[c] * (at[0] == end) for c in X_FACE]

    def polynomials(index):
        v = velocity(index)
        inside = np.all((index >= 0) & (index < NV), axis=0)
        vx, vy, vz = v
        return np.stack([np.ones_like(vx), vx, vy, vz, vx * vx, vy * vy, vz * vz, vx * vy, vx * vz, vy * vz]) * inside

    def moved(*steps):
        index = at.copy()
        for axis, step in steps:
            index[axis] += step
        return polynomials(index)

    v = velocity(at)
    first = [(moved((i, -1)) - moved((i, 1))) / (2 * STEP) for i in range(3)]
    terms = [sum(v[i] * first[i] for i in range(3))] + first
    terms += [(moved((i, -1)) - 2 * moved() + moved((i, 1))) / STEP**2 for i in range(3)]
    for i, j in ((0, 1), (0, 2), (1, 2)):
        corner = {(p, q): moved((i, p), (j, q)) for p in (-1, 1) for q in (-1, 1)}
        terms.append((corner[-1, -1] - corner[-1, 1] - corner[1, -1] + corner[1, 1]) / (2 * STEP**2))
    wanted = np.concatenate(terms)
    found = np.linalg.lstsq(np.stack(basis).T, wanted.T, rcond=None)[0]
    found = np.round(found * 1024) / 1024
    assert np.abs(np.stack(basis).T @ found - wanted.T).max() < 1e-6
    out = np.zeros((128, 100))
    out[: len(basis)] = found
    return out


def small_matrices():
    row = np.arange(128)[:, None]
    col = np.arange(1280)[None, :] // 128
    ratios = row // 16 == col[:, :768]
    moments = row == np.array(MOMENTS)[col]
    products = (row % 10 == col) & (row < 110)
    stencil = np.zeros((128, 128))
    stencil[:, :100] = stencil_moments()
    for m, lane in enumerate(MOMENTS):
        stencil[lane, 100 + m] = 1.0
    plain = [a.astype(jnp.bfloat16) for a in (ratios, moments, products)]
    whole = np.concatenate(plain + list(two_parts(stencil)), axis=1)
    return np.concatenate(np.split(whole, whole.shape[1] // 128, axis=1), axis=0)


def split2(x):
    hi = x.astype(BF16)
    return hi, (x - hi.astype(F32)).astype(BF16)


def split3(x):
    hi = x.astype(BF16)
    r = x - hi.astype(F32)
    mid = r.astype(BF16)
    return hi, mid, (r - mid.astype(F32)).astype(BF16)


def lane_sums(acc):
    ones = jnp.ones((16, 128), BF16)
    total = None
    for part in split3(acc):
        term = lax.dot_general(ones, part, (((1,), (1,)), ((), ())), preferred_element_type=F32)
        total = term if total is None else total + term
    return total[0:1]


def times(x, matrix):
    out = jnp.dot(jnp.concatenate(split3(x), axis=0), matrix, preferred_element_type=F32)
    return out[0:16] + out[16:32] + out[32:48]


def spread(row, matrix):
    lane = lax.broadcasted_iota(jnp.int32, (CELLS, 128), 1)
    cell = lax.broadcasted_iota(jnp.int32, (CELLS, 128), 0)
    own = jnp.where((lane & (CELLS - 1)) == cell, jnp.broadcast_to(row, (CELLS, 128)), 0.0)
    return times(own, matrix)


def columns(matrix, first, count):
    return jnp.concatenate([matrix[128 * i : 128 * i + 128, :] for i in range(first, first + count)], axis=1)


FAR_FIRST = sorted(range(1, VELS), key=lambda d: -min(d, VELS - d))


def rep(x, n):
    return jnp.concatenate([x] * n, axis=1)


def kernel(
    dist, free_h, area_h, vol_h, nb_h, wall_h, send_h, wts_h, mat_h, out,
    free, area, vol, nb, wall, send, distv, hs, hr, wts, mat, pb, fa, wb, fb, relay, qm, fq, pm,
    yt, zt, mt, prm, sb, lhs, fsend, frecv, mrecv,
    in_sem, h_ssem, h_rsem, f_ssem, f_rsem, m_ssem, m_rsem, p_ssem, p_rsem,
    s_sem, z_ssem, z_rsem, r_ssem, r_rsem,
):
    space = lax.axis_index("space")
    vel = lax.axis_index("vel")
    blocks = lax.axis_size("space")
    has_below, has_above = space > 0, space < blocks - 1
    has_left, has_right = vel > 0, vel < VELS - 1

    loads = [pltpu.make_async_copy(dist.at[p], distv.at[p], in_sem.at[p]) for p in range(PLANES)]
    small = [
        pltpu.make_async_copy(src, dst, s_sem.at[i])
        for i, (src, dst) in enumerate(
            ((area_h, area), (nb_h, nb), (wall_h, wall), (vol_h, vol), (send_h, send), (free_h, free))
        )
    ]
    late = [
        pltpu.make_async_copy(src, dst, s_sem.at[6 + i]) for i, (src, dst) in enumerate(((wts_h, wts), (mat_h, mat)))
    ]
    for copy in small + loads + late:
        copy.start()

    barrier = pltpu.get_barrier_semaphore()
    for d in FAR_FIRST:
        pl.semaphore_signal(barrier, 1, device_id=(space, lax.rem(vel + d, VELS)), device_id_type=MESH)

    @pl.when(has_below)
    def _():
        pl.semaphore_signal(barrier, 1, device_id=(space - 1, vel), device_id_type=MESH)

    @pl.when(has_above)
    def _():
        pl.semaphore_signal(barrier, 1, device_id=(space + 1, vel), device_id_type=MESH)

    flat = lax.broadcasted_iota(jnp.int32, (CELLS, FLAT), 1).astype(F32)
    row = jnp.floor((flat + 0.5) / NV)
    y = (row - (NV - 1) / 2.0) * STEP
    z = (flat - row * NV - (NV - 1) / 2.0) * STEP
    yt[...] = y
    zt[...] = z
    mt[...] = jnp.exp(-(y * y + z * z) / 2.0)
    for buf, count in ((fa, PLANES + 4), (fb, PLANES + 2)):
        for plane in range(count):
            buf[plane, :, 0:MARGIN] = jnp.zeros((CELLS, MARGIN), F32)
            buf[plane, :, MARGIN + FLAT :] = jnp.zeros((CELLS, MARGIN), F32)

    @pl.when(jnp.logical_not(has_left))
    def _():
        for plane in (fa.at[0], fa.at[1], fb.at[0]):
            plane[...] = jnp.zeros((CELLS, WIDE), F32)

    @pl.when(jnp.logical_not(has_right))
    def _():
        for plane in (fa.at[PLANES + 2], fa.at[PLANES + 3], fb.at[PLANES + 1]):
            plane[...] = jnp.zeros((CELLS, WIDE), F32)

    for copy in small:
        copy.wait()

    prm[...] = jnp.zeros((32, 128), F32)
    for i in range(3):
        prm[6 * i : 6 * i + 6, 0:CELLS] = area[i]
    prm[18:24, 0:CELLS] = nb[...].astype(F32)
    prm[24:30, 0:CELLS] = wall[...].astype(F32)
    prm[30:31, 0:CELLS] = DT / vol[...]
    cols = prm[...].T[0:CELLS]
    for r in range(31):
        sb[r] = jnp.broadcast_to(cols[:, r : r + 1], (CELLS, 128))
    lane = lax.broadcasted_iota(jnp.int32, (CELLS, 64), 1) & 31
    for s in range(FACES):
        inside = (lane.astype(F32) == sb[18 + s][:, 0:64]) & (sb[24 + s][:, 0:64] < 0.5)
        lhs[16 * s : 16 * s + 16, :] = jnp.where(inside, 1.0, 0.0).astype(BF16)

    for copy in loads:
        copy.wait()
    for p in range(PLANES):
        for side in range(2):
            for r in range(HALO):
                hs[side, p, r : r + 1, :] = distv[p, pl.ds(send[side, r], 1), :]

    def x_of(p):
        return ((vel * PLANES + p).astype(F32) - (NV - 1) / 2.0) * STEP

    xs = {p: x_of(p) for p in range(-2, PLANES + 2)}
    mx = {p: jnp.exp(jnp.full((CELLS, 128), -0.5, F32) * (x * x)) for p, x in xs.items()}

    def gather_copy(src, dst, ssem, rsem, d):
        return pltpu.make_async_remote_copy(
            src_ref=src, dst_ref=dst.at[d], send_sem=ssem.at[d], recv_sem=rsem.at[d],
            device_id=(space, lax.rem(vel + d, VELS)), device_id_type=MESH,
        )

    def total(src, dst, ssem, rsem):
        acc = src[...]
        for d in range(1, VELS):
            gather_copy(src, dst, ssem, rsem, d).wait_recv()
            acc = acc + dst[d]
        return acc

    def flux_plane(p, carry):
        sx = [sb[s] * xs[p] for s in range(FACES)]

        def step(t, carry):
            off = pl.multiple_of(t * 256, 128)
            outs, ins = list(carry[:FACES]), list(carry[FACES:])
            for j in range(2):
                o = pl.ds(off + 128 * j, 128)
                dd, yy, zz = distv[p, :, o], yt[:, o], zt[:, o]
                mm = mt[:, o] * mx[p]
                for s in range(FACES):
                    w = jnp.maximum(sx[s] + sb[6 + s] * yy + sb[12 + s] * zz, 0.0)
                    outs[s] = outs[s] + w * dd
                    ins[s] = ins[s] + w * mm
            return tuple(outs + ins)

        return lax.fori_loop(0, FLAT // 256, step, carry)

    carry = tuple(jnp.zeros((CELLS, 128), F32) for _ in range(2 * FACES))
    for p in range(PLANES):
        carry = flux_plane(p, carry)
    fsend[0:1, 0:96] = lane_sums(jnp.concatenate(carry[:FACES], axis=0))
    fsend[0:1, 128:224] = lane_sums(jnp.concatenate(carry[FACES:], axis=0))
    fsend[0:1, 96:128] = jnp.zeros((1, 32), F32)
    fsend[0:1, 224:256] = jnp.ones((1, 32), F32)
    peers = VELS - 1 + has_below.astype(jnp.int32) + has_above.astype(jnp.int32)
    pl.semaphore_wait(barrier, peers)

    def halo(side, p, target):
        return pltpu.make_async_remote_copy(
            src_ref=hs.at[side, p], dst_ref=hr.at[1 - side, p],
            send_sem=h_ssem.at[side, p], recv_sem=h_rsem.at[1 - side, p],
            device_id=(target, vel), device_id_type=MESH,
        )

    y_at, z_at = lax.rem(vel, LANES), vel // LANES
    first = jnp.where(y_at == LANES - 1, PLANES - 1, 0)
    order = (1, first, PLANES - 1 - first)
    for p in order:

        @pl.when(has_above)
        def _():
            halo(1, p, space + 1).start()

        @pl.when(has_below)
        def _():
            halo(0, p, space - 1).start()

    @pl.when(jnp.logical_not(has_below))
    def _():
        for p in range(PLANES):
            hr[0, p] = jnp.broadcast_to(free[p : p + 1, :], (HALO, FLAT))

    @pl.when(jnp.logical_not(has_above))
    def _():
        for p in range(PLANES):
            hr[1, p] = jnp.broadcast_to(free[p : p + 1, :], (HALO, FLAT))

    for d in FAR_FIRST:
        gather_copy(fsend, frecv, f_ssem, f_rsem, d).start()

    for copy in late:
        copy.wait()

    def unit_walls(t, acc):
        off = pl.multiple_of(t * 128, 128)
        o = pl.ds(off, 128)
        yy, zz, mm = yt[:, o], zt[:, o], mt[:, o]
        for s in range(FACES):
            along = sb[6 + s] * yy + sb[12 + s] * zz
            for p in range(PLANES):
                at = (s * PLANES + p) * CELLS
                hi, lo = split2(jnp.minimum(sb[s] * xs[p] + along, 0.0) * (mm * mx[p]))
                qm[at : at + CELLS, o] = hi
                qm[WALL_ROWS + at : WALL_ROWS + at + CELLS, o] = lo
        return acc

    lax.fori_loop(0, FLAT // 128, unit_walls, 0, unroll=3)
    unit = jnp.dot(qm[...], wts[...], preferred_element_type=F32)
    fq[...] = unit[0:WALL_ROWS] + unit[WALL_ROWS:]

    def sides(right):
        return (LANES - 1, 0, 1, z_at < LANES - 1) if right else (0, LANES - 1, -1, z_at > 0)

    def ends(right, n):
        return (1 + n, n) if right else (n, PLANES + 2 + n)

    def lanes_of(right, q):
        begin, last = PARTS[q if right else LANES - 1 - q]
        return begin, last - begin

    def near_copy(right, n):
        src, dst = ends(right, n)
        i = 1 if right else 0
        return pltpu.make_async_remote_copy(
            src_ref=pb.at[src], dst_ref=fa.at[dst, :, pl.ds(MARGIN, FLAT)],
            send_sem=p_ssem.at[i, n], recv_sem=p_rsem.at[i, n],
            device_id=(space, vel + 1 if right else vel - 1), device_id_type=MESH,
        )

    def part_copy(right, n, q):
        home, other, dz, _ = sides(right)
        src, dst = ends(right, n)
        begin, count = lanes_of(right, q)
        lanes, wide = pl.ds(128 * begin, 128 * count), pl.ds(MARGIN + 128 * begin, 128 * count)
        i = 1 if right else 0
        if q == home:
            dst_ref, recv, to = fa.at[dst, :, wide], z_rsem.at[i, q, n], (z_at + dz) * LANES + other
        else:
            dst_ref, recv, to = relay.at[i, n, :, pl.ds(0, 128 * count)], r_rsem.at[i, n], z_at * LANES + q
        return pltpu.make_async_remote_copy(
            src_ref=pb.at[src, :, lanes], dst_ref=dst_ref, send_sem=z_ssem.at[i, q, n], recv_sem=recv,
            device_id=(space, to), device_id_type=MESH,
        )

    def relay_copy(right, n, q):
        home, other, dz, _ = sides(right)
        src, dst = ends(right, n)
        begin, count = lanes_of(right, q)
        wide = pl.ds(MARGIN + 128 * begin, 128 * count)
        i = 1 if right else 0
        return pltpu.make_async_remote_copy(
            src_ref=relay.at[i, n, :, pl.ds(0, 128 * count)], dst_ref=fa.at[dst, :, wide],
            send_sem=r_ssem.at[i, n], recv_sem=z_rsem.at[i, q, n],
            device_id=(space, (z_at + dz) * LANES + other), device_id_type=MESH,
        )

    def send_plane(right, n):
        home, _, _, inner = sides(right)

        @pl.when(y_at != home)
        def _():
            near_copy(right, n).start()

        @pl.when((y_at == home) & inner)
        def _():
            for q in range(LANES):
                part_copy(right, n, q).start()

    def pass_on():
        for step in range(2):
            for right in (True, False):
                n = step if right else 1 - step
                home, _, _, inner = sides(right)
                for q in range(LANES):
                    if q != home:

                        @pl.when((y_at == q) & inner)
                        def _():
                            part_copy(right, n, q).wait_recv()
                            relay_copy(right, n, q).start()

    def recv_planes(right, when):
        home, other, _, _ = sides(right)
        from_z = z_at > 0 if right else z_at < LANES - 1

        @pl.when((y_at != other) & when)
        def _():
            for n in range(2):
                near_copy(right, n).wait_recv()

        @pl.when((y_at == other) & from_z & when)
        def _():
            for n in range(2):
                for q in range(LANES):
                    if q == home:
                        part_copy(right, n, q).wait_recv()
                    else:
                        relay_copy(right, n, q).wait_recv()

    def end_planes():
        for right in (True, False):
            home, _, _, inner = sides(right)

            @pl.when(y_at != home)
            def _():
                for n in range(2):
                    near_copy(right, n).wait_send()

            @pl.when((y_at == home) & inner)
            def _():
                for n in range(2):
                    for q in range(LANES):
                        part_copy(right, n, q).wait_send()

            for q in range(LANES):
                if q != home:

                    @pl.when((y_at == q) & inner)
                    def _():
                        for n in range(2):
                            relay_copy(right, n, q).wait_send()

    def flow_plane(p):
        x = x_of(p)
        sx = [sb[s] * x for s in range(FACES)]
        scale = sb[30]

        def step(t, acc):
            off = pl.multiple_of(t * 256, 128)
            o = pl.ds(off, 256)
            ext = jnp.concatenate([distv[p, :, o], hr[0, p, :, o], hr[1, p, :, o], jnp.zeros((8, 256), F32)], axis=0)
            picked = jnp.dot(lhs[...], jnp.concatenate(split2(ext), axis=0), preferred_element_type=F32)
            for j in range(2):
                o = pl.ds(off + 128 * j, 128)
                dd, yy, zz = distv[p, :, o], yt[:, o], zt[:, o]
                out_sum, in_sum = None, None
                for s in range(FACES):
                    w = sx[s] + sb[6 + s] * yy + sb[12 + s] * zz
                    up = jnp.maximum(w, 0.0)
                    term = (w - up) * picked[16 * s : 16 * s + 16, 128 * j : 128 * j + 128]
                    out_sum = up if s == 0 else out_sum + up
                    in_sum = term if s == 0 else in_sum + term
                f = dd - scale * (out_sum * dd + in_sum)
                pb[p, :, o] = f
                for i, part in enumerate(split3(f)):
                    pm[pl.ds(pl.multiple_of((i * PLANES + p) * CELLS, CELLS), CELLS), o] = part
            return acc

        lax.fori_loop(0, FLAT // 256, step, 0, unroll=True)

    for step, p in enumerate(order):

        @pl.when(has_below)
        def _():
            halo(1, p, space + 1).wait_recv()

        @pl.when(has_above)
        def _():
            halo(0, p, space - 1).wait_recv()

        flow_plane(p)
        if step == 0:
            send_plane(True, 0)
            send_plane(False, 1)
        else:

            @pl.when(p == PLANES - 1)
            def _():
                send_plane(True, 1)

            @pl.when(p == 0)
            def _():
                send_plane(False, 0)

    rows = PLANES * CELLS
    flow = jnp.dot(pm[...], wts[...], preferred_element_type=F32)
    flow = flow[0:rows] + flow[rows : 2 * rows] + flow[2 * rows :]

    flux = total(fsend, frecv, f_ssem, f_rsem)
    ratio = spread(flux[:, 0:128] / jnp.where(flux[:, 128:256] > 0.0, flux[:, 128:256], 1.0), columns(mat, 0, 6))
    for s in range(FACES):
        sb[18 + s] = jnp.where(sb[24 + s] > 0.5, -sb[30] * ratio[:, 128 * s : 128 * s + 128], 0.0)

    def wall_planes(off, planes):
        o = pl.ds(off, 128)
        yy, zz, mm = yt[:, o], zt[:, o], mt[:, o]
        sums = [None] * len(planes)
        for s in range(FACES):
            along = sb[6 + s] * yy + sb[12 + s] * zz
            for i, p in enumerate(planes):
                term = jnp.minimum(sb[s] * xs[p] + along, 0.0) * sb[18 + s]
                sums[i] = term if s == 0 else sums[i] + term
        return [sums[i] * (mm * mx[p]) for i, p in enumerate(planes)]

    acc = []
    for p in range(PLANES):
        plane = flow[CELLS * p : CELLS * p + CELLS]
        for s in range(FACES):
            at = (s * PLANES + p) * CELLS
            plane = plane + sb[18 + s] * fq[at : at + CELLS, :]
        acc.append(plane)
    acc = jnp.concatenate(acc, axis=0)
    acc = acc + pltpu.roll(acc, 64, 1)
    lane = lax.broadcasted_iota(jnp.int32, (CELLS, 128), 1) & 63
    sent = None
    for p in range(PLANES):
        face = 0.0
        if p == 0:
            face = jnp.where(has_left, 0.0, 1.0)
        if p == PLANES - 1:
            face = jnp.where(has_right, 0.0, 1.0)
        weight = jnp.where(
            lane < AT_X, 1.0, jnp.where(lane < AT_XX, xs[p], jnp.where(lane < AT_FACE, xs[p] * xs[p], face))
        )
        term = weight * acc[CELLS * p : CELLS * p + CELLS]
        sent = term if p == 0 else sent + term
    low = lax.broadcasted_iota(jnp.int32, (8, 128), 1) < 64
    mrecv[0] = jnp.where(low, sent[0:8], sent[8:16])
    for d in FAR_FIRST:
        gather_copy(mrecv.at[0], mrecv, m_ssem, m_rsem, d).start()

    def add_walls(t, acc):
        off = pl.multiple_of(t * 128, 128)
        walls = wall_planes(off, range(PLANES))
        for p in range(PLANES):
            fa[p + 2, :, pl.ds(off + MARGIN, 128)] = pb[p, :, pl.ds(off, 128)] + walls[p]
        return acc

    lax.fori_loop(0, FLAT // 128, add_walls, 0, unroll=3)

    halo_planes = (-2, -1, PLANES, PLANES + 1)

    def halo_walls(t, acc):
        off = pl.multiple_of(t * 128, 128)
        walls = wall_planes(off, halo_planes)
        for i in range(4):
            wb[i, :, pl.ds(off, 128)] = walls[i]
        return acc

    pass_on()
    lax.fori_loop(0, FLAT // 128, halo_walls, 0, unroll=3)

    for d in range(1, VELS):
        gather_copy(mrecv.at[0], mrecv, m_ssem, m_rsem, d).wait_recv()
    packed = mrecv[0]
    for d in range(1, VELS):
        packed = packed + mrecv[d]

    def unpack(x):
        return jnp.concatenate([x, pltpu.roll(x, 64, 1)], axis=0)

    lane = lax.broadcasted_iota(jnp.int32, (CELLS, 128), 1)
    on_face = (lane >= AT_FACE) & (lane < 64)
    least = unpack(mrecv[vel])
    largest = unpack(mrecv[lax.rem(vel + 1, VELS)])
    sums = jnp.where(lane < AT_FACE, unpack(packed), jnp.where(on_face, least, 0.0))
    sums = sums + pltpu.roll(jnp.where(on_face, largest, 0.0), len(X_FACE), 1)

    def coefficients(allm):
        m = [allm[:, 128 * i : 128 * i + 128] for i in range(10)]
        inv = 1.0 / m[0]
        ux, uy, uz = m[1] * inv, m[2] * inv, m[3] * inv
        cxx, cyy, czz = m[4] * inv - ux * ux, m[5] * inv - uy * uy, m[6] * inv - uz * uz
        cxy, cxz, cyz = m[7] * inv - ux * uy, m[8] * inv - ux * uz, m[9] * inv - uy * uz
        theta = (cxx + cyy + czz) / 3.0
        a = (RATE * STEP**3) * m[0] * jnp.exp(0.19 * jnp.log(theta))
        lx, ly, lz = 0.5 * (theta + cxx), 0.5 * (theta + cyy), 0.5 * (theta + czz)
        terms = (a, -a * ux, -a * uy, -a * uz, a * lx, a * ly, a * lz, 0.5 * a * cxy, 0.5 * a * cxz, 0.5 * a * cyz)
        return terms, dict(
            ux=ux, a=a, k0=1.0 - 32.0 * a * (lx + ly + lz), lx=16.0 * a * lx,
            ys=a * (16.0 * ly + 0.5), a2=2.0 * a, a2uy=2.0 * a * uy, a2uz=2.0 * a * uz, zq=16.0 * a * lz,
            gxy=4.0 * a * cxy, gxz=4.0 * a * cxz, gyz=4.0 * a * cyz,
        )

    terms, c1 = coefficients(times(sums, columns(mat, 6, 10)))
    factor = jnp.where(lane < 110, 1.0, 0.0)
    for t in range(10):
        factor = jnp.where((lane >= 10 * t) & (lane < 10 * t + 10), terms[t], factor)
    stencil = times(sums, columns(mat, 26, 2))
    _, c2 = coefficients(times(factor * (stencil[:, 0:128] + stencil[:, 128:256]), columns(mat, 16, 10)))

    width = 768

    def relax_plane(src, at, dst, dst_at, p, c):
        n = width // 128
        margin = MARGIN if dst.shape[-1] == WIDE else 0
        x = x_of(p)
        drift_n = c["a2"] * (x + STEP - c["ux"]) + c["lx"]
        drift_p = c["lx"] - c["a2"] * (x - STEP - c["ux"])
        kn, kp, k0 = rep(drift_n, n), rep(drift_p, n), rep(c["k0"], n)
        ys, a2, a2uy, a2uz, zq = (rep(c[q], n) for q in ("ys", "a2", "a2uy", "a2uz", "zq"))
        gxy, gxz, gyz = (rep(c[q], n) for q in ("gxy", "gxz", "gyz"))

        def step(t, acc):
            off = pl.multiple_of(t * width, 128)
            win = pl.ds(off, width + 2 * MARGIN)
            cen = pl.ds(off, width)
            cw, nw, pw = src[at, :, win], src[at + 1, :, win], src[at - 1, :, win]
            xw = nw - pw
            yy, zz = yt[:, cen], zt[:, cen]
            total_w = width + 2 * MARGIN

            def up(v):
                return pltpu.roll(v, total_w - NV, 1)[:, MARGIN : MARGIN + width]

            def down(v):
                return pltpu.roll(v, NV, 1)[:, MARGIN : MARGIN + width]

            cc, nn, pp = (v[:, MARGIN : MARGIN + width] for v in (cw, nw, pw))
            u, d = up(cw), down(cw)
            diff = u - d
            res = k0 * cc + kn * nn + kp * pp
            res = res + ys * (u + d) + (a2 * yy - a2uy) * diff + gxy * (up(xw) - down(xw))
            cross = gxz * (nn - pp) + gyz * diff
            zr = a2 * zz - a2uz
            plus = (zq + zr) * cc + cross
            minus = (zq - zr) * cc - cross
            edge = (NV - 1) / 2.0 * STEP
            res = res + jnp.where(zz < edge - 0.1, pltpu.roll(plus, width - 1, 1), 0.0)
            res = res + jnp.where(zz > 0.1 - edge, pltpu.roll(minus, 1, 1), 0.0)
            dst[dst_at, :, pl.ds(off + margin, width)] = res
            return acc

        lax.fori_loop(0, FLAT // width, step, 0, unroll=True)

    relax_plane(fa, 3, fb, 2, 1, c1)

    def relax_side(right):
        left = jnp.logical_not(right)
        recv_planes(True, left)
        recv_planes(False, right)
        arrived = jnp.where(right, PLANES + 2, 0)
        walls = jnp.where(right, 2, 0)
        halo_at = jnp.where(right, PLANES + 2, 1)
        edge_at = jnp.where(right, PLANES + 1, 2)

        @pl.when((right & has_right) | (left & has_left))
        def _():
            for i in range(2):
                fa[arrived + i, :, MARGIN : MARGIN + FLAT] = fa[arrived + i, :, MARGIN : MARGIN + FLAT] + wb[walls + i]
            relax_plane(fa, halo_at, fb, halo_at - 1, halo_at - 2, c1)

        relax_plane(fa, edge_at, fb, edge_at - 1, edge_at - 2, c1)
        relax_plane(fb, edge_at - 1, out, edge_at - 2, edge_at - 2, c2)

    right_first = y_at == 0
    relax_side(right_first)
    relax_side(jnp.logical_not(right_first))
    relax_plane(fb, 2, out, 1, 1, c2)

    @pl.when(has_above)
    def _():
        for p in range(PLANES):
            halo(1, p, space + 1).wait_send()

    @pl.when(has_below)
    def _():
        for p in range(PLANES):
            halo(0, p, space - 1).wait_send()

    for d in range(1, VELS):
        gather_copy(fsend, frecv, f_ssem, f_rsem, d).wait_send()
        gather_copy(mrecv.at[0], mrecv, m_ssem, m_rsem, d).wait_send()
    end_planes()


def body(distribution, freestream, face_area, cell_volume, neighbours, wall_flags, send_cells):
    dma = pltpu.SemaphoreType.DMA
    hbm = pl.BlockSpec(memory_space=pltpu.HBM)
    new = pl.pallas_call(
        kernel,
        out_shape=pltpu.VMEM((PLANES, CELLS, FLAT), F32),
        in_specs=[hbm] * 9,
        out_specs=pl.BlockSpec(memory_space=pltpu.VMEM),
        scratch_shapes=[
            pltpu.VMEM((PLANES, FLAT), F32),
            pltpu.VMEM((3, FACES, CELLS), F32),
            pltpu.VMEM((1, CELLS), F32),
            pltpu.VMEM((FACES, CELLS), jnp.int32),
            pltpu.VMEM((FACES, CELLS), jnp.int32),
            pltpu.SMEM((2, HALO), jnp.int32),
            pltpu.VMEM((PLANES, CELLS, FLAT), F32),
            pltpu.VMEM((2, PLANES, HALO, FLAT), F32),
            pltpu.VMEM((2, PLANES, HALO, FLAT), F32),
            pltpu.VMEM((FLAT, 128), BF16),
            pltpu.VMEM((28 * 128, 128), BF16),
            pltpu.VMEM((PLANES, CELLS, FLAT), F32),
            pltpu.VMEM((PLANES + 4, CELLS, WIDE), F32),
            pltpu.VMEM((4, CELLS, FLAT), F32),
            pltpu.VMEM((PLANES + 2, CELLS, WIDE), F32),
            pltpu.VMEM((2, 2, CELLS, 4 * 128), F32),
            pltpu.VMEM((2 * FACES * PLANES * CELLS, FLAT), BF16),
            pltpu.VMEM((FACES * PLANES * CELLS, 128), F32),
            pltpu.VMEM((3 * PLANES * CELLS, FLAT), BF16),
            pltpu.VMEM((CELLS, FLAT), F32),
            pltpu.VMEM((CELLS, FLAT), F32),
            pltpu.VMEM((CELLS, FLAT), F32),
            pltpu.VMEM((32, 128), F32),
            pltpu.VMEM((32, CELLS, 128), F32),
            pltpu.VMEM((96, 64), BF16),
            pltpu.VMEM((1, 256), F32),
            pltpu.VMEM((VELS, 1, 256), F32),
            pltpu.VMEM((VELS, 8, 128), F32),
            dma((PLANES,)), dma((2, PLANES)), dma((2, PLANES)),
            dma((VELS,)), dma((VELS,)), dma((VELS,)), dma((VELS,)), dma((2, 2)), dma((2, 2)),
            dma((8,)), dma((2, LANES, 2)), dma((2, LANES, 2)), dma((2, 2)), dma((2, 2)),
        ],
        compiler_params=pltpu.CompilerParams(
            collective_id=0, has_side_effects=True, vmem_limit_bytes=56 * 1024 * 1024
        ),
    )(
        jnp.transpose(distribution, (1, 0, 2)), freestream, face_area, cell_volume.reshape(1, CELLS), neighbours,
        wall_flags, send_cells, jnp.asarray(sum_weights()), jnp.asarray(small_matrices()),
    )
    return jnp.transpose(new, (1, 0, 2))


def solution(mesh):
    in_specs = (
        P("space", "vel", None),
        P("vel", None),
        P(None, None, "space"),
        P("space"),
        P(None, "space"),
        P(None, "space"),
        P(None, "space"),
    )
    out_specs = P("space", "vel", None)
    return jax.shard_map(body, mesh=mesh, in_specs=in_specs, out_specs=out_specs, check_vma=False)
```

```python
import jax
import jax.numpy as jnp
import numpy as np
from jax import lax
from jax.experimental import pallas as pl
from jax.experimental.pallas import tpu as pltpu
from jax.sharding import PartitionSpec as P

NV = 48
FLAT = NV * NV
STEP = 0.25
DT = 0.02
RATE = 0.002
FACES = 6
HALO = 4
CELLS = 16
PLANES = 3
MARGIN = 128
WIDE = FLAT + 2 * MARGIN
VELS = 16
WALL_ROWS = FACES * PLANES * CELLS
LANES = 4
PARTS = ((8, 12), (12, 15), (15, 18), (0, 8))
MESH = pl.DeviceIdType.MESH
F32 = jnp.float32
BF16 = jnp.bfloat16


X_FACE = tuple(range(18))
SUMMED = (
    ((0, 0), (0, 1), (1, 0), (2, 0), (0, 2), (3, 0), (4, 0), (1, 1), (2, 1), (5, 0))
    + tuple((c, 0) for c in range(6, 22))
    + tuple((c, 1) for c in (6, 7, 9, 10, 12, 13, 15, 16, 18, 19, 20, 21))
    + tuple((c, 2) for c in (6, 9, 12, 15, 18, 19, 20, 21))
)
AT_FACE = len(SUMMED)
SENT = tuple(c for c, _ in SUMMED) + X_FACE
KINDS = tuple(power for _, power in SUMMED) + (3,) * len(X_FACE)


def plane_sums(j, k):
    y, z = (j - (NV - 1) / 2.0) * STEP, (k - (NV - 1) / 2.0) * STEP
    one = np.ones_like(y)
    lo_y, hi_y, lo_z, hi_z = ((at == end).astype(np.float64) for at in (j, k) for end in (0, NV - 1))
    sums = [one, y, z, y * y, z * z, y * z]
    for face in (lo_y, hi_y):
        sums += [face, face * z, face * z * z]
    for face in (lo_z, hi_z):
        sums += [face, face * y, face * y * y]
    sums += [lo_y * lo_z, lo_y * hi_z, hi_y * lo_z, hi_y * hi_z]
    return np.stack(sums)


def two_parts(x):
    hi = x.astype(jnp.bfloat16)
    return hi, (x - hi.astype(np.float64)).astype(jnp.bfloat16)


def sum_weights():
    at = np.arange(FLAT)
    weights = plane_sums(at // NV, at % NV)[list(SENT)].T
    return np.concatenate(two_parts(weights), axis=1)


def stencil_moments():
    line = np.array([0, 1, 2, 17, 23, 30, 45, 46, 47])
    at = np.stack(np.meshgrid(line, line, line, indexing="ij")).reshape(3, -1)

    def velocity(index):
        return (index - (NV - 1) / 2.0) * STEP

    planes = plane_sums(at[1], at[2])
    x = velocity(at[0])
    basis = [planes[c] * x**power for c, power in SUMMED]
    for end in (0, NV - 1):
        basis += [planes[c] * (at[0] == end) for c in X_FACE]

    def polynomials(index):
        v = velocity(index)
        inside = np.all((index >= 0) & (index < NV), axis=0)
        vx, vy, vz = v
        return np.stack([np.ones_like(vx), vx, vy, vz, vx * vx, vy * vy, vz * vz, vx * vy, vx * vz, vy * vz]) * inside

    def moved(*steps):
        index = at.copy()
        for axis, step in steps:
            index[axis] += step
        return polynomials(index)

    v = velocity(at)
    first = [(moved((i, -1)) - moved((i, 1))) / (2 * STEP) for i in range(3)]
    terms = [sum(v[i] * first[i] for i in range(3))] + first
    terms += [(moved((i, -1)) - 2 * moved() + moved((i, 1))) / STEP**2 for i in range(3)]
    for i, j in ((0, 1), (0, 2), (1, 2)):
        corner = {(p, q): moved((i, p), (j, q)) for p in (-1, 1) for q in (-1, 1)}
        terms.append((corner[-1, -1] - corner[-1, 1] - corner[1, -1] + corner[1, 1]) / (2 * STEP**2))
    wanted = np.concatenate(terms)
    found = np.linalg.lstsq(np.stack(basis).T, wanted.T, rcond=None)[0]
    found = np.round(found * 1024) / 1024
    assert np.abs(np.stack(basis).T @ found - wanted.T).max() < 1e-6
    out = np.zeros((128, 100))
    out[: len(basis)] = found
    return out


def small_matrices():
    row = np.arange(128)[:, None]
    col = np.arange(1280)[None, :] // 128
    ratios = row // 16 == col[:, :768]
    moments = row % 16 == col
    products = (row % 10 == col) & (row < 110)
    stencil = np.zeros((128, 128))
    stencil[:, :100] = stencil_moments()
    for m in range(10):
        stencil[m, 100 + m] = 1.0
    plain = [a.astype(jnp.bfloat16) for a in (ratios, moments, products)]
    whole = np.concatenate(plain + list(two_parts(stencil)), axis=1)
    kinds = np.zeros((16, 128))
    kinds[0:4] = np.arange(4)[:, None] == np.array(KINDS + KINDS)[None, :]
    return np.concatenate(np.split(whole, whole.shape[1] // 128, axis=1) + [kinds.astype(jnp.bfloat16)], axis=0)


def split2(x):
    hi = x.astype(BF16)
    return hi, (x - hi.astype(F32)).astype(BF16)


def split3(x):
    hi = x.astype(BF16)
    r = x - hi.astype(F32)
    mid = r.astype(BF16)
    return hi, mid, (r - mid.astype(F32)).astype(BF16)


def lane_sums(acc):
    ones = jnp.ones((16, 128), BF16)
    total = None
    for part in split3(acc):
        term = lax.dot_general(ones, part, (((1,), (1,)), ((), ())), preferred_element_type=F32)
        total = term if total is None else total + term
    return total[0:1]


def times(x, matrix):
    out = jnp.dot(jnp.concatenate(split3(x), axis=0), matrix, preferred_element_type=F32)
    return out[0:16] + out[16:32] + out[32:48]


def spread(row, matrix):
    lane = lax.broadcasted_iota(jnp.int32, (CELLS, 128), 1)
    cell = lax.broadcasted_iota(jnp.int32, (CELLS, 128), 0)
    own = jnp.where((lane & (CELLS - 1)) == cell, jnp.broadcast_to(row, (CELLS, 128)), 0.0)
    return times(own, matrix)


def columns(matrix, first, count):
    return jnp.concatenate([matrix[128 * i : 128 * i + 128, :] for i in range(first, first + count)], axis=1)


FAR_FIRST = sorted(range(1, VELS), key=lambda d: -min(d, VELS - d))


def rep(x, n):
    return jnp.concatenate([x] * n, axis=1)


def kernel(
    dist, free_h, area_h, vol_h, nb_h, wall_h, send_h, wts_h, mat_h, out,
    free, area, vol, nb, wall, send, distv, hs, hr, wts, mat, pb, fa, wb, fb, relay, qm, fq, pm,
    yt, zt, mt, prm, sb, lhs, fsend, frecv, asend, arecv, yrecv, zrecv,
    in_sem, h_ssem, h_rsem, f_ssem, f_rsem, m_ssem, m_rsem, p_ssem, p_rsem,
    s_sem, z_ssem, z_rsem, r_ssem, r_rsem, b_ssem, b_rsem,
):
    space = lax.axis_index("space")
    vel = lax.axis_index("vel")
    blocks = lax.axis_size("space")
    has_below, has_above = space > 0, space < blocks - 1
    has_left, has_right = vel > 0, vel < VELS - 1

    loads = [pltpu.make_async_copy(dist.at[p], distv.at[p], in_sem.at[p]) for p in range(PLANES)]
    small = [
        pltpu.make_async_copy(src, dst, s_sem.at[i])
        for i, (src, dst) in enumerate(
            ((area_h, area), (nb_h, nb), (wall_h, wall), (vol_h, vol), (send_h, send), (free_h, free))
        )
    ]
    late = [
        pltpu.make_async_copy(src, dst, s_sem.at[6 + i]) for i, (src, dst) in enumerate(((wts_h, wts), (mat_h, mat)))
    ]
    for copy in small + loads + late:
        copy.start()

    barrier = pltpu.get_barrier_semaphore()
    for d in FAR_FIRST:
        pl.semaphore_signal(barrier, 1, device_id=(space, lax.rem(vel + d, VELS)), device_id_type=MESH)

    @pl.when(has_below)
    def _():
        pl.semaphore_signal(barrier, 1, device_id=(space - 1, vel), device_id_type=MESH)

    @pl.when(has_above)
    def _():
        pl.semaphore_signal(barrier, 1, device_id=(space + 1, vel), device_id_type=MESH)

    flat = lax.broadcasted_iota(jnp.int32, (CELLS, FLAT), 1).astype(F32)
    row = jnp.floor((flat + 0.5) / NV)
    y = (row - (NV - 1) / 2.0) * STEP
    z = (flat - row * NV - (NV - 1) / 2.0) * STEP
    yt[...] = y
    zt[...] = z
    mt[...] = jnp.exp(-(y * y + z * z) / 2.0)
    for buf, count in ((fa, PLANES + 4), (fb, PLANES + 2)):
        for plane in range(count):
            buf[plane, :, 0:MARGIN] = jnp.zeros((CELLS, MARGIN), F32)
            buf[plane, :, MARGIN + FLAT :] = jnp.zeros((CELLS, MARGIN), F32)

    @pl.when(jnp.logical_not(has_left))
    def _():
        for plane in (fa.at[0], fa.at[1], fb.at[0]):
            plane[...] = jnp.zeros((CELLS, WIDE), F32)

    @pl.when(jnp.logical_not(has_right))
    def _():
        for plane in (fa.at[PLANES + 2], fa.at[PLANES + 3], fb.at[PLANES + 1]):
            plane[...] = jnp.zeros((CELLS, WIDE), F32)

    for copy in small:
        copy.wait()

    prm[...] = jnp.zeros((32, 128), F32)
    for i in range(3):
        prm[6 * i : 6 * i + 6, 0:CELLS] = area[i]
    prm[18:24, 0:CELLS] = nb[...].astype(F32)
    prm[24:30, 0:CELLS] = wall[...].astype(F32)
    prm[30:31, 0:CELLS] = DT / vol[...]
    cols = prm[...].T[0:CELLS]
    for r in range(31):
        sb[r] = jnp.broadcast_to(cols[:, r : r + 1], (CELLS, 128))
    lane = lax.broadcasted_iota(jnp.int32, (CELLS, 64), 1) & 31
    for s in range(FACES):
        inside = (lane.astype(F32) == sb[18 + s][:, 0:64]) & (sb[24 + s][:, 0:64] < 0.5)
        lhs[16 * s : 16 * s + 16, :] = jnp.where(inside, 1.0, 0.0).astype(BF16)

    for copy in loads:
        copy.wait()
    for p in range(PLANES):
        for side in range(2):
            for r in range(HALO):
                hs[side, p, r : r + 1, :] = distv[p, pl.ds(send[side, r], 1), :]

    def x_of(p):
        return ((vel * PLANES + p).astype(F32) - (NV - 1) / 2.0) * STEP

    xs = {p: x_of(p) for p in range(-2, PLANES + 2)}
    mx = {p: jnp.exp(jnp.full((CELLS, 128), -0.5, F32) * (x * x)) for p, x in xs.items()}

    def gather_copy(src, dst, ssem, rsem, d):
        return pltpu.make_async_remote_copy(
            src_ref=src, dst_ref=dst.at[d], send_sem=ssem.at[d], recv_sem=rsem.at[d],
            device_id=(space, lax.rem(vel + d, VELS)), device_id_type=MESH,
        )

    def total(src, dst, ssem, rsem):
        acc = src[...]
        for d in range(1, VELS):
            gather_copy(src, dst, ssem, rsem, d).wait_recv()
            acc = acc + dst[d]
        return acc

    def flux_plane(p, carry):
        sx = [sb[s] * xs[p] for s in range(FACES)]

        def step(t, carry):
            off = pl.multiple_of(t * 256, 128)
            outs, ins = list(carry[:FACES]), list(carry[FACES:])
            for j in range(2):
                o = pl.ds(off + 128 * j, 128)
                dd, yy, zz = distv[p, :, o], yt[:, o], zt[:, o]
                mm = mt[:, o] * mx[p]
                for s in range(FACES):
                    w = jnp.maximum(sx[s] + sb[6 + s] * yy + sb[12 + s] * zz, 0.0)
                    outs[s] = outs[s] + w * dd
                    ins[s] = ins[s] + w * mm
            return tuple(outs + ins)

        return lax.fori_loop(0, FLAT // 256, step, carry)

    carry = tuple(jnp.zeros((CELLS, 128), F32) for _ in range(2 * FACES))
    for p in range(PLANES):
        carry = flux_plane(p, carry)
    fsend[0:1, 0:96] = lane_sums(jnp.concatenate(carry[:FACES], axis=0))
    fsend[0:1, 128:224] = lane_sums(jnp.concatenate(carry[FACES:], axis=0))
    fsend[0:1, 96:128] = jnp.zeros((1, 32), F32)
    fsend[0:1, 224:256] = jnp.ones((1, 32), F32)
    peers = VELS - 1 + has_below.astype(jnp.int32) + has_above.astype(jnp.int32)
    pl.semaphore_wait(barrier, peers)

    def halo(side, p, target):
        return pltpu.make_async_remote_copy(
            src_ref=hs.at[side, p], dst_ref=hr.at[1 - side, p],
            send_sem=h_ssem.at[side, p], recv_sem=h_rsem.at[1 - side, p],
            device_id=(target, vel), device_id_type=MESH,
        )

    y_at, z_at = lax.rem(vel, LANES), vel // LANES
    first = jnp.where(y_at == LANES - 1, PLANES - 1, 0)
    order = (1, first, PLANES - 1 - first)
    for p in order:

        @pl.when(has_above)
        def _():
            halo(1, p, space + 1).start()

        @pl.when(has_below)
        def _():
            halo(0, p, space - 1).start()

    @pl.when(jnp.logical_not(has_below))
    def _():
        for p in range(PLANES):
            hr[0, p] = jnp.broadcast_to(free[p : p + 1, :], (HALO, FLAT))

    @pl.when(jnp.logical_not(has_above))
    def _():
        for p in range(PLANES):
            hr[1, p] = jnp.broadcast_to(free[p : p + 1, :], (HALO, FLAT))

    for d in FAR_FIRST:
        gather_copy(fsend, frecv, f_ssem, f_rsem, d).start()

    for copy in late:
        copy.wait()

    def unit_walls(t, acc):
        off = pl.multiple_of(t * 128, 128)
        o = pl.ds(off, 128)
        yy, zz, mm = yt[:, o], zt[:, o], mt[:, o]
        for s in range(FACES):
            along = sb[6 + s] * yy + sb[12 + s] * zz
            for p in range(PLANES):
                at = (s * PLANES + p) * CELLS
                hi, lo = split2(jnp.minimum(sb[s] * xs[p] + along, 0.0) * (mm * mx[p]))
                qm[at : at + CELLS, o] = hi
                qm[WALL_ROWS + at : WALL_ROWS + at + CELLS, o] = lo
        return acc

    lax.fori_loop(0, FLAT // 128, unit_walls, 0, unroll=3)
    unit = jnp.dot(qm[...], wts[...], preferred_element_type=F32)
    fq[...] = unit[0:WALL_ROWS] + unit[WALL_ROWS:]

    def sides(right):
        return (LANES - 1, 0, 1, z_at < LANES - 1) if right else (0, LANES - 1, -1, z_at > 0)

    def ends(right, n):
        return (1 + n, n) if right else (n, PLANES + 2 + n)

    def lanes_of(right, q):
        begin, last = PARTS[q if right else LANES - 1 - q]
        return begin, last - begin

    def near_copy(right, n):
        src, dst = ends(right, n)
        i = 1 if right else 0
        return pltpu.make_async_remote_copy(
            src_ref=pb.at[src], dst_ref=fa.at[dst, :, pl.ds(MARGIN, FLAT)],
            send_sem=p_ssem.at[i, n], recv_sem=p_rsem.at[i, n],
            device_id=(space, vel + 1 if right else vel - 1), device_id_type=MESH,
        )

    def part_copy(right, n, q):
        home, other, dz, _ = sides(right)
        src, dst = ends(right, n)
        begin, count = lanes_of(right, q)
        lanes, wide = pl.ds(128 * begin, 128 * count), pl.ds(MARGIN + 128 * begin, 128 * count)
        i = 1 if right else 0
        if q == home:
            dst_ref, recv, to = fa.at[dst, :, wide], z_rsem.at[i, q, n], (z_at + dz) * LANES + other
        else:
            dst_ref, recv, to = relay.at[i, n, :, pl.ds(0, 128 * count)], r_rsem.at[i, n], z_at * LANES + q
        return pltpu.make_async_remote_copy(
            src_ref=pb.at[src, :, lanes], dst_ref=dst_ref, send_sem=z_ssem.at[i, q, n], recv_sem=recv,
            device_id=(space, to), device_id_type=MESH,
        )

    def relay_copy(right, n, q):
        home, other, dz, _ = sides(right)
        src, dst = ends(right, n)
        begin, count = lanes_of(right, q)
        wide = pl.ds(MARGIN + 128 * begin, 128 * count)
        i = 1 if right else 0
        return pltpu.make_async_remote_copy(
            src_ref=relay.at[i, n, :, pl.ds(0, 128 * count)], dst_ref=fa.at[dst, :, wide],
            send_sem=r_ssem.at[i, n], recv_sem=z_rsem.at[i, q, n],
            device_id=(space, (z_at + dz) * LANES + other), device_id_type=MESH,
        )

    def send_plane(right, n):
        home, _, _, inner = sides(right)

        @pl.when(y_at != home)
        def _():
            near_copy(right, n).start()

        @pl.when((y_at == home) & inner)
        def _():
            for q in range(LANES):
                part_copy(right, n, q).start()

    def pass_on():
        for step in range(2):
            for right in (True, False):
                n = step if right else 1 - step
                home, _, _, inner = sides(right)
                for q in range(LANES):
                    if q != home:

                        @pl.when((y_at == q) & inner)
                        def _():
                            part_copy(right, n, q).wait_recv()
                            relay_copy(right, n, q).start()

    def recv_planes(right, when):
        home, other, _, _ = sides(right)
        from_z = z_at > 0 if right else z_at < LANES - 1

        @pl.when((y_at != other) & when)
        def _():
            for n in range(2):
                near_copy(right, n).wait_recv()

        @pl.when((y_at == other) & from_z & when)
        def _():
            for n in range(2):
                for q in range(LANES):
                    if q == home:
                        part_copy(right, n, q).wait_recv()
                    else:
                        relay_copy(right, n, q).wait_recv()

    def end_planes():
        for right in (True, False):
            home, _, _, inner = sides(right)

            @pl.when(y_at != home)
            def _():
                for n in range(2):
                    near_copy(right, n).wait_send()

            @pl.when((y_at == home) & inner)
            def _():
                for n in range(2):
                    for q in range(LANES):
                        part_copy(right, n, q).wait_send()

            for q in range(LANES):
                if q != home:

                    @pl.when((y_at == q) & inner)
                    def _():
                        for n in range(2):
                            relay_copy(right, n, q).wait_send()

    def flow_plane(p):
        x = x_of(p)
        sx = [sb[s] * x for s in range(FACES)]
        scale = sb[30]

        def step(t, acc):
            off = pl.multiple_of(t * 256, 128)
            o = pl.ds(off, 256)
            ext = jnp.concatenate([distv[p, :, o], hr[0, p, :, o], hr[1, p, :, o], jnp.zeros((8, 256), F32)], axis=0)
            picked = jnp.dot(lhs[...], jnp.concatenate(split2(ext), axis=0), preferred_element_type=F32)
            for j in range(2):
                o = pl.ds(off + 128 * j, 128)
                dd, yy, zz = distv[p, :, o], yt[:, o], zt[:, o]
                out_sum, in_sum = None, None
                for s in range(FACES):
                    w = sx[s] + sb[6 + s] * yy + sb[12 + s] * zz
                    up = jnp.maximum(w, 0.0)
                    term = (w - up) * picked[16 * s : 16 * s + 16, 128 * j : 128 * j + 128]
                    out_sum = up if s == 0 else out_sum + up
                    in_sum = term if s == 0 else in_sum + term
                f = dd - scale * (out_sum * dd + in_sum)
                pb[p, :, o] = f
                for i, part in enumerate(split3(f)):
                    pm[pl.ds(pl.multiple_of((i * PLANES + p) * CELLS, CELLS), CELLS), o] = part
            return acc

        lax.fori_loop(0, FLAT // 256, step, 0, unroll=True)

    for step, p in enumerate(order):

        @pl.when(has_below)
        def _():
            halo(1, p, space + 1).wait_recv()

        @pl.when(has_above)
        def _():
            halo(0, p, space - 1).wait_recv()

        flow_plane(p)
        if step == 0:
            send_plane(True, 0)
            send_plane(False, 1)
        else:

            @pl.when(p == PLANES - 1)
            def _():
                send_plane(True, 1)

            @pl.when(p == 0)
            def _():
                send_plane(False, 0)

    rows = PLANES * CELLS
    flow = jnp.dot(pm[...], wts[...], preferred_element_type=F32)
    flow = flow[0:rows] + flow[rows : 2 * rows] + flow[2 * rows :]

    flux = total(fsend, frecv, f_ssem, f_rsem)
    ratio = spread(flux[:, 0:128] / jnp.where(flux[:, 128:256] > 0.0, flux[:, 128:256], 1.0), columns(mat, 0, 6))
    for s in range(FACES):
        sb[18 + s] = jnp.where(sb[24 + s] > 0.5, -sb[30] * ratio[:, 128 * s : 128 * s + 128], 0.0)

    def wall_planes(off, planes):
        o = pl.ds(off, 128)
        yy, zz, mm = yt[:, o], zt[:, o], mt[:, o]
        sums = [None] * len(planes)
        for s in range(FACES):
            along = sb[6 + s] * yy + sb[12 + s] * zz
            for i, p in enumerate(planes):
                term = jnp.minimum(sb[s] * xs[p] + along, 0.0) * sb[18 + s]
                sums[i] = term if s == 0 else sums[i] + term
        return [sums[i] * (mm * mx[p]) for i, p in enumerate(planes)]

    acc = []
    for p in range(PLANES):
        plane = flow[CELLS * p : CELLS * p + CELLS]
        for s in range(FACES):
            at = (s * PLANES + p) * CELLS
            plane = plane + sb[18 + s] * fq[at : at + CELLS, :]
        acc.append(plane)
    acc = jnp.concatenate(acc, axis=0)
    acc = acc + pltpu.roll(acc, 64, 1)
    kinds = mat[28 * 128 : 28 * 128 + 16, :].astype(F32)
    sent = None
    for p in range(PLANES):
        weight = kinds[0:1] + kinds[1:2] * xs[p] + kinds[2:3] * (xs[p] * xs[p])
        if p == 0:
            weight = weight + kinds[3:4] * jnp.where(has_left, 0.0, 1.0)
        if p == PLANES - 1:
            weight = weight + kinds[3:4] * jnp.where(has_right, 0.0, 1.0)
        term = weight * acc[CELLS * p : CELLS * p + CELLS]
        sent = term if p == 0 else sent + term

    lane8 = lax.broadcasted_iota(jnp.int32, (8, 128), 1)
    for half in range(2):
        own = jnp.where(lane8 < 16, sent[8 * half : 8 * half + 8], 0.0)
        asend[half : half + 1, :] = jnp.sum(pltpu.roll(own, 0, 1, stride=16, stride_axis=0), axis=0, keepdims=True)
    for d in FAR_FIRST:
        gather_copy(asend, arecv, m_ssem, m_rsem, d).start()

    def along_copy(buf, k, d, to):
        return pltpu.make_async_remote_copy(
            src_ref=buf.at[0], dst_ref=buf.at[d], send_sem=b_ssem.at[k, d], recv_sem=b_rsem.at[k, d],
            device_id=(space, to), device_id_type=MESH,
        )

    def y_copy(d):
        return along_copy(yrecv, 0, d, z_at * LANES + lax.rem(y_at + d, LANES))

    def z_copy(d):
        return along_copy(zrecv, 1, d, lax.rem(z_at + d, LANES) * LANES + y_at)

    yrecv[0] = jnp.where(lane8 < 64, sent[0:8], sent[8:16])
    for d in (2, 1, 3):
        y_copy(d).start()

    def add_walls(t, acc):
        off = pl.multiple_of(t * 128, 128)
        walls = wall_planes(off, range(PLANES))
        for p in range(PLANES):
            fa[p + 2, :, pl.ds(off + MARGIN, 128)] = pb[p, :, pl.ds(off, 128)] + walls[p]
        return acc

    lax.fori_loop(0, FLAT // 128, add_walls, 0, unroll=3)

    halo_planes = (-2, -1, PLANES, PLANES + 1)

    def halo_walls(t, acc):
        off = pl.multiple_of(t * 128, 128)
        walls = wall_planes(off, halo_planes)
        for i in range(4):
            wb[i, :, pl.ds(off, 128)] = walls[i]
        return acc

    pass_on()
    for d in range(1, LANES):
        y_copy(d).wait_recv()
    zrecv[0] = (yrecv[0] + yrecv[1]) + (yrecv[2] + yrecv[3])
    for d in (2, 1, 3):
        z_copy(d).start()
    lax.fori_loop(0, FLAT // 128, halo_walls, 0, unroll=3)

    def coefficients(allm):
        m = [allm[:, 128 * i : 128 * i + 128] for i in range(10)]
        inv = 1.0 / m[0]
        ux, uy, uz = m[1] * inv, m[2] * inv, m[3] * inv
        cxx, cyy, czz = m[4] * inv - ux * ux, m[5] * inv - uy * uy, m[6] * inv - uz * uz
        cxy, cxz, cyz = m[7] * inv - ux * uy, m[8] * inv - ux * uz, m[9] * inv - uy * uz
        theta = (cxx + cyy + czz) / 3.0
        a = (RATE * STEP**3) * m[0] * jnp.exp(0.19 * jnp.log(theta))
        lx, ly, lz = 0.5 * (theta + cxx), 0.5 * (theta + cyy), 0.5 * (theta + czz)
        terms = (a, -a * ux, -a * uy, -a * uz, a * lx, a * ly, a * lz, 0.5 * a * cxy, 0.5 * a * cxz, 0.5 * a * cyz)
        return terms, dict(
            ux=ux, a=a, k0=1.0 - 32.0 * a * (lx + ly + lz), lx=16.0 * a * lx,
            ys=a * (16.0 * ly + 0.5), a2=2.0 * a, a2uy=2.0 * a * uy, a2uz=2.0 * a * uz, zq=16.0 * a * lz,
            gxy=4.0 * a * cxy, gxz=4.0 * a * cxz, gyz=4.0 * a * cyz,
        )

    lane = lax.broadcasted_iota(jnp.int32, (CELLS, 128), 1)
    cell = lax.broadcasted_iota(jnp.int32, (CELLS, 128), 0)
    moments = total(asend, arecv, m_ssem, m_rsem)
    moments = jnp.concatenate([jnp.broadcast_to(moments[half : half + 1], (8, 128)) for half in range(2)], axis=0)
    moments = jnp.where((lane >> 4) == (cell & 7), moments, 0.0)
    terms, c1 = coefficients(times(moments, columns(mat, 6, 10)))

    def second_coefficients():
        for d in range(1, LANES):
            z_copy(d).wait_recv()
        packed = (zrecv[0] + zrecv[1]) + (zrecv[2] + zrecv[3])

        def unpack(x):
            return jnp.concatenate([x, pltpu.roll(x, 64, 1)], axis=0)

        on_face = (lane >= AT_FACE) & (lane < 64)
        least = unpack(zrecv[z_at])
        largest = unpack(zrecv[lax.rem(z_at + 1, LANES)])
        sums = jnp.where(lane < AT_FACE, unpack(packed), jnp.where(on_face, least, 0.0))
        sums = sums + pltpu.roll(jnp.where(on_face, largest, 0.0), len(X_FACE), 1)
        factor = jnp.where(lane < 110, 1.0, 0.0)
        for t in range(10):
            factor = jnp.where((lane >= 10 * t) & (lane < 10 * t + 10), terms[t], factor)
        stencil = times(sums, columns(mat, 26, 2))
        return coefficients(times(factor * (stencil[:, 0:128] + stencil[:, 128:256]), columns(mat, 16, 10)))[1]

    width = 768

    def relax_plane(src, at, dst, dst_at, p, c):
        n = width // 128
        margin = MARGIN if dst.shape[-1] == WIDE else 0
        x = x_of(p)
        drift_n = c["a2"] * (x + STEP - c["ux"]) + c["lx"]
        drift_p = c["lx"] - c["a2"] * (x - STEP - c["ux"])
        kn, kp, k0 = rep(drift_n, n), rep(drift_p, n), rep(c["k0"], n)
        ys, a2, a2uy, a2uz, zq = (rep(c[q], n) for q in ("ys", "a2", "a2uy", "a2uz", "zq"))
        gxy, gxz, gyz = (rep(c[q], n) for q in ("gxy", "gxz", "gyz"))

        def step(t, acc):
            off = pl.multiple_of(t * width, 128)
            win = pl.ds(off, width + 2 * MARGIN)
            cen = pl.ds(off, width)
            cw, nw, pw = src[at, :, win], src[at + 1, :, win], src[at - 1, :, win]
            xw = nw - pw
            yy, zz = yt[:, cen], zt[:, cen]
            total_w = width + 2 * MARGIN

            def up(v):
                return pltpu.roll(v, total_w - NV, 1)[:, MARGIN : MARGIN + width]

            def down(v):
                return pltpu.roll(v, NV, 1)[:, MARGIN : MARGIN + width]

            cc, nn, pp = (v[:, MARGIN : MARGIN + width] for v in (cw, nw, pw))
            u, d = up(cw), down(cw)
            diff = u - d
            res = k0 * cc + kn * nn + kp * pp
            res = res + ys * (u + d) + (a2 * yy - a2uy) * diff + gxy * (up(xw) - down(xw))
            cross = gxz * (nn - pp) + gyz * diff
            zr = a2 * zz - a2uz
            plus = (zq + zr) * cc + cross
            minus = (zq - zr) * cc - cross
            edge = (NV - 1) / 2.0 * STEP
            res = res + jnp.where(zz < edge - 0.1, pltpu.roll(plus, width - 1, 1), 0.0)
            res = res + jnp.where(zz > 0.1 - edge, pltpu.roll(minus, 1, 1), 0.0)
            dst[dst_at, :, pl.ds(off + margin, width)] = res
            return acc

        lax.fori_loop(0, FLAT // width, step, 0, unroll=True)

    relax_plane(fa, 3, fb, 2, 1, c1)

    def edge(right):
        return jnp.where(right, PLANES + 1, 2)

    def relax_side(right):
        left = jnp.logical_not(right)
        recv_planes(True, left)
        recv_planes(False, right)
        arrived = jnp.where(right, PLANES + 2, 0)
        walls = jnp.where(right, 2, 0)
        halo_at = jnp.where(right, PLANES + 2, 1)

        @pl.when((right & has_right) | (left & has_left))
        def _():
            for i in range(2):
                fa[arrived + i, :, MARGIN : MARGIN + FLAT] = fa[arrived + i, :, MARGIN : MARGIN + FLAT] + wb[walls + i]
            relax_plane(fa, halo_at, fb, halo_at - 1, halo_at - 2, c1)

        relax_plane(fa, edge(right), fb, edge(right) - 1, edge(right) - 2, c1)

    def relax_again(right):
        relax_plane(fb, edge(right) - 1, out, edge(right) - 2, edge(right) - 2, c2)

    right_first = y_at == 0
    right_last = jnp.logical_not(right_first)
    relax_side(right_first)
    c2 = second_coefficients()
    relax_again(right_first)
    relax_side(right_last)
    relax_again(right_last)
    relax_plane(fb, 2, out, 1, 1, c2)

    @pl.when(has_above)
    def _():
        for p in range(PLANES):
            halo(1, p, space + 1).wait_send()

    @pl.when(has_below)
    def _():
        for p in range(PLANES):
            halo(0, p, space - 1).wait_send()

    for d in range(1, VELS):
        gather_copy(fsend, frecv, f_ssem, f_rsem, d).wait_send()
        gather_copy(asend, arecv, m_ssem, m_rsem, d).wait_send()
    for d in range(1, LANES):
        y_copy(d).wait_send()
        z_copy(d).wait_send()
    end_planes()


def body(distribution, freestream, face_area, cell_volume, neighbours, wall_flags, send_cells):
    dma = pltpu.SemaphoreType.DMA
    hbm = pl.BlockSpec(memory_space=pltpu.HBM)
    new = pl.pallas_call(
        kernel,
        out_shape=pltpu.VMEM((PLANES, CELLS, FLAT), F32),
        in_specs=[hbm] * 9,
        out_specs=pl.BlockSpec(memory_space=pltpu.VMEM),
        scratch_shapes=[
            pltpu.VMEM((PLANES, FLAT), F32),
            pltpu.VMEM((3, FACES, CELLS), F32),
            pltpu.VMEM((1, CELLS), F32),
            pltpu.VMEM((FACES, CELLS), jnp.int32),
            pltpu.VMEM((FACES, CELLS), jnp.int32),
            pltpu.SMEM((2, HALO), jnp.int32),
            pltpu.VMEM((PLANES, CELLS, FLAT), F32),
            pltpu.VMEM((2, PLANES, HALO, FLAT), F32),
            pltpu.VMEM((2, PLANES, HALO, FLAT), F32),
            pltpu.VMEM((FLAT, 128), BF16),
            pltpu.VMEM((28 * 128 + 16, 128), BF16),
            pltpu.VMEM((PLANES, CELLS, FLAT), F32),
            pltpu.VMEM((PLANES + 4, CELLS, WIDE), F32),
            pltpu.VMEM((4, CELLS, FLAT), F32),
            pltpu.VMEM((PLANES + 2, CELLS, WIDE), F32),
            pltpu.VMEM((2, 2, CELLS, 4 * 128), F32),
            pltpu.VMEM((2 * FACES * PLANES * CELLS, FLAT), BF16),
            pltpu.VMEM((FACES * PLANES * CELLS, 128), F32),
            pltpu.VMEM((3 * PLANES * CELLS, FLAT), BF16),
            pltpu.VMEM((CELLS, FLAT), F32),
            pltpu.VMEM((CELLS, FLAT), F32),
            pltpu.VMEM((CELLS, FLAT), F32),
            pltpu.VMEM((32, 128), F32),
            pltpu.VMEM((32, CELLS, 128), F32),
            pltpu.VMEM((96, 64), BF16),
            pltpu.VMEM((1, 256), F32),
            pltpu.VMEM((VELS, 1, 256), F32),
            pltpu.VMEM((2, 128), F32),
            pltpu.VMEM((VELS, 2, 128), F32),
            pltpu.VMEM((LANES, 8, 128), F32),
            pltpu.VMEM((LANES, 8, 128), F32),
            dma((PLANES,)), dma((2, PLANES)), dma((2, PLANES)),
            dma((VELS,)), dma((VELS,)), dma((VELS,)), dma((VELS,)), dma((2, 2)), dma((2, 2)),
            dma((8,)), dma((2, LANES, 2)), dma((2, LANES, 2)), dma((2, 2)), dma((2, 2)),
            dma((2, LANES)), dma((2, LANES)),
        ],
        compiler_params=pltpu.CompilerParams(
            collective_id=0, has_side_effects=True, vmem_limit_bytes=56 * 1024 * 1024
        ),
    )(
        jnp.transpose(distribution, (1, 0, 2)), freestream, face_area, cell_volume.reshape(1, CELLS), neighbours,
        wall_flags, send_cells, jnp.asarray(sum_weights()), jnp.asarray(small_matrices()),
    )
    return jnp.transpose(new, (1, 0, 2))


def solution(mesh):
    in_specs = (
        P("space", "vel", None),
        P("vel", None),
        P(None, None, "space"),
        P("space"),
        P(None, "space"),
        P(None, "space"),
        P(None, "space"),
    )
    out_specs = P("space", "vel", None)
    return jax.shard_map(body, mesh=mesh, in_specs=in_specs, out_specs=out_specs, check_vma=False)
```

```python
import jax
import jax.numpy as jnp
import numpy as np
from jax import lax
from jax.experimental import pallas as pl
from jax.experimental.pallas import tpu as pltpu
from jax.sharding import PartitionSpec as P

NV = 48
FLAT = NV * NV
STEP = 0.25
DT = 0.02
RATE = 0.002
FACES = 6
HALO = 4
CELLS = 16
PLANES = 3
MARGIN = 128
WIDE = FLAT + 2 * MARGIN
VELS = 16
WALL_ROWS = FACES * PLANES * CELLS
LANES = 4
PARTS = ((8, 12), (12, 15), (15, 18), (0, 8))
MESH = pl.DeviceIdType.MESH
F32 = jnp.float32
BF16 = jnp.bfloat16


X_FACE = tuple(range(18))
SUMMED = (
    ((0, 0), (0, 1), (1, 0), (2, 0), (0, 2), (3, 0), (4, 0), (1, 1), (2, 1), (5, 0))
    + tuple((c, 0) for c in range(6, 22))
    + tuple((c, 1) for c in (6, 7, 9, 10, 12, 13, 15, 16, 18, 19, 20, 21))
    + tuple((c, 2) for c in (6, 9, 12, 15, 18, 19, 20, 21))
)
AT_FACE = len(SUMMED)
SENT = tuple(c for c, _ in SUMMED) + X_FACE
KINDS = tuple(power for _, power in SUMMED) + (3,) * len(X_FACE)


def plane_sums(j, k):
    y, z = (j - (NV - 1) / 2.0) * STEP, (k - (NV - 1) / 2.0) * STEP
    one = np.ones_like(y)
    lo_y, hi_y, lo_z, hi_z = ((at == end).astype(np.float64) for at in (j, k) for end in (0, NV - 1))
    sums = [one, y, z, y * y, z * z, y * z]
    for face in (lo_y, hi_y):
        sums += [face, face * z, face * z * z]
    for face in (lo_z, hi_z):
        sums += [face, face * y, face * y * y]
    sums += [lo_y * lo_z, lo_y * hi_z, hi_y * lo_z, hi_y * hi_z]
    return np.stack(sums)


def two_parts(x):
    hi = x.astype(jnp.bfloat16)
    return hi, (x - hi.astype(np.float64)).astype(jnp.bfloat16)


def sum_weights():
    at = np.arange(FLAT)
    weights = plane_sums(at // NV, at % NV)[list(SENT)].T
    return np.concatenate(two_parts(weights), axis=1)


def stencil_moments():
    line = np.array([0, 1, 2, 17, 23, 30, 45, 46, 47])
    at = np.stack(np.meshgrid(line, line, line, indexing="ij")).reshape(3, -1)

    def velocity(index):
        return (index - (NV - 1) / 2.0) * STEP

    planes = plane_sums(at[1], at[2])
    x = velocity(at[0])
    basis = [planes[c] * x**power for c, power in SUMMED]
    for end in (0, NV - 1):
        basis += [planes[c] * (at[0] == end) for c in X_FACE]

    def polynomials(index):
        v = velocity(index)
        inside = np.all((index >= 0) & (index < NV), axis=0)
        vx, vy, vz = v
        return np.stack([np.ones_like(vx), vx, vy, vz, vx * vx, vy * vy, vz * vz, vx * vy, vx * vz, vy * vz]) * inside

    def moved(*steps):
        index = at.copy()
        for axis, step in steps:
            index[axis] += step
        return polynomials(index)

    v = velocity(at)
    first = [(moved((i, -1)) - moved((i, 1))) / (2 * STEP) for i in range(3)]
    terms = [sum(v[i] * first[i] for i in range(3))] + first
    terms += [(moved((i, -1)) - 2 * moved() + moved((i, 1))) / STEP**2 for i in range(3)]
    for i, j in ((0, 1), (0, 2), (1, 2)):
        corner = {(p, q): moved((i, p), (j, q)) for p in (-1, 1) for q in (-1, 1)}
        terms.append((corner[-1, -1] - corner[-1, 1] - corner[1, -1] + corner[1, 1]) / (2 * STEP**2))
    wanted = np.concatenate(terms)
    found = np.linalg.lstsq(np.stack(basis).T, wanted.T, rcond=None)[0]
    found = np.round(found * 1024) / 1024
    assert np.abs(np.stack(basis).T @ found - wanted.T).max() < 1e-6
    out = np.zeros((128, 100))
    out[: len(basis)] = found
    return out


def small_matrices():
    row = np.arange(128)[:, None]
    col = np.arange(1280)[None, :] // 128
    ratios = row // 16 == col[:, :768]
    moments = row % 16 == col
    products = (row % 10 == col) & (row < 110)
    stencil = np.zeros((128, 128))
    stencil[:, :100] = stencil_moments()
    for m in range(10):
        stencil[m, 100 + m] = 1.0
    plain = [a.astype(jnp.bfloat16) for a in (ratios, moments, products)]
    whole = np.concatenate(plain + list(two_parts(stencil)), axis=1)
    kinds = np.zeros((16, 128))
    kinds[0:4] = np.arange(4)[:, None] == np.array(KINDS + KINDS)[None, :]
    return np.concatenate(np.split(whole, whole.shape[1] // 128, axis=1) + [kinds.astype(jnp.bfloat16)], axis=0)


def split2(x):
    hi = x.astype(BF16)
    return hi, (x - hi.astype(F32)).astype(BF16)


def split3(x):
    hi = x.astype(BF16)
    r = x - hi.astype(F32)
    mid = r.astype(BF16)
    return hi, mid, (r - mid.astype(F32)).astype(BF16)


def lane_sums(acc):
    ones = jnp.ones((16, 128), BF16)
    total = None
    for part in split3(acc):
        term = lax.dot_general(ones, part, (((1,), (1,)), ((), ())), preferred_element_type=F32)
        total = term if total is None else total + term
    return total[0:1]


def times(x, matrix):
    out = jnp.dot(jnp.concatenate(split3(x), axis=0), matrix, preferred_element_type=F32)
    return out[0:16] + out[16:32] + out[32:48]


def spread(row, matrix):
    lane = lax.broadcasted_iota(jnp.int32, (CELLS, 128), 1)
    cell = lax.broadcasted_iota(jnp.int32, (CELLS, 128), 0)
    own = jnp.where((lane & (CELLS - 1)) == cell, jnp.broadcast_to(row, (CELLS, 128)), 0.0)
    return times(own, matrix)


def columns(matrix, first, count):
    return jnp.concatenate([matrix[128 * i : 128 * i + 128, :] for i in range(first, first + count)], axis=1)


FAR_FIRST = sorted(range(1, VELS), key=lambda d: -min(d, VELS - d))


def rep(x, n):
    return jnp.concatenate([x] * n, axis=1)


def kernel(
    dist, free_h, area_h, vol_h, nb_h, wall_h, send_h, wts_h, mat_h, out,
    free, area, vol, nb, wall, send, distv, hs, hr, wts, mat, pb, fa, wb, fb, relay, qm, fq, pm,
    yt, zt, mt, kt, lf, prm, sb, lhs, fsend, frecv, asend, arecv, yrecv, zrecv,
    in_sem, h_ssem, h_rsem, f_ssem, f_rsem, m_ssem, m_rsem, p_ssem, p_rsem,
    s_sem, z_ssem, z_rsem, r_ssem, r_rsem, b_ssem, b_rsem,
):
    space = lax.axis_index("space")
    vel = lax.axis_index("vel")
    blocks = lax.axis_size("space")
    has_below, has_above = space > 0, space < blocks - 1
    has_left, has_right = vel > 0, vel < VELS - 1

    loads = [pltpu.make_async_copy(dist.at[p], distv.at[p], in_sem.at[p]) for p in range(PLANES)]
    small = [
        pltpu.make_async_copy(src, dst, s_sem.at[i])
        for i, (src, dst) in enumerate(
            ((area_h, area), (nb_h, nb), (wall_h, wall), (vol_h, vol), (send_h, send), (free_h, free))
        )
    ]
    late = [
        pltpu.make_async_copy(src, dst, s_sem.at[6 + i]) for i, (src, dst) in enumerate(((wts_h, wts), (mat_h, mat)))
    ]
    for copy in small + loads + late:
        copy.start()

    barrier = pltpu.get_barrier_semaphore()
    for d in FAR_FIRST:
        pl.semaphore_signal(barrier, 1, device_id=(space, lax.rem(vel + d, VELS)), device_id_type=MESH)

    @pl.when(has_below)
    def _():
        pl.semaphore_signal(barrier, 1, device_id=(space - 1, vel), device_id_type=MESH)

    @pl.when(has_above)
    def _():
        pl.semaphore_signal(barrier, 1, device_id=(space + 1, vel), device_id_type=MESH)

    flat = lax.broadcasted_iota(jnp.int32, (CELLS, FLAT), 1).astype(F32)
    row = jnp.floor((flat + 0.5) / NV)
    y = (row - (NV - 1) / 2.0) * STEP
    z = (flat - row * NV - (NV - 1) / 2.0) * STEP
    yt[...] = y
    zt[...] = z
    last_z = (NV - 1) / 2.0 * STEP - 0.1
    kt[0] = jnp.where(z < last_z, 1.0, 0.0)
    kt[1] = jnp.where(z > -last_z, 1.0, 0.0)
    mt[...] = jnp.exp(-(y * y + z * z) / 2.0)
    for buf, count in ((fa, PLANES + 4), (fb, PLANES + 2)):
        for plane in range(count):
            buf[plane, :, 0:MARGIN] = jnp.zeros((CELLS, MARGIN), F32)
            buf[plane, :, MARGIN + FLAT :] = jnp.zeros((CELLS, MARGIN), F32)

    @pl.when(jnp.logical_not(has_left))
    def _():
        for plane in (fa.at[0], fa.at[1], fb.at[0]):
            plane[...] = jnp.zeros((CELLS, WIDE), F32)

    @pl.when(jnp.logical_not(has_right))
    def _():
        for plane in (fa.at[PLANES + 2], fa.at[PLANES + 3], fb.at[PLANES + 1]):
            plane[...] = jnp.zeros((CELLS, WIDE), F32)

    for copy in small:
        copy.wait()

    prm[...] = jnp.zeros((32, 128), F32)
    for i in range(3):
        prm[6 * i : 6 * i + 6, 0:CELLS] = area[i]
    prm[18:24, 0:CELLS] = nb[...].astype(F32)
    prm[24:30, 0:CELLS] = wall[...].astype(F32)
    prm[30:31, 0:CELLS] = DT / vol[...]
    cols = prm[...].T[0:CELLS]
    for r in range(31):
        sb[r] = jnp.broadcast_to(cols[:, r : r + 1], (CELLS, 128))
    lane = lax.broadcasted_iota(jnp.int32, (CELLS, 64), 1) & 31
    for s in range(FACES):
        inside = (lane.astype(F32) == sb[18 + s][:, 0:64]) & (sb[24 + s][:, 0:64] < 0.5)
        lhs[16 * s : 16 * s + 16, :] = jnp.where(inside, 1.0, 0.0).astype(BF16)

    for copy in loads:
        copy.wait()
    for p in range(PLANES):
        for side in range(2):
            for r in range(HALO):
                hs[side, p, r : r + 1, :] = distv[p, pl.ds(send[side, r], 1), :]

    def x_of(p):
        return ((vel * PLANES + p).astype(F32) - (NV - 1) / 2.0) * STEP

    xs = {p: x_of(p) for p in range(-2, PLANES + 2)}
    mx = {p: jnp.exp(jnp.full((CELLS, 128), -0.5, F32) * (x * x)) for p, x in xs.items()}

    def gather_copy(src, dst, ssem, rsem, d):
        return pltpu.make_async_remote_copy(
            src_ref=src, dst_ref=dst.at[d], send_sem=ssem.at[d], recv_sem=rsem.at[d],
            device_id=(space, lax.rem(vel + d, VELS)), device_id_type=MESH,
        )

    def total(src, dst, ssem, rsem):
        acc = src[...]
        for d in range(1, VELS):
            gather_copy(src, dst, ssem, rsem, d).wait_recv()
            acc = acc + dst[d]
        return acc

    def flux_plane(p, carry):
        sx = [sb[s] * xs[p] for s in range(FACES)]

        def step(t, carry):
            off = pl.multiple_of(t * 256, 128)
            outs, ins = list(carry[:FACES]), list(carry[FACES:])
            for j in range(2):
                o = pl.ds(off + 128 * j, 128)
                dd, yy, zz = distv[p, :, o], yt[:, o], zt[:, o]
                mm = mt[:, o] * mx[p]
                for s in range(FACES):
                    w = jnp.maximum(sx[s] + sb[6 + s] * yy + sb[12 + s] * zz, 0.0)
                    outs[s] = outs[s] + w * dd
                    ins[s] = ins[s] + w * mm
            return tuple(outs + ins)

        return lax.fori_loop(0, FLAT // 256, step, carry)

    carry = tuple(jnp.zeros((CELLS, 128), F32) for _ in range(2 * FACES))
    for p in range(PLANES):
        carry = flux_plane(p, carry)
    fsend[0:1, 0:96] = lane_sums(jnp.concatenate(carry[:FACES], axis=0))
    fsend[0:1, 128:224] = lane_sums(jnp.concatenate(carry[FACES:], axis=0))
    fsend[0:1, 96:128] = jnp.zeros((1, 32), F32)
    fsend[0:1, 224:256] = jnp.ones((1, 32), F32)
    peers = VELS - 1 + has_below.astype(jnp.int32) + has_above.astype(jnp.int32)
    pl.semaphore_wait(barrier, peers)

    def halo(side, p, target):
        return pltpu.make_async_remote_copy(
            src_ref=hs.at[side, p], dst_ref=hr.at[1 - side, p],
            send_sem=h_ssem.at[side, p], recv_sem=h_rsem.at[1 - side, p],
            device_id=(target, vel), device_id_type=MESH,
        )

    y_at, z_at = lax.rem(vel, LANES), vel // LANES
    first = jnp.where(y_at == LANES - 1, PLANES - 1, 0)
    order = (1, first, PLANES - 1 - first)
    for p in order:

        @pl.when(has_above)
        def _():
            halo(1, p, space + 1).start()

        @pl.when(has_below)
        def _():
            halo(0, p, space - 1).start()

    @pl.when(jnp.logical_not(has_below))
    def _():
        for p in range(PLANES):
            hr[0, p] = jnp.broadcast_to(free[p : p + 1, :], (HALO, FLAT))

    @pl.when(jnp.logical_not(has_above))
    def _():
        for p in range(PLANES):
            hr[1, p] = jnp.broadcast_to(free[p : p + 1, :], (HALO, FLAT))

    for d in FAR_FIRST:
        gather_copy(fsend, frecv, f_ssem, f_rsem, d).start()

    for copy in late:
        copy.wait()

    def unit_walls(t, acc):
        off = pl.multiple_of(t * 128, 128)
        o = pl.ds(off, 128)
        yy, zz, mm = yt[:, o], zt[:, o], mt[:, o]
        for s in range(FACES):
            along = sb[6 + s] * yy + sb[12 + s] * zz
            for p in range(PLANES):
                at = (s * PLANES + p) * CELLS
                hi, lo = split2(jnp.minimum(sb[s] * xs[p] + along, 0.0) * (mm * mx[p]))
                qm[at : at + CELLS, o] = hi
                qm[WALL_ROWS + at : WALL_ROWS + at + CELLS, o] = lo
        return acc

    lax.fori_loop(0, FLAT // 128, unit_walls, 0, unroll=3)
    unit = jnp.dot(qm[...], wts[...], preferred_element_type=F32)
    fq[...] = unit[0:WALL_ROWS] + unit[WALL_ROWS:]

    def sides(right):
        return (LANES - 1, 0, 1, z_at < LANES - 1) if right else (0, LANES - 1, -1, z_at > 0)

    def ends(right, n):
        return (1 + n, n) if right else (n, PLANES + 2 + n)

    def lanes_of(right, q):
        begin, last = PARTS[q if right else LANES - 1 - q]
        return begin, last - begin

    def near_copy(right, n):
        src, dst = ends(right, n)
        i = 1 if right else 0
        return pltpu.make_async_remote_copy(
            src_ref=pb.at[src], dst_ref=fa.at[dst, :, pl.ds(MARGIN, FLAT)],
            send_sem=p_ssem.at[i, n], recv_sem=p_rsem.at[i, n],
            device_id=(space, vel + 1 if right else vel - 1), device_id_type=MESH,
        )

    def part_copy(right, n, q):
        home, other, dz, _ = sides(right)
        src, dst = ends(right, n)
        begin, count = lanes_of(right, q)
        lanes, wide = pl.ds(128 * begin, 128 * count), pl.ds(MARGIN + 128 * begin, 128 * count)
        i = 1 if right else 0
        if q == home:
            dst_ref, recv, to = fa.at[dst, :, wide], z_rsem.at[i, q, n], (z_at + dz) * LANES + other
        else:
            dst_ref, recv, to = relay.at[i, n, :, pl.ds(0, 128 * count)], r_rsem.at[i, n], z_at * LANES + q
        return pltpu.make_async_remote_copy(
            src_ref=pb.at[src, :, lanes], dst_ref=dst_ref, send_sem=z_ssem.at[i, q, n], recv_sem=recv,
            device_id=(space, to), device_id_type=MESH,
        )

    def relay_copy(right, n, q):
        home, other, dz, _ = sides(right)
        src, dst = ends(right, n)
        begin, count = lanes_of(right, q)
        wide = pl.ds(MARGIN + 128 * begin, 128 * count)
        i = 1 if right else 0
        return pltpu.make_async_remote_copy(
            src_ref=relay.at[i, n, :, pl.ds(0, 128 * count)], dst_ref=fa.at[dst, :, wide],
            send_sem=r_ssem.at[i, n], recv_sem=z_rsem.at[i, q, n],
            device_id=(space, (z_at + dz) * LANES + other), device_id_type=MESH,
        )

    def send_far(right, n):
        home, _, _, inner = sides(right)

        @pl.when((y_at == home) & inner)
        def _():
            for q in range(LANES):
                part_copy(right, n, q).start()

    def send_near():
        for right in (True, False):
            home, _, _, _ = sides(right)

            @pl.when(y_at != home)
            def _():
                for n in range(2):
                    near_copy(right, n).start()

    def pass_on():
        for step in range(2):
            for right in (True, False):
                n = step if right else 1 - step
                home, _, _, inner = sides(right)
                for q in range(LANES):
                    if q != home:

                        @pl.when((y_at == q) & inner)
                        def _():
                            part_copy(right, n, q).wait_recv()
                            relay_copy(right, n, q).start()

    def recv_planes(right, when):
        home, other, _, _ = sides(right)
        from_z = z_at > 0 if right else z_at < LANES - 1

        @pl.when((y_at != other) & when)
        def _():
            for n in range(2):
                near_copy(right, n).wait_recv()

        @pl.when((y_at == other) & from_z & when)
        def _():
            for n in range(2):
                for q in range(LANES):
                    if q == home:
                        part_copy(right, n, q).wait_recv()
                    else:
                        relay_copy(right, n, q).wait_recv()

    def end_planes():
        for right in (True, False):
            home, _, _, inner = sides(right)

            @pl.when(y_at != home)
            def _():
                for n in range(2):
                    near_copy(right, n).wait_send()

            @pl.when((y_at == home) & inner)
            def _():
                for n in range(2):
                    for q in range(LANES):
                        part_copy(right, n, q).wait_send()

            for q in range(LANES):
                if q != home:

                    @pl.when((y_at == q) & inner)
                    def _():
                        for n in range(2):
                            relay_copy(right, n, q).wait_send()

    def flow_plane(p):
        x = x_of(p)
        sx = [sb[s] * x for s in range(FACES)]
        scale = sb[30]

        def step(t, acc):
            off = pl.multiple_of(t * 256, 128)
            o = pl.ds(off, 256)
            ext = jnp.concatenate([distv[p, :, o], hr[0, p, :, o], hr[1, p, :, o], jnp.zeros((8, 256), F32)], axis=0)
            picked = jnp.dot(lhs[...], jnp.concatenate(split2(ext), axis=0), preferred_element_type=F32)
            for j in range(2):
                o = pl.ds(off + 128 * j, 128)
                dd, yy, zz = distv[p, :, o], yt[:, o], zt[:, o]
                out_sum, in_sum = None, None
                for s in range(FACES):
                    w = sx[s] + sb[6 + s] * yy + sb[12 + s] * zz
                    up = jnp.maximum(w, 0.0)
                    term = (w - up) * picked[16 * s : 16 * s + 16, 128 * j : 128 * j + 128]
                    out_sum = up if s == 0 else out_sum + up
                    in_sum = term if s == 0 else in_sum + term
                f = dd - scale * (out_sum * dd + in_sum)
                pb[p, :, o] = f
                for i, part in enumerate(split3(f)):
                    pm[pl.ds(pl.multiple_of((i * PLANES + p) * CELLS, CELLS), CELLS), o] = part
            return acc

        lax.fori_loop(0, FLAT // 256, step, 0, unroll=True)

    for step, p in enumerate(order):

        @pl.when(has_below)
        def _():
            halo(1, p, space + 1).wait_recv()

        @pl.when(has_above)
        def _():
            halo(0, p, space - 1).wait_recv()

        flow_plane(p)
        if step == 0:
            send_far(True, 0)
            send_far(False, 1)
        else:

            @pl.when(p == PLANES - 1)
            def _():
                send_far(True, 1)

            @pl.when(p == 0)
            def _():
                send_far(False, 0)

    rows = PLANES * CELLS
    flow = jnp.dot(pm[...], wts[...], preferred_element_type=F32)
    flow = flow[0:rows] + flow[rows : 2 * rows] + flow[2 * rows :]

    flux = total(fsend, frecv, f_ssem, f_rsem)
    ratio = spread(flux[:, 0:128] / jnp.where(flux[:, 128:256] > 0.0, flux[:, 128:256], 1.0), columns(mat, 0, 6))
    for s in range(FACES):
        sb[18 + s] = jnp.where(sb[24 + s] > 0.5, -sb[30] * ratio[:, 128 * s : 128 * s + 128], 0.0)

    def wall_planes(off, planes):
        o = pl.ds(off, 128)
        yy, zz, mm = yt[:, o], zt[:, o], mt[:, o]
        sums = [None] * len(planes)
        for s in range(FACES):
            along = sb[6 + s] * yy + sb[12 + s] * zz
            for i, p in enumerate(planes):
                term = jnp.minimum(sb[s] * xs[p] + along, 0.0) * sb[18 + s]
                sums[i] = term if s == 0 else sums[i] + term
        return [sums[i] * (mm * mx[p]) for i, p in enumerate(planes)]

    acc = []
    for p in range(PLANES):
        plane = flow[CELLS * p : CELLS * p + CELLS]
        for s in range(FACES):
            at = (s * PLANES + p) * CELLS
            plane = plane + sb[18 + s] * fq[at : at + CELLS, :]
        acc.append(plane)
    acc = jnp.concatenate(acc, axis=0)
    acc = acc + pltpu.roll(acc, 64, 1)
    kinds = mat[28 * 128 : 28 * 128 + 16, :].astype(F32)
    sent = None
    for p in range(PLANES):
        weight = kinds[0:1] + kinds[1:2] * xs[p] + kinds[2:3] * (xs[p] * xs[p])
        if p == 0:
            weight = weight + kinds[3:4] * jnp.where(has_left, 0.0, 1.0)
        if p == PLANES - 1:
            weight = weight + kinds[3:4] * jnp.where(has_right, 0.0, 1.0)
        term = weight * acc[CELLS * p : CELLS * p + CELLS]
        sent = term if p == 0 else sent + term

    lane8 = lax.broadcasted_iota(jnp.int32, (8, 128), 1)
    for half in range(2):
        own = jnp.where(lane8 < 16, sent[8 * half : 8 * half + 8], 0.0)
        asend[half : half + 1, :] = jnp.sum(pltpu.roll(own, 0, 1, stride=16, stride_axis=0), axis=0, keepdims=True)
    for d in FAR_FIRST:
        gather_copy(asend, arecv, m_ssem, m_rsem, d).start()

    def along_copy(buf, k, d, to):
        return pltpu.make_async_remote_copy(
            src_ref=buf.at[0], dst_ref=buf.at[d], send_sem=b_ssem.at[k, d], recv_sem=b_rsem.at[k, d],
            device_id=(space, to), device_id_type=MESH,
        )

    def y_copy(d):
        return along_copy(yrecv, 0, d, z_at * LANES + lax.rem(y_at + d, LANES))

    def z_copy(d):
        return along_copy(zrecv, 1, d, lax.rem(z_at + d, LANES) * LANES + y_at)

    yrecv[0] = jnp.where(lane8 < 64, sent[0:8], sent[8:16])
    for d in (2, 1, 3):
        y_copy(d).start()
    send_near()

    def add_walls(t, acc):
        off = pl.multiple_of(t * 128, 128)
        walls = wall_planes(off, range(PLANES))
        for p in range(PLANES):
            fa[p + 2, :, pl.ds(off + MARGIN, 128)] = pb[p, :, pl.ds(off, 128)] + walls[p]
        return acc

    lax.fori_loop(0, FLAT // 128, add_walls, 0, unroll=3)

    halo_planes = (-2, -1, PLANES, PLANES + 1)

    def halo_walls(t, acc):
        off = pl.multiple_of(t * 128, 128)
        walls = wall_planes(off, halo_planes)
        for i in range(4):
            wb[i, :, pl.ds(off, 128)] = walls[i]
        return acc

    pass_on()
    for d in range(1, LANES):
        y_copy(d).wait_recv()
    zrecv[0] = (yrecv[0] + yrecv[1]) + (yrecv[2] + yrecv[3])
    for d in (2, 1, 3):
        z_copy(d).start()
    lax.fori_loop(0, FLAT // 128, halo_walls, 0, unroll=3)

    def coefficients(allm):
        m = [allm[:, 128 * i : 128 * i + 128] for i in range(10)]
        inv = 1.0 / m[0]
        ux, uy, uz = m[1] * inv, m[2] * inv, m[3] * inv
        cxx, cyy, czz = m[4] * inv - ux * ux, m[5] * inv - uy * uy, m[6] * inv - uz * uz
        cxy, cxz, cyz = m[7] * inv - ux * uy, m[8] * inv - ux * uz, m[9] * inv - uy * uz
        theta = (cxx + cyy + czz) / 3.0
        a = (RATE * STEP**3) * m[0] * jnp.exp(0.19 * jnp.log(theta))
        lx, ly, lz = 0.5 * (theta + cxx), 0.5 * (theta + cyy), 0.5 * (theta + czz)
        terms = (a, -a * ux, -a * uy, -a * uz, a * lx, a * ly, a * lz, 0.5 * a * cxy, 0.5 * a * cxz, 0.5 * a * cyz)
        return terms, dict(
            ux=ux, a=a, k0=1.0 - 32.0 * a * (lx + ly + lz), lx=16.0 * a * lx,
            ys=a * (16.0 * ly + 0.5), a2=2.0 * a, a2uy=2.0 * a * uy, a2uz=2.0 * a * uz, zq=16.0 * a * lz,
            gxy=4.0 * a * cxy, gxz=4.0 * a * cxz, gyz=4.0 * a * cyz,
        )

    lane = lax.broadcasted_iota(jnp.int32, (CELLS, 128), 1)
    cell = lax.broadcasted_iota(jnp.int32, (CELLS, 128), 0)
    moments = total(asend, arecv, m_ssem, m_rsem)
    moments = jnp.concatenate([jnp.broadcast_to(moments[half : half + 1], (8, 128)) for half in range(2)], axis=0)
    moments = jnp.where((lane >> 4) == (cell & 7), moments, 0.0)
    terms, c1 = coefficients(times(moments, columns(mat, 6, 10)))

    def second_coefficients():
        for d in range(1, LANES):
            z_copy(d).wait_recv()
        packed = (zrecv[0] + zrecv[1]) + (zrecv[2] + zrecv[3])

        def unpack(x):
            return jnp.concatenate([x, pltpu.roll(x, 64, 1)], axis=0)

        on_face = (lane >= AT_FACE) & (lane < 64)
        least = unpack(zrecv[z_at])
        largest = unpack(zrecv[lax.rem(z_at + 1, LANES)])
        sums = jnp.where(lane < AT_FACE, unpack(packed), jnp.where(on_face, least, 0.0))
        sums = sums + pltpu.roll(jnp.where(on_face, largest, 0.0), len(X_FACE), 1)
        factor = jnp.where(lane < 110, 1.0, 0.0)
        for t in range(10):
            factor = jnp.where((lane >= 10 * t) & (lane < 10 * t + 10), terms[t], factor)
        stencil = times(sums, columns(mat, 26, 2))
        return coefficients(times(factor * (stencil[:, 0:128] + stencil[:, 128:256]), columns(mat, 16, 10)))[1]

    width = FLAT

    def lane_factors(k, c):
        a2, a2uy, a2uz, zq = (rep(c[q], FLAT // 128) for q in ("a2", "a2uy", "a2uz", "zq"))
        drift = a2 * zt[...] - a2uz
        lf[k, 0] = a2 * yt[...] - a2uy
        lf[k, 1] = zq + drift
        lf[k, 2] = zq - drift

    def relax_plane(src, at, dst, dst_at, p, c, k):
        n = width // 128
        margin = MARGIN if dst.shape[-1] == WIDE else 0
        x = x_of(p)
        drift_n = c["a2"] * (x + STEP - c["ux"]) + c["lx"]
        drift_p = c["lx"] - c["a2"] * (x - STEP - c["ux"])
        kn, kp, k0 = rep(drift_n, n), rep(drift_p, n), rep(c["k0"], n)
        ys, gxy, gxz, gyz = (rep(c[q], n) for q in ("ys", "gxy", "gxz", "gyz"))

        def step(t, acc):
            off = pl.multiple_of(t * width, 128)
            win = pl.ds(off, width + 2 * MARGIN)
            cen = pl.ds(off, width)
            cw, nw, pw = src[at, :, win], src[at + 1, :, win], src[at - 1, :, win]
            xw = nw - pw
            total_w = width + 2 * MARGIN

            def up(v):
                return pltpu.roll(v, total_w - NV, 1)[:, MARGIN : MARGIN + width]

            def down(v):
                return pltpu.roll(v, NV, 1)[:, MARGIN : MARGIN + width]

            cc, nn, pp = (v[:, MARGIN : MARGIN + width] for v in (cw, nw, pw))
            u, d = up(cw), down(cw)
            diff = u - d
            res = k0 * cc + kn * nn + kp * pp
            res = res + ys * (u + d) + lf[k, 0, :, cen] * diff + gxy * (up(xw) - down(xw))
            cross = gxz * (nn - pp) + gyz * diff
            plus = lf[k, 1, :, cen] * cc + cross
            minus = lf[k, 2, :, cen] * cc - cross
            res = res + kt[0, :, cen] * pltpu.roll(plus, width - 1, 1)
            res = res + kt[1, :, cen] * pltpu.roll(minus, 1, 1)
            dst[dst_at, :, pl.ds(off + margin, width)] = res
            return acc

        lax.fori_loop(0, FLAT // width, step, 0, unroll=True)

    lane_factors(0, c1)
    relax_plane(fa, 3, fb, 2, 1, c1, 0)

    def edge(right):
        return jnp.where(right, PLANES + 1, 2)

    def relax_side(right):
        left = jnp.logical_not(right)
        recv_planes(True, left)
        recv_planes(False, right)
        arrived = jnp.where(right, PLANES + 2, 0)
        walls = jnp.where(right, 2, 0)
        halo_at = jnp.where(right, PLANES + 2, 1)

        @pl.when((right & has_right) | (left & has_left))
        def _():
            for i in range(2):
                fa[arrived + i, :, MARGIN : MARGIN + FLAT] = fa[arrived + i, :, MARGIN : MARGIN + FLAT] + wb[walls + i]
            relax_plane(fa, halo_at, fb, halo_at - 1, halo_at - 2, c1, 0)

        relax_plane(fa, edge(right), fb, edge(right) - 1, edge(right) - 2, c1, 0)

    def relax_again(right):
        relax_plane(fb, edge(right) - 1, out, edge(right) - 2, edge(right) - 2, c2, 1)

    right_first = y_at == 0
    right_last = jnp.logical_not(right_first)
    relax_side(right_first)
    c2 = second_coefficients()
    lane_factors(1, c2)
    relax_again(right_first)
    relax_side(right_last)
    relax_again(right_last)
    relax_plane(fb, 2, out, 1, 1, c2, 1)

    @pl.when(has_above)
    def _():
        for p in range(PLANES):
            halo(1, p, space + 1).wait_send()

    @pl.when(has_below)
    def _():
        for p in range(PLANES):
            halo(0, p, space - 1).wait_send()

    for d in range(1, VELS):
        gather_copy(fsend, frecv, f_ssem, f_rsem, d).wait_send()
        gather_copy(asend, arecv, m_ssem, m_rsem, d).wait_send()
    for d in range(1, LANES):
        y_copy(d).wait_send()
        z_copy(d).wait_send()
    end_planes()


def body(distribution, freestream, face_area, cell_volume, neighbours, wall_flags, send_cells):
    dma = pltpu.SemaphoreType.DMA
    hbm = pl.BlockSpec(memory_space=pltpu.HBM)
    new = pl.pallas_call(
        kernel,
        out_shape=pltpu.VMEM((PLANES, CELLS, FLAT), F32),
        in_specs=[hbm] * 9,
        out_specs=pl.BlockSpec(memory_space=pltpu.VMEM),
        scratch_shapes=[
            pltpu.VMEM((PLANES, FLAT), F32),
            pltpu.VMEM((3, FACES, CELLS), F32),
            pltpu.VMEM((1, CELLS), F32),
            pltpu.VMEM((FACES, CELLS), jnp.int32),
            pltpu.VMEM((FACES, CELLS), jnp.int32),
            pltpu.SMEM((2, HALO), jnp.int32),
            pltpu.VMEM((PLANES, CELLS, FLAT), F32),
            pltpu.VMEM((2, PLANES, HALO, FLAT), F32),
            pltpu.VMEM((2, PLANES, HALO, FLAT), F32),
            pltpu.VMEM((FLAT, 128), BF16),
            pltpu.VMEM((28 * 128 + 16, 128), BF16),
            pltpu.VMEM((PLANES, CELLS, FLAT), F32),
            pltpu.VMEM((PLANES + 4, CELLS, WIDE), F32),
            pltpu.VMEM((4, CELLS, FLAT), F32),
            pltpu.VMEM((PLANES + 2, CELLS, WIDE), F32),
            pltpu.VMEM((2, 2, CELLS, 4 * 128), F32),
            pltpu.VMEM((2 * FACES * PLANES * CELLS, FLAT), BF16),
            pltpu.VMEM((FACES * PLANES * CELLS, 128), F32),
            pltpu.VMEM((3 * PLANES * CELLS, FLAT), BF16),
            pltpu.VMEM((CELLS, FLAT), F32),
            pltpu.VMEM((CELLS, FLAT), F32),
            pltpu.VMEM((CELLS, FLAT), F32),
            pltpu.VMEM((2, CELLS, FLAT), F32),
            pltpu.VMEM((2, 3, CELLS, FLAT), F32),
            pltpu.VMEM((32, 128), F32),
            pltpu.VMEM((32, CELLS, 128), F32),
            pltpu.VMEM((96, 64), BF16),
            pltpu.VMEM((1, 256), F32),
            pltpu.VMEM((VELS, 1, 256), F32),
            pltpu.VMEM((2, 128), F32),
            pltpu.VMEM((VELS, 2, 128), F32),
            pltpu.VMEM((LANES, 8, 128), F32),
            pltpu.VMEM((LANES, 8, 128), F32),
            dma((PLANES,)), dma((2, PLANES)), dma((2, PLANES)),
            dma((VELS,)), dma((VELS,)), dma((VELS,)), dma((VELS,)), dma((2, 2)), dma((2, 2)),
            dma((8,)), dma((2, LANES, 2)), dma((2, LANES, 2)), dma((2, 2)), dma((2, 2)),
            dma((2, LANES)), dma((2, LANES)),
        ],
        compiler_params=pltpu.CompilerParams(
            collective_id=0, has_side_effects=True, vmem_limit_bytes=56 * 1024 * 1024
        ),
    )(
        jnp.transpose(distribution, (1, 0, 2)), freestream, face_area, cell_volume.reshape(1, CELLS), neighbours,
        wall_flags, send_cells, jnp.asarray(sum_weights()), jnp.asarray(small_matrices()),
    )
    return jnp.transpose(new, (1, 0, 2))


def solution(mesh):
    in_specs = (
        P("space", "vel", None),
        P("vel", None),
        P(None, None, "space"),
        P("space"),
        P(None, "space"),
        P(None, "space"),
        P(None, "space"),
    )
    out_specs = P("space", "vel", None)
    return jax.shard_map(body, mesh=mesh, in_specs=in_specs, out_specs=out_specs, check_vma=False)
```

```python
import jax
import jax.numpy as jnp
import numpy as np
from jax import lax
from jax.experimental import pallas as pl
from jax.experimental.pallas import tpu as pltpu
from jax.sharding import PartitionSpec as P

NV = 48
FLAT = NV * NV
STEP = 0.25
DT = 0.02
RATE = 0.002
FACES = 6
HALO = 4
CELLS = 16
PLANES = 3
MARGIN = 128
WIDE = FLAT + 2 * MARGIN
VELS = 16
WALL_ROWS = FACES * PLANES * CELLS
LANES = 4
PARTS = ((8, 12), (12, 15), (15, 18), (0, 8))
MESH = pl.DeviceIdType.MESH
F32 = jnp.float32
BF16 = jnp.bfloat16


X_FACE = tuple(range(18))
SUMMED = (
    ((0, 0), (0, 1), (1, 0), (2, 0), (0, 2), (3, 0), (4, 0), (1, 1), (2, 1), (5, 0))
    + tuple((c, 0) for c in range(6, 22))
    + tuple((c, 1) for c in (6, 7, 9, 10, 12, 13, 15, 16, 18, 19, 20, 21))
    + tuple((c, 2) for c in (6, 9, 12, 15, 18, 19, 20, 21))
)
AT_FACE = len(SUMMED)
SENT = tuple(c for c, _ in SUMMED) + X_FACE
KINDS = tuple(power for _, power in SUMMED) + (3,) * len(X_FACE)


def plane_sums(j, k):
    y, z = (j - (NV - 1) / 2.0) * STEP, (k - (NV - 1) / 2.0) * STEP
    one = np.ones_like(y)
    lo_y, hi_y, lo_z, hi_z = ((at == end).astype(np.float64) for at in (j, k) for end in (0, NV - 1))
    sums = [one, y, z, y * y, z * z, y * z]
    for face in (lo_y, hi_y):
        sums += [face, face * z, face * z * z]
    for face in (lo_z, hi_z):
        sums += [face, face * y, face * y * y]
    sums += [lo_y * lo_z, lo_y * hi_z, hi_y * lo_z, hi_y * hi_z]
    return np.stack(sums)


def two_parts(x):
    hi = x.astype(jnp.bfloat16)
    return hi, (x - hi.astype(np.float64)).astype(jnp.bfloat16)


def sum_weights():
    at = np.arange(FLAT)
    weights = plane_sums(at // NV, at % NV)[list(SENT)].T
    return np.concatenate(two_parts(weights), axis=1)


def stencil_moments():
    line = np.array([0, 1, 2, 17, 23, 30, 45, 46, 47])
    at = np.stack(np.meshgrid(line, line, line, indexing="ij")).reshape(3, -1)

    def velocity(index):
        return (index - (NV - 1) / 2.0) * STEP

    planes = plane_sums(at[1], at[2])
    x = velocity(at[0])
    basis = [planes[c] * x**power for c, power in SUMMED]
    for end in (0, NV - 1):
        basis += [planes[c] * (at[0] == end) for c in X_FACE]

    def polynomials(index):
        v = velocity(index)
        inside = np.all((index >= 0) & (index < NV), axis=0)
        vx, vy, vz = v
        return np.stack([np.ones_like(vx), vx, vy, vz, vx * vx, vy * vy, vz * vz, vx * vy, vx * vz, vy * vz]) * inside

    def moved(*steps):
        index = at.copy()
        for axis, step in steps:
            index[axis] += step
        return polynomials(index)

    v = velocity(at)
    first = [(moved((i, -1)) - moved((i, 1))) / (2 * STEP) for i in range(3)]
    terms = [sum(v[i] * first[i] for i in range(3))] + first
    terms += [(moved((i, -1)) - 2 * moved() + moved((i, 1))) / STEP**2 for i in range(3)]
    for i, j in ((0, 1), (0, 2), (1, 2)):
        corner = {(p, q): moved((i, p), (j, q)) for p in (-1, 1) for q in (-1, 1)}
        terms.append((corner[-1, -1] - corner[-1, 1] - corner[1, -1] + corner[1, 1]) / (2 * STEP**2))
    wanted = np.concatenate(terms)
    found = np.linalg.lstsq(np.stack(basis).T, wanted.T, rcond=None)[0]
    found = np.round(found * 1024) / 1024
    assert np.abs(np.stack(basis).T @ found - wanted.T).max() < 1e-6
    out = np.zeros((128, 100))
    out[: len(basis)] = found
    return out


def small_matrices():
    row = np.arange(128)[:, None]
    col = np.arange(1280)[None, :] // 128
    ratios = row // 16 == col[:, :768]
    moments = row % 16 == col
    products = (row % 10 == col) & (row < 110)
    stencil = np.zeros((128, 128))
    stencil[:, :100] = stencil_moments()
    for m in range(10):
        stencil[m, 100 + m] = 1.0
    plain = [a.astype(jnp.bfloat16) for a in (ratios, moments, products)]
    whole = np.concatenate(plain + list(two_parts(stencil)), axis=1)
    kinds = np.zeros((16, 128))
    kinds[0:4] = np.arange(4)[:, None] == np.array(KINDS + KINDS)[None, :]
    return np.concatenate(np.split(whole, whole.shape[1] // 128, axis=1) + [kinds.astype(jnp.bfloat16)], axis=0)


def split2(x):
    hi = x.astype(BF16)
    return hi, (x - hi.astype(F32)).astype(BF16)


def split3(x):
    hi = x.astype(BF16)
    r = x - hi.astype(F32)
    mid = r.astype(BF16)
    return hi, mid, (r - mid.astype(F32)).astype(BF16)


def lane_sums(acc):
    ones = jnp.ones((16, 128), BF16)
    total = None
    for part in split3(acc):
        term = lax.dot_general(ones, part, (((1,), (1,)), ((), ())), preferred_element_type=F32)
        total = term if total is None else total + term
    return total[0:1]


def times(x, matrix):
    out = jnp.dot(jnp.concatenate(split3(x), axis=0), matrix, preferred_element_type=F32)
    return out[0:16] + out[16:32] + out[32:48]


def spread(row, matrix):
    lane = lax.broadcasted_iota(jnp.int32, (CELLS, 128), 1)
    cell = lax.broadcasted_iota(jnp.int32, (CELLS, 128), 0)
    own = jnp.where((lane & (CELLS - 1)) == cell, jnp.broadcast_to(row, (CELLS, 128)), 0.0)
    return times(own, matrix)


def columns(matrix, first, count):
    return jnp.concatenate([matrix[128 * i : 128 * i + 128, :] for i in range(first, first + count)], axis=1)


FAR_FIRST = sorted(range(1, VELS), key=lambda d: -min(d, VELS - d))


def rep(x, n):
    return jnp.concatenate([x] * n, axis=1)


def kernel(
    dist, free_h, area_h, vol_h, nb_h, wall_h, send_h, wts_h, mat_h, out,
    free, area, vol, nb, wall, send, distv, hs, hr, wts, mat, pb, fa, wb, fb, relay, qm, fq, pm,
    yt, zt, mt, kt, lf, prm, sb, lhs, fsend, frecv, asend, arecv, yrecv, zrecv,
    in_sem, h_ssem, h_rsem, f_ssem, f_rsem, m_ssem, m_rsem, p_ssem, p_rsem,
    s_sem, z_ssem, z_rsem, r_ssem, r_rsem, b_ssem, b_rsem,
):
    space = lax.axis_index("space")
    vel = lax.axis_index("vel")
    blocks = lax.axis_size("space")
    has_below, has_above = space > 0, space < blocks - 1
    has_left, has_right = vel > 0, vel < VELS - 1

    loads = [pltpu.make_async_copy(dist.at[p], distv.at[p], in_sem.at[p]) for p in range(PLANES)]
    small = [
        pltpu.make_async_copy(src, dst, s_sem.at[i])
        for i, (src, dst) in enumerate(
            ((area_h, area), (nb_h, nb), (wall_h, wall), (vol_h, vol), (send_h, send), (free_h, free))
        )
    ]
    late = [
        pltpu.make_async_copy(src, dst, s_sem.at[6 + i]) for i, (src, dst) in enumerate(((wts_h, wts), (mat_h, mat)))
    ]
    for copy in small + loads + late:
        copy.start()

    barrier = pltpu.get_barrier_semaphore()
    for d in FAR_FIRST:
        pl.semaphore_signal(barrier, 1, device_id=(space, lax.rem(vel + d, VELS)), device_id_type=MESH)

    @pl.when(has_below)
    def _():
        pl.semaphore_signal(barrier, 1, device_id=(space - 1, vel), device_id_type=MESH)

    @pl.when(has_above)
    def _():
        pl.semaphore_signal(barrier, 1, device_id=(space + 1, vel), device_id_type=MESH)

    flat = lax.broadcasted_iota(jnp.int32, (CELLS, FLAT), 1).astype(F32)
    row = jnp.floor((flat + 0.5) / NV)
    y = (row - (NV - 1) / 2.0) * STEP
    z = (flat - row * NV - (NV - 1) / 2.0) * STEP
    yt[...] = y
    zt[...] = z
    last_z = (NV - 1) / 2.0 * STEP - 0.1
    kt[0] = jnp.where(z < last_z, 1.0, 0.0)
    kt[1] = jnp.where(z > -last_z, 1.0, 0.0)
    mt[...] = jnp.exp(-(y * y + z * z) / 2.0)
    for buf, count in ((fa, PLANES + 4), (fb, PLANES + 2)):
        for plane in range(count):
            buf[plane, :, 0:MARGIN] = jnp.zeros((CELLS, MARGIN), F32)
            buf[plane, :, MARGIN + FLAT :] = jnp.zeros((CELLS, MARGIN), F32)

    @pl.when(jnp.logical_not(has_left))
    def _():
        for plane in (fa.at[0], fa.at[1], fb.at[0]):
            plane[...] = jnp.zeros((CELLS, WIDE), F32)

    @pl.when(jnp.logical_not(has_right))
    def _():
        for plane in (fa.at[PLANES + 2], fa.at[PLANES + 3], fb.at[PLANES + 1]):
            plane[...] = jnp.zeros((CELLS, WIDE), F32)

    for copy in small:
        copy.wait()

    prm[...] = jnp.zeros((32, 128), F32)
    for i in range(3):
        prm[6 * i : 6 * i + 6, 0:CELLS] = area[i]
    prm[18:24, 0:CELLS] = nb[...].astype(F32)
    prm[24:30, 0:CELLS] = wall[...].astype(F32)
    prm[30:31, 0:CELLS] = DT / vol[...]
    cols = prm[...].T[0:CELLS]
    for r in range(31):
        sb[r] = jnp.broadcast_to(cols[:, r : r + 1], (CELLS, 128))
    lane = lax.broadcasted_iota(jnp.int32, (CELLS, 64), 1) & 31
    for s in range(FACES):
        inside = (lane.astype(F32) == sb[18 + s][:, 0:64]) & (sb[24 + s][:, 0:64] < 0.5)
        lhs[16 * s : 16 * s + 16, :] = jnp.where(inside, 1.0, 0.0).astype(BF16)

    for copy in loads:
        copy.wait()
    for p in range(PLANES):
        for side in range(2):
            for r in range(HALO):
                hs[side, p, r : r + 1, :] = distv[p, pl.ds(send[side, r], 1), :]

    def x_of(p):
        return ((vel * PLANES + p).astype(F32) - (NV - 1) / 2.0) * STEP

    xs = {p: x_of(p) for p in range(-2, PLANES + 2)}
    mx = {p: jnp.exp(jnp.full((CELLS, 128), -0.5, F32) * (x * x)) for p, x in xs.items()}

    def gather_copy(src, dst, ssem, rsem, d):
        return pltpu.make_async_remote_copy(
            src_ref=src, dst_ref=dst.at[d], send_sem=ssem.at[d], recv_sem=rsem.at[d],
            device_id=(space, lax.rem(vel + d, VELS)), device_id_type=MESH,
        )

    def total(src, dst, ssem, rsem):
        acc = src[...]
        for d in range(1, VELS):
            gather_copy(src, dst, ssem, rsem, d).wait_recv()
            acc = acc + dst[d]
        return acc

    def flux_plane(p, carry):
        sx = [sb[s] * xs[p] for s in range(FACES)]

        def step(t, carry):
            off = pl.multiple_of(t * 256, 128)
            outs, ins = list(carry[:FACES]), list(carry[FACES:])
            for j in range(2):
                o = pl.ds(off + 128 * j, 128)
                dd, yy, zz = distv[p, :, o], yt[:, o], zt[:, o]
                mm = mt[:, o] * mx[p]
                for s in range(FACES):
                    w = jnp.maximum(sx[s] + sb[6 + s] * yy + sb[12 + s] * zz, 0.0)
                    outs[s] = outs[s] + w * dd
                    ins[s] = ins[s] + w * mm
            return tuple(outs + ins)

        return lax.fori_loop(0, FLAT // 256, step, carry)

    carry = tuple(jnp.zeros((CELLS, 128), F32) for _ in range(2 * FACES))
    for p in range(PLANES):
        carry = flux_plane(p, carry)
    fsend[0:1, 0:96] = lane_sums(jnp.concatenate(carry[:FACES], axis=0))
    fsend[0:1, 128:224] = lane_sums(jnp.concatenate(carry[FACES:], axis=0))
    fsend[0:1, 96:128] = jnp.zeros((1, 32), F32)
    fsend[0:1, 224:256] = jnp.ones((1, 32), F32)
    peers = VELS - 1 + has_below.astype(jnp.int32) + has_above.astype(jnp.int32)
    pl.semaphore_wait(barrier, peers)

    def halo(side, p, target):
        return pltpu.make_async_remote_copy(
            src_ref=hs.at[side, p], dst_ref=hr.at[1 - side, p],
            send_sem=h_ssem.at[side, p], recv_sem=h_rsem.at[1 - side, p],
            device_id=(target, vel), device_id_type=MESH,
        )

    y_at, z_at = lax.rem(vel, LANES), vel // LANES
    first = jnp.where(y_at == LANES - 1, PLANES - 1, 0)
    order = (1, first, PLANES - 1 - first)
    for d in FAR_FIRST:
        gather_copy(fsend, frecv, f_ssem, f_rsem, d).start()

    for p in order:

        @pl.when(has_above)
        def _():
            halo(1, p, space + 1).start()

        @pl.when(has_below)
        def _():
            halo(0, p, space - 1).start()

    @pl.when(jnp.logical_not(has_below))
    def _():
        for p in range(PLANES):
            hr[0, p] = jnp.broadcast_to(free[p : p + 1, :], (HALO, FLAT))

    @pl.when(jnp.logical_not(has_above))
    def _():
        for p in range(PLANES):
            hr[1, p] = jnp.broadcast_to(free[p : p + 1, :], (HALO, FLAT))

    for copy in late:
        copy.wait()

    def unit_walls(t, acc):
        off = pl.multiple_of(t * 128, 128)
        o = pl.ds(off, 128)
        yy, zz, mm = yt[:, o], zt[:, o], mt[:, o]
        for s in range(FACES):
            along = sb[6 + s] * yy + sb[12 + s] * zz
            for p in range(PLANES):
                at = (s * PLANES + p) * CELLS
                hi, lo = split2(jnp.minimum(sb[s] * xs[p] + along, 0.0) * (mm * mx[p]))
                qm[at : at + CELLS, o] = hi
                qm[WALL_ROWS + at : WALL_ROWS + at + CELLS, o] = lo
        return acc

    lax.fori_loop(0, FLAT // 128, unit_walls, 0, unroll=3)
    unit = jnp.dot(qm[...], wts[...], preferred_element_type=F32)
    fq[...] = unit[0:WALL_ROWS] + unit[WALL_ROWS:]

    def sides(right):
        return (LANES - 1, 0, 1, z_at < LANES - 1) if right else (0, LANES - 1, -1, z_at > 0)

    def ends(right, n):
        return (1 + n, n) if right else (n, PLANES + 2 + n)

    def lanes_of(right, q):
        begin, last = PARTS[q if right else LANES - 1 - q]
        return begin, last - begin

    def near_copy(right, n):
        src, dst = ends(right, n)
        i = 1 if right else 0
        return pltpu.make_async_remote_copy(
            src_ref=pb.at[src], dst_ref=fa.at[dst, :, pl.ds(MARGIN, FLAT)],
            send_sem=p_ssem.at[i, n], recv_sem=p_rsem.at[i, n],
            device_id=(space, vel + 1 if right else vel - 1), device_id_type=MESH,
        )

    def part_copy(right, n, q):
        home, other, dz, _ = sides(right)
        src, dst = ends(right, n)
        begin, count = lanes_of(right, q)
        lanes, wide = pl.ds(128 * begin, 128 * count), pl.ds(MARGIN + 128 * begin, 128 * count)
        i = 1 if right else 0
        if q == home:
            dst_ref, recv, to = fa.at[dst, :, wide], z_rsem.at[i, q, n], (z_at + dz) * LANES + other
        else:
            dst_ref, recv, to = relay.at[i, n, :, pl.ds(0, 128 * count)], r_rsem.at[i, n], z_at * LANES + q
        return pltpu.make_async_remote_copy(
            src_ref=pb.at[src, :, lanes], dst_ref=dst_ref, send_sem=z_ssem.at[i, q, n], recv_sem=recv,
            device_id=(space, to), device_id_type=MESH,
        )

    def relay_copy(right, n, q):
        home, other, dz, _ = sides(right)
        src, dst = ends(right, n)
        begin, count = lanes_of(right, q)
        wide = pl.ds(MARGIN + 128 * begin, 128 * count)
        i = 1 if right else 0
        return pltpu.make_async_remote_copy(
            src_ref=relay.at[i, n, :, pl.ds(0, 128 * count)], dst_ref=fa.at[dst, :, wide],
            send_sem=r_ssem.at[i, n], recv_sem=z_rsem.at[i, q, n],
            device_id=(space, (z_at + dz) * LANES + other), device_id_type=MESH,
        )

    def send_far(right, n):
        home, _, _, inner = sides(right)

        @pl.when((y_at == home) & inner)
        def _():
            for q in sorted(range(LANES), key=lambda q: q == home):
                part_copy(right, n, q).start()

    def send_near():
        for right in (True, False):
            home, _, _, _ = sides(right)

            @pl.when(y_at != home)
            def _():
                for n in range(2):
                    near_copy(right, n).start()

    def pass_on():
        for step in range(2):
            for right in (True, False):
                n = step if right else 1 - step
                home, _, _, inner = sides(right)
                for q in range(LANES):
                    if q != home:

                        @pl.when((y_at == q) & inner)
                        def _():
                            part_copy(right, n, q).wait_recv()
                            relay_copy(right, n, q).start()

    def recv_planes(right, when):
        home, other, _, _ = sides(right)
        from_z = z_at > 0 if right else z_at < LANES - 1

        @pl.when((y_at != other) & when)
        def _():
            for n in range(2):
                near_copy(right, n).wait_recv()

        @pl.when((y_at == other) & from_z & when)
        def _():
            for n in range(2):
                for q in range(LANES):
                    if q == home:
                        part_copy(right, n, q).wait_recv()
                    else:
                        relay_copy(right, n, q).wait_recv()

    def end_planes():
        for right in (True, False):
            home, _, _, inner = sides(right)

            @pl.when(y_at != home)
            def _():
                for n in range(2):
                    near_copy(right, n).wait_send()

            @pl.when((y_at == home) & inner)
            def _():
                for n in range(2):
                    for q in range(LANES):
                        part_copy(right, n, q).wait_send()

            for q in range(LANES):
                if q != home:

                    @pl.when((y_at == q) & inner)
                    def _():
                        for n in range(2):
                            relay_copy(right, n, q).wait_send()

    def flow_plane(p):
        x = x_of(p)
        sx = [sb[s] * x for s in range(FACES)]
        scale = sb[30]

        def step(t, acc):
            off = pl.multiple_of(t * 256, 128)
            o = pl.ds(off, 256)
            ext = jnp.concatenate([distv[p, :, o], hr[0, p, :, o], hr[1, p, :, o], jnp.zeros((8, 256), F32)], axis=0)
            picked = jnp.dot(lhs[...], jnp.concatenate(split2(ext), axis=0), preferred_element_type=F32)
            for j in range(2):
                o = pl.ds(off + 128 * j, 128)
                dd, yy, zz = distv[p, :, o], yt[:, o], zt[:, o]
                out_sum, in_sum = None, None
                for s in range(FACES):
                    w = sx[s] + sb[6 + s] * yy + sb[12 + s] * zz
                    up = jnp.maximum(w, 0.0)
                    term = (w - up) * picked[16 * s : 16 * s + 16, 128 * j : 128 * j + 128]
                    out_sum = up if s == 0 else out_sum + up
                    in_sum = term if s == 0 else in_sum + term
                f = dd - scale * (out_sum * dd + in_sum)
                pb[p, :, o] = f
                for i, part in enumerate(split3(f)):
                    pm[pl.ds(pl.multiple_of((i * PLANES + p) * CELLS, CELLS), CELLS), o] = part
            return acc

        lax.fori_loop(0, FLAT // 256, step, 0, unroll=True)

    for step, p in enumerate(order):

        @pl.when(has_below)
        def _():
            halo(1, p, space + 1).wait_recv()

        @pl.when(has_above)
        def _():
            halo(0, p, space - 1).wait_recv()

        flow_plane(p)
        if step == 0:
            send_far(True, 0)
            send_far(False, 1)
        else:

            @pl.when(p == PLANES - 1)
            def _():
                send_far(True, 1)

            @pl.when(p == 0)
            def _():
                send_far(False, 0)

    rows = PLANES * CELLS
    flow = jnp.dot(pm[...], wts[...], preferred_element_type=F32)
    flow = flow[0:rows] + flow[rows : 2 * rows] + flow[2 * rows :]

    flux = total(fsend, frecv, f_ssem, f_rsem)
    ratio = spread(flux[:, 0:128] / jnp.where(flux[:, 128:256] > 0.0, flux[:, 128:256], 1.0), columns(mat, 0, 6))
    for s in range(FACES):
        sb[18 + s] = jnp.where(sb[24 + s] > 0.5, -sb[30] * ratio[:, 128 * s : 128 * s + 128], 0.0)

    def wall_planes(off, planes):
        o = pl.ds(off, 128)
        yy, zz, mm = yt[:, o], zt[:, o], mt[:, o]
        sums = [None] * len(planes)
        for s in range(FACES):
            along = sb[6 + s] * yy + sb[12 + s] * zz
            for i, p in enumerate(planes):
                term = jnp.minimum(sb[s] * xs[p] + along, 0.0) * sb[18 + s]
                sums[i] = term if s == 0 else sums[i] + term
        return [sums[i] * (mm * mx[p]) for i, p in enumerate(planes)]

    acc = []
    for p in range(PLANES):
        plane = flow[CELLS * p : CELLS * p + CELLS]
        for s in range(FACES):
            at = (s * PLANES + p) * CELLS
            plane = plane + sb[18 + s] * fq[at : at + CELLS, :]
        acc.append(plane)
    acc = jnp.concatenate(acc, axis=0)
    acc = acc + pltpu.roll(acc, 64, 1)
    kinds = mat[28 * 128 : 28 * 128 + 16, :].astype(F32)
    sent = None
    for p in range(PLANES):
        weight = kinds[0:1] + kinds[1:2] * xs[p] + kinds[2:3] * (xs[p] * xs[p])
        if p == 0:
            weight = weight + kinds[3:4] * jnp.where(has_left, 0.0, 1.0)
        if p == PLANES - 1:
            weight = weight + kinds[3:4] * jnp.where(has_right, 0.0, 1.0)
        term = weight * acc[CELLS * p : CELLS * p + CELLS]
        sent = term if p == 0 else sent + term

    lane8 = lax.broadcasted_iota(jnp.int32, (8, 128), 1)
    for half in range(2):
        own = jnp.where(lane8 < 16, sent[8 * half : 8 * half + 8], 0.0)
        asend[half : half + 1, :] = jnp.sum(pltpu.roll(own, 0, 1, stride=16, stride_axis=0), axis=0, keepdims=True)
    for d in FAR_FIRST:
        gather_copy(asend, arecv, m_ssem, m_rsem, d).start()

    def along_copy(buf, k, d, to):
        return pltpu.make_async_remote_copy(
            src_ref=buf.at[0], dst_ref=buf.at[d], send_sem=b_ssem.at[k, d], recv_sem=b_rsem.at[k, d],
            device_id=(space, to), device_id_type=MESH,
        )

    def y_copy(d):
        return along_copy(yrecv, 0, d, z_at * LANES + lax.rem(y_at + d, LANES))

    def z_copy(d):
        return along_copy(zrecv, 1, d, lax.rem(z_at + d, LANES) * LANES + y_at)

    yrecv[0] = jnp.where(lane8 < 64, sent[0:8], sent[8:16])
    for d in (2, 1, 3):
        y_copy(d).start()

    def add_walls(t, acc):
        off = pl.multiple_of(t * 128, 128)
        walls = wall_planes(off, range(PLANES))
        for p in range(PLANES):
            fa[p + 2, :, pl.ds(off + MARGIN, 128)] = pb[p, :, pl.ds(off, 128)] + walls[p]
        return acc


    halo_planes = (-2, -1, PLANES, PLANES + 1)

    def halo_walls(t, acc):
        off = pl.multiple_of(t * 128, 128)
        walls = wall_planes(off, halo_planes)
        for i in range(4):
            wb[i, :, pl.ds(off, 128)] = walls[i]
        return acc

    pass_on()
    send_near()
    for d in range(1, LANES):
        y_copy(d).wait_recv()
    zrecv[0] = (yrecv[0] + yrecv[1]) + (yrecv[2] + yrecv[3])
    for d in (2, 1, 3):
        z_copy(d).start()
    lax.fori_loop(0, FLAT // 128, add_walls, 0, unroll=3)
    lax.fori_loop(0, FLAT // 128, halo_walls, 0, unroll=3)

    def coefficients(allm):
        m = [allm[:, 128 * i : 128 * i + 128] for i in range(10)]
        inv = 1.0 / m[0]
        ux, uy, uz = m[1] * inv, m[2] * inv, m[3] * inv
        cxx, cyy, czz = m[4] * inv - ux * ux, m[5] * inv - uy * uy, m[6] * inv - uz * uz
        cxy, cxz, cyz = m[7] * inv - ux * uy, m[8] * inv - ux * uz, m[9] * inv - uy * uz
        theta = (cxx + cyy + czz) / 3.0
        a = (RATE * STEP**3) * m[0] * jnp.exp(0.19 * jnp.log(theta))
        lx, ly, lz = 0.5 * (theta + cxx), 0.5 * (theta + cyy), 0.5 * (theta + czz)
        terms = (a, -a * ux, -a * uy, -a * uz, a * lx, a * ly, a * lz, 0.5 * a * cxy, 0.5 * a * cxz, 0.5 * a * cyz)
        return terms, dict(
            ux=ux, a=a, k0=1.0 - 32.0 * a * (lx + ly + lz), lx=16.0 * a * lx,
            ys=a * (16.0 * ly + 0.5), a2=2.0 * a, a2uy=2.0 * a * uy, a2uz=2.0 * a * uz, zq=16.0 * a * lz,
            gxy=4.0 * a * cxy, gxz=4.0 * a * cxz, gyz=4.0 * a * cyz,
        )

    lane = lax.broadcasted_iota(jnp.int32, (CELLS, 128), 1)
    cell = lax.broadcasted_iota(jnp.int32, (CELLS, 128), 0)
    moments = total(asend, arecv, m_ssem, m_rsem)
    moments = jnp.concatenate([jnp.broadcast_to(moments[half : half + 1], (8, 128)) for half in range(2)], axis=0)
    moments = jnp.where((lane >> 4) == (cell & 7), moments, 0.0)
    terms, c1 = coefficients(times(moments, columns(mat, 6, 10)))

    def second_coefficients():
        for d in range(1, LANES):
            z_copy(d).wait_recv()
        packed = (zrecv[0] + zrecv[1]) + (zrecv[2] + zrecv[3])

        def unpack(x):
            return jnp.concatenate([x, pltpu.roll(x, 64, 1)], axis=0)

        on_face = (lane >= AT_FACE) & (lane < 64)
        least = unpack(zrecv[z_at])
        largest = unpack(zrecv[lax.rem(z_at + 1, LANES)])
        sums = jnp.where(lane < AT_FACE, unpack(packed), jnp.where(on_face, least, 0.0))
        sums = sums + pltpu.roll(jnp.where(on_face, largest, 0.0), len(X_FACE), 1)
        factor = jnp.where(lane < 110, 1.0, 0.0)
        for t in range(10):
            factor = jnp.where((lane >= 10 * t) & (lane < 10 * t + 10), terms[t], factor)
        stencil = times(sums, columns(mat, 26, 2))
        return coefficients(times(factor * (stencil[:, 0:128] + stencil[:, 128:256]), columns(mat, 16, 10)))[1]

    width = FLAT

    def lane_factors(k, c):
        a2, a2uy, a2uz, zq = (rep(c[q], FLAT // 128) for q in ("a2", "a2uy", "a2uz", "zq"))
        drift = a2 * zt[...] - a2uz
        lf[k, 0] = a2 * yt[...] - a2uy
        lf[k, 1] = zq + drift
        lf[k, 2] = zq - drift

    def relax_plane(src, at, dst, dst_at, p, c, k):
        n = width // 128
        margin = MARGIN if dst.shape[-1] == WIDE else 0
        x = x_of(p)
        drift_n = c["a2"] * (x + STEP - c["ux"]) + c["lx"]
        drift_p = c["lx"] - c["a2"] * (x - STEP - c["ux"])
        kn, kp, k0 = rep(drift_n, n), rep(drift_p, n), rep(c["k0"], n)
        ys, gxy, gxz, gyz = (rep(c[q], n) for q in ("ys", "gxy", "gxz", "gyz"))

        def step(t, acc):
            off = pl.multiple_of(t * width, 128)
            win = pl.ds(off, width + 2 * MARGIN)
            cen = pl.ds(off, width)
            cw, nw, pw = src[at, :, win], src[at + 1, :, win], src[at - 1, :, win]
            xw = nw - pw
            total_w = width + 2 * MARGIN

            def up(v):
                return pltpu.roll(v, total_w - NV, 1)[:, MARGIN : MARGIN + width]

            def down(v):
                return pltpu.roll(v, NV, 1)[:, MARGIN : MARGIN + width]

            cc, nn, pp = (v[:, MARGIN : MARGIN + width] for v in (cw, nw, pw))
            u, d = up(cw), down(cw)
            diff = u - d
            res = k0 * cc + kn * nn + kp * pp
            res = res + ys * (u + d) + lf[k, 0, :, cen] * diff + gxy * (up(xw) - down(xw))
            cross = gxz * (nn - pp) + gyz * diff
            plus = lf[k, 1, :, cen] * cc + cross
            minus = lf[k, 2, :, cen] * cc - cross
            res = res + kt[0, :, cen] * pltpu.roll(plus, width - 1, 1)
            res = res + kt[1, :, cen] * pltpu.roll(minus, 1, 1)
            dst[dst_at, :, pl.ds(off + margin, width)] = res
            return acc

        lax.fori_loop(0, FLAT // width, step, 0, unroll=True)

    lane_factors(0, c1)
    relax_plane(fa, 3, fb, 2, 1, c1, 0)

    def edge(right):
        return jnp.where(right, PLANES + 1, 2)

    def relax_side(right):
        left = jnp.logical_not(right)
        recv_planes(True, left)
        recv_planes(False, right)
        arrived = jnp.where(right, PLANES + 2, 0)
        walls = jnp.where(right, 2, 0)
        halo_at = jnp.where(right, PLANES + 2, 1)

        @pl.when((right & has_right) | (left & has_left))
        def _():
            for i in range(2):
                fa[arrived + i, :, MARGIN : MARGIN + FLAT] = fa[arrived + i, :, MARGIN : MARGIN + FLAT] + wb[walls + i]
            relax_plane(fa, halo_at, fb, halo_at - 1, halo_at - 2, c1, 0)

        relax_plane(fa, edge(right), fb, edge(right) - 1, edge(right) - 2, c1, 0)

    def relax_again(right):
        relax_plane(fb, edge(right) - 1, out, edge(right) - 2, edge(right) - 2, c2, 1)

    right_first = y_at == 0
    right_last = jnp.logical_not(right_first)
    relax_side(right_first)
    relax_side(right_last)
    c2 = second_coefficients()
    lane_factors(1, c2)
    relax_again(right_first)
    relax_again(right_last)
    relax_plane(fb, 2, out, 1, 1, c2, 1)

    @pl.when(has_above)
    def _():
        for p in range(PLANES):
            halo(1, p, space + 1).wait_send()

    @pl.when(has_below)
    def _():
        for p in range(PLANES):
            halo(0, p, space - 1).wait_send()

    for d in range(1, VELS):
        gather_copy(fsend, frecv, f_ssem, f_rsem, d).wait_send()
        gather_copy(asend, arecv, m_ssem, m_rsem, d).wait_send()
    for d in range(1, LANES):
        y_copy(d).wait_send()
        z_copy(d).wait_send()
    end_planes()


def body(distribution, freestream, face_area, cell_volume, neighbours, wall_flags, send_cells):
    dma = pltpu.SemaphoreType.DMA
    hbm = pl.BlockSpec(memory_space=pltpu.HBM)
    new = pl.pallas_call(
        kernel,
        out_shape=pltpu.VMEM((PLANES, CELLS, FLAT), F32),
        in_specs=[hbm] * 9,
        out_specs=pl.BlockSpec(memory_space=pltpu.VMEM),
        scratch_shapes=[
            pltpu.VMEM((PLANES, FLAT), F32),
            pltpu.VMEM((3, FACES, CELLS), F32),
            pltpu.VMEM((1, CELLS), F32),
            pltpu.VMEM((FACES, CELLS), jnp.int32),
            pltpu.VMEM((FACES, CELLS), jnp.int32),
            pltpu.SMEM((2, HALO), jnp.int32),
            pltpu.VMEM((PLANES, CELLS, FLAT), F32),
            pltpu.VMEM((2, PLANES, HALO, FLAT), F32),
            pltpu.VMEM((2, PLANES, HALO, FLAT), F32),
            pltpu.VMEM((FLAT, 128), BF16),
            pltpu.VMEM((28 * 128 + 16, 128), BF16),
            pltpu.VMEM((PLANES, CELLS, FLAT), F32),
            pltpu.VMEM((PLANES + 4, CELLS, WIDE), F32),
            pltpu.VMEM((4, CELLS, FLAT), F32),
            pltpu.VMEM((PLANES + 2, CELLS, WIDE), F32),
            pltpu.VMEM((2, 2, CELLS, 4 * 128), F32),
            pltpu.VMEM((2 * FACES * PLANES * CELLS, FLAT), BF16),
            pltpu.VMEM((FACES * PLANES * CELLS, 128), F32),
            pltpu.VMEM((3 * PLANES * CELLS, FLAT), BF16),
            pltpu.VMEM((CELLS, FLAT), F32),
            pltpu.VMEM((CELLS, FLAT), F32),
            pltpu.VMEM((CELLS, FLAT), F32),
            pltpu.VMEM((2, CELLS, FLAT), F32),
            pltpu.VMEM((2, 3, CELLS, FLAT), F32),
            pltpu.VMEM((32, 128), F32),
            pltpu.VMEM((32, CELLS, 128), F32),
            pltpu.VMEM((96, 64), BF16),
            pltpu.VMEM((1, 256), F32),
            pltpu.VMEM((VELS, 1, 256), F32),
            pltpu.VMEM((2, 128), F32),
            pltpu.VMEM((VELS, 2, 128), F32),
            pltpu.VMEM((LANES, 8, 128), F32),
            pltpu.VMEM((LANES, 8, 128), F32),
            dma((PLANES,)), dma((2, PLANES)), dma((2, PLANES)),
            dma((VELS,)), dma((VELS,)), dma((VELS,)), dma((VELS,)), dma((2, 2)), dma((2, 2)),
            dma((8,)), dma((2, LANES, 2)), dma((2, LANES, 2)), dma((2, 2)), dma((2, 2)),
            dma((2, LANES)), dma((2, LANES)),
        ],
        compiler_params=pltpu.CompilerParams(
            collective_id=0, has_side_effects=True, vmem_limit_bytes=56 * 1024 * 1024
        ),
    )(
        jnp.transpose(distribution, (1, 0, 2)), freestream, face_area, cell_volume.reshape(1, CELLS), neighbours,
        wall_flags, send_cells, jnp.asarray(sum_weights()), jnp.asarray(small_matrices()),
    )
    return jnp.transpose(new, (1, 0, 2))


def solution(mesh):
    in_specs = (
        P("space", "vel", None),
        P("vel", None),
        P(None, None, "space"),
        P("space"),
        P(None, "space"),
        P(None, "space"),
        P(None, "space"),
    )
    out_specs = P("space", "vel", None)
    return jax.shard_map(body, mesh=mesh, in_specs=in_specs, out_specs=out_specs, check_vma=False)
```

```python
import jax
import jax.numpy as jnp
import numpy as np
from jax import lax
from jax.experimental import pallas as pl
from jax.experimental.pallas import tpu as pltpu
from jax.sharding import PartitionSpec as P

NV = 48
FLAT = NV * NV
STEP = 0.25
DT = 0.02
RATE = 0.002
FACES = 6
HALO = 4
CELLS = 16
PLANES = 3
MARGIN = 128
WIDE = FLAT + 2 * MARGIN
VELS = 16
WALL_ROWS = FACES * PLANES * CELLS
LANES = 4
PARTS = ((8, 12), (12, 15), (15, 18), (0, 8))
MESH = pl.DeviceIdType.MESH
F32 = jnp.float32
BF16 = jnp.bfloat16


X_FACE = tuple(range(18))
SUMMED = (
    ((0, 0), (0, 1), (1, 0), (2, 0), (0, 2), (3, 0), (4, 0), (1, 1), (2, 1), (5, 0))
    + tuple((c, 0) for c in range(6, 22))
    + tuple((c, 1) for c in (6, 7, 9, 10, 12, 13, 15, 16, 18, 19, 20, 21))
    + tuple((c, 2) for c in (6, 9, 12, 15, 18, 19, 20, 21))
)
AT_FACE = len(SUMMED)
SENT = tuple(c for c, _ in SUMMED) + X_FACE
KINDS = tuple(power for _, power in SUMMED) + (3,) * len(X_FACE)


def plane_sums(j, k):
    y, z = (j - (NV - 1) / 2.0) * STEP, (k - (NV - 1) / 2.0) * STEP
    one = np.ones_like(y)
    lo_y, hi_y, lo_z, hi_z = ((at == end).astype(np.float64) for at in (j, k) for end in (0, NV - 1))
    sums = [one, y, z, y * y, z * z, y * z]
    for face in (lo_y, hi_y):
        sums += [face, face * z, face * z * z]
    for face in (lo_z, hi_z):
        sums += [face, face * y, face * y * y]
    sums += [lo_y * lo_z, lo_y * hi_z, hi_y * lo_z, hi_y * hi_z]
    return np.stack(sums)


def two_parts(x):
    hi = x.astype(jnp.bfloat16)
    return hi, (x - hi.astype(np.float64)).astype(jnp.bfloat16)


def sum_weights():
    at = np.arange(FLAT)
    weights = plane_sums(at // NV, at % NV)[list(SENT)].T
    return np.concatenate(two_parts(weights), axis=1)


def stencil_moments():
    line = np.array([0, 1, 2, 17, 23, 30, 45, 46, 47])
    at = np.stack(np.meshgrid(line, line, line, indexing="ij")).reshape(3, -1)

    def velocity(index):
        return (index - (NV - 1) / 2.0) * STEP

    planes = plane_sums(at[1], at[2])
    x = velocity(at[0])
    basis = [planes[c] * x**power for c, power in SUMMED]
    for end in (0, NV - 1):
        basis += [planes[c] * (at[0] == end) for c in X_FACE]

    def polynomials(index):
        v = velocity(index)
        inside = np.all((index >= 0) & (index < NV), axis=0)
        vx, vy, vz = v
        return np.stack([np.ones_like(vx), vx, vy, vz, vx * vx, vy * vy, vz * vz, vx * vy, vx * vz, vy * vz]) * inside

    def moved(*steps):
        index = at.copy()
        for axis, step in steps:
            index[axis] += step
        return polynomials(index)

    v = velocity(at)
    first = [(moved((i, -1)) - moved((i, 1))) / (2 * STEP) for i in range(3)]
    terms = [sum(v[i] * first[i] for i in range(3))] + first
    terms += [(moved((i, -1)) - 2 * moved() + moved((i, 1))) / STEP**2 for i in range(3)]
    for i, j in ((0, 1), (0, 2), (1, 2)):
        corner = {(p, q): moved((i, p), (j, q)) for p in (-1, 1) for q in (-1, 1)}
        terms.append((corner[-1, -1] - corner[-1, 1] - corner[1, -1] + corner[1, 1]) / (2 * STEP**2))
    wanted = np.concatenate(terms)
    found = np.linalg.lstsq(np.stack(basis).T, wanted.T, rcond=None)[0]
    found = np.round(found * 1024) / 1024
    assert np.abs(np.stack(basis).T @ found - wanted.T).max() < 1e-6
    out = np.zeros((128, 100))
    out[: len(basis)] = found
    return out


def small_matrices():
    row = np.arange(128)[:, None]
    col = np.arange(1280)[None, :] // 128
    ratios = row // 16 == col[:, :768]
    moments = row % 16 == col
    products = (row % 10 == col) & (row < 110)
    stencil = np.zeros((128, 128))
    stencil[:, :100] = stencil_moments()
    for m in range(10):
        stencil[m, 100 + m] = 1.0
    plain = [a.astype(jnp.bfloat16) for a in (ratios, moments, products)]
    whole = np.concatenate(plain + list(two_parts(stencil)), axis=1)
    kinds = np.zeros((16, 128))
    kinds[0:4] = np.arange(4)[:, None] == np.array(KINDS + KINDS)[None, :]
    return np.concatenate(np.split(whole, whole.shape[1] // 128, axis=1) + [kinds.astype(jnp.bfloat16)], axis=0)


def split2(x):
    hi = x.astype(BF16)
    return hi, (x - hi.astype(F32)).astype(BF16)


def split3(x):
    hi = x.astype(BF16)
    r = x - hi.astype(F32)
    mid = r.astype(BF16)
    return hi, mid, (r - mid.astype(F32)).astype(BF16)


def lane_sums(acc):
    ones = jnp.ones((16, 128), BF16)
    total = None
    for part in split3(acc):
        term = lax.dot_general(ones, part, (((1,), (1,)), ((), ())), preferred_element_type=F32)
        total = term if total is None else total + term
    return total[0:1]


def times(x, matrix):
    out = jnp.dot(jnp.concatenate(split3(x), axis=0), matrix, preferred_element_type=F32)
    return out[0:16] + out[16:32] + out[32:48]


def spread(row, matrix):
    lane = lax.broadcasted_iota(jnp.int32, (CELLS, 128), 1)
    cell = lax.broadcasted_iota(jnp.int32, (CELLS, 128), 0)
    own = jnp.where((lane & (CELLS - 1)) == cell, jnp.broadcast_to(row, (CELLS, 128)), 0.0)
    return times(own, matrix)


def columns(matrix, first, count):
    return jnp.concatenate([matrix[128 * i : 128 * i + 128, :] for i in range(first, first + count)], axis=1)


FAR_FIRST = sorted(range(1, VELS), key=lambda d: -min(d, VELS - d))


def rep(x, n):
    return jnp.concatenate([x] * n, axis=1)


def kernel(
    dist, free_h, area_h, vol_h, nb_h, wall_h, send_h, wts_h, mat_h, out,
    free, area, vol, nb, wall, send, distv, hs, hr, wts, mat, pb, fa, wb, fb, relay, qm, fq, pm,
    yt, zt, mt, kt, lf, prm, sb, lhs, fsend, frecv, asend, arecv, yrecv, zrecv,
    in_sem, h_ssem, h_rsem, f_ssem, f_rsem, m_ssem, m_rsem, p_ssem, p_rsem,
    s_sem, z_ssem, z_rsem, r_ssem, r_rsem, b_ssem, b_rsem,
):
    space = lax.axis_index("space")
    vel = lax.axis_index("vel")
    blocks = lax.axis_size("space")
    has_below, has_above = space > 0, space < blocks - 1
    has_left, has_right = vel > 0, vel < VELS - 1

    barrier = pltpu.get_barrier_semaphore()
    for d in FAR_FIRST:
        pl.semaphore_signal(barrier, 1, device_id=(space, lax.rem(vel + d, VELS)), device_id_type=MESH)

    @pl.when(has_below)
    def _():
        pl.semaphore_signal(barrier, 1, device_id=(space - 1, vel), device_id_type=MESH)

    @pl.when(has_above)
    def _():
        pl.semaphore_signal(barrier, 1, device_id=(space + 1, vel), device_id_type=MESH)

    loads = [pltpu.make_async_copy(dist.at[p], distv.at[p], in_sem.at[p]) for p in range(PLANES)]
    small = [
        pltpu.make_async_copy(src, dst, s_sem.at[i])
        for i, (src, dst) in enumerate(
            ((area_h, area), (nb_h, nb), (wall_h, wall), (vol_h, vol), (send_h, send), (free_h, free))
        )
    ]
    late = [
        pltpu.make_async_copy(src, dst, s_sem.at[6 + i]) for i, (src, dst) in enumerate(((wts_h, wts), (mat_h, mat)))
    ]
    for copy in small + loads + late:
        copy.start()

    flat = lax.broadcasted_iota(jnp.int32, (CELLS, FLAT), 1).astype(F32)
    row = jnp.floor((flat + 0.5) / NV)
    y = (row - (NV - 1) / 2.0) * STEP
    z = (flat - row * NV - (NV - 1) / 2.0) * STEP
    yt[...] = y
    zt[...] = z
    last_z = (NV - 1) / 2.0 * STEP - 0.1
    kt[0] = jnp.where(z < last_z, 1.0, 0.0)
    kt[1] = jnp.where(z > -last_z, 1.0, 0.0)
    mt[...] = jnp.exp(-(y * y + z * z) / 2.0)
    for buf, count in ((fa, PLANES + 4), (fb, PLANES + 2)):
        for plane in range(count):
            buf[plane, :, 0:MARGIN] = jnp.zeros((CELLS, MARGIN), F32)
            buf[plane, :, MARGIN + FLAT :] = jnp.zeros((CELLS, MARGIN), F32)

    @pl.when(jnp.logical_not(has_left))
    def _():
        for plane in (fa.at[0], fa.at[1], fb.at[0]):
            plane[...] = jnp.zeros((CELLS, WIDE), F32)

    @pl.when(jnp.logical_not(has_right))
    def _():
        for plane in (fa.at[PLANES + 2], fa.at[PLANES + 3], fb.at[PLANES + 1]):
            plane[...] = jnp.zeros((CELLS, WIDE), F32)

    for copy in small:
        copy.wait()

    prm[...] = jnp.zeros((32, 128), F32)
    for i in range(3):
        prm[6 * i : 6 * i + 6, 0:CELLS] = area[i]
    prm[18:24, 0:CELLS] = nb[...].astype(F32)
    prm[24:30, 0:CELLS] = wall[...].astype(F32)
    prm[30:31, 0:CELLS] = DT / vol[...]
    cols = prm[...].T[0:CELLS]
    for r in range(31):
        sb[r] = jnp.broadcast_to(cols[:, r : r + 1], (CELLS, 128))
    lane = lax.broadcasted_iota(jnp.int32, (CELLS, 64), 1) & 31
    for s in range(FACES):
        inside = (lane.astype(F32) == sb[18 + s][:, 0:64]) & (sb[24 + s][:, 0:64] < 0.5)
        lhs[16 * s : 16 * s + 16, :] = jnp.where(inside, 1.0, 0.0).astype(BF16)

    for copy in loads:
        copy.wait()
    for p in range(PLANES):
        for side in range(2):
            for r in range(HALO):
                hs[side, p, r : r + 1, :] = distv[p, pl.ds(send[side, r], 1), :]

    def x_of(p):
        return ((vel * PLANES + p).astype(F32) - (NV - 1) / 2.0) * STEP

    xs = {p: x_of(p) for p in range(-2, PLANES + 2)}
    mx = {p: jnp.exp(jnp.full((CELLS, 128), -0.5, F32) * (x * x)) for p, x in xs.items()}

    def gather_copy(src, dst, ssem, rsem, d):
        return pltpu.make_async_remote_copy(
            src_ref=src, dst_ref=dst.at[d], send_sem=ssem.at[d], recv_sem=rsem.at[d],
            device_id=(space, lax.rem(vel + d, VELS)), device_id_type=MESH,
        )

    def total(src, dst, ssem, rsem):
        acc = src[...]
        for d in range(1, VELS):
            gather_copy(src, dst, ssem, rsem, d).wait_recv()
            acc = acc + dst[d]
        return acc

    def flux_plane(p, carry):
        sx = [sb[s] * xs[p] for s in range(FACES)]

        def step(t, carry):
            off = pl.multiple_of(t * 256, 128)
            outs, ins = list(carry[:FACES]), list(carry[FACES:])
            for j in range(2):
                o = pl.ds(off + 128 * j, 128)
                dd, yy, zz = distv[p, :, o], yt[:, o], zt[:, o]
                mm = mt[:, o] * mx[p]
                for s in range(FACES):
                    w = jnp.maximum(sx[s] + sb[6 + s] * yy + sb[12 + s] * zz, 0.0)
                    outs[s] = outs[s] + w * dd
                    ins[s] = ins[s] + w * mm
            return tuple(outs + ins)

        return lax.fori_loop(0, FLAT // 256, step, carry)

    carry = tuple(jnp.zeros((CELLS, 128), F32) for _ in range(2 * FACES))
    for p in range(PLANES):
        carry = flux_plane(p, carry)
    fsend[0:1, 0:96] = lane_sums(jnp.concatenate(carry[:FACES], axis=0))
    fsend[0:1, 128:224] = lane_sums(jnp.concatenate(carry[FACES:], axis=0))
    fsend[0:1, 96:128] = jnp.zeros((1, 32), F32)
    fsend[0:1, 224:256] = jnp.ones((1, 32), F32)
    peers = VELS - 1 + has_below.astype(jnp.int32) + has_above.astype(jnp.int32)
    pl.semaphore_wait(barrier, peers)

    def halo(side, p, target):
        return pltpu.make_async_remote_copy(
            src_ref=hs.at[side, p], dst_ref=hr.at[1 - side, p],
            send_sem=h_ssem.at[side, p], recv_sem=h_rsem.at[1 - side, p],
            device_id=(target, vel), device_id_type=MESH,
        )

    y_at, z_at = lax.rem(vel, LANES), vel // LANES
    first = jnp.where(y_at == LANES - 1, PLANES - 1, 0)
    order = (1, first, PLANES - 1 - first)
    for d in FAR_FIRST:
        gather_copy(fsend, frecv, f_ssem, f_rsem, d).start()

    for p in order:

        @pl.when(has_above)
        def _():
            halo(1, p, space + 1).start()

        @pl.when(has_below)
        def _():
            halo(0, p, space - 1).start()

    @pl.when(jnp.logical_not(has_below))
    def _():
        for p in range(PLANES):
            hr[0, p] = jnp.broadcast_to(free[p : p + 1, :], (HALO, FLAT))

    @pl.when(jnp.logical_not(has_above))
    def _():
        for p in range(PLANES):
            hr[1, p] = jnp.broadcast_to(free[p : p + 1, :], (HALO, FLAT))

    for copy in late:
        copy.wait()

    def unit_walls(t, acc):
        off = pl.multiple_of(t * 128, 128)
        o = pl.ds(off, 128)
        yy, zz, mm = yt[:, o], zt[:, o], mt[:, o]
        for s in range(FACES):
            along = sb[6 + s] * yy + sb[12 + s] * zz
            for p in range(PLANES):
                at = (s * PLANES + p) * CELLS
                hi, lo = split2(jnp.minimum(sb[s] * xs[p] + along, 0.0) * (mm * mx[p]))
                qm[at : at + CELLS, o] = hi
                qm[WALL_ROWS + at : WALL_ROWS + at + CELLS, o] = lo
        return acc

    lax.fori_loop(0, FLAT // 128, unit_walls, 0, unroll=3)
    unit = jnp.dot(qm[...], wts[...], preferred_element_type=F32)
    fq[...] = unit[0:WALL_ROWS] + unit[WALL_ROWS:]

    def sides(right):
        return (LANES - 1, 0, 1, z_at < LANES - 1) if right else (0, LANES - 1, -1, z_at > 0)

    def ends(right, n):
        return (1 + n, n) if right else (n, PLANES + 2 + n)

    def lanes_of(right, q):
        begin, last = PARTS[q if right else LANES - 1 - q]
        return begin, last - begin

    def near_copy(right, n):
        src, dst = ends(right, n)
        i = 1 if right else 0
        return pltpu.make_async_remote_copy(
            src_ref=pb.at[src], dst_ref=fa.at[dst, :, pl.ds(MARGIN, FLAT)],
            send_sem=p_ssem.at[i, n], recv_sem=p_rsem.at[i, n],
            device_id=(space, vel + 1 if right else vel - 1), device_id_type=MESH,
        )

    def part_copy(right, n, q):
        home, other, dz, _ = sides(right)
        src, dst = ends(right, n)
        begin, count = lanes_of(right, q)
        lanes, wide = pl.ds(128 * begin, 128 * count), pl.ds(MARGIN + 128 * begin, 128 * count)
        i = 1 if right else 0
        if q == home:
            dst_ref, recv, to = fa.at[dst, :, wide], z_rsem.at[i, q, n], (z_at + dz) * LANES + other
        else:
            dst_ref, recv, to = relay.at[i, n, :, pl.ds(0, 128 * count)], r_rsem.at[i, n], z_at * LANES + q
        return pltpu.make_async_remote_copy(
            src_ref=pb.at[src, :, lanes], dst_ref=dst_ref, send_sem=z_ssem.at[i, q, n], recv_sem=recv,
            device_id=(space, to), device_id_type=MESH,
        )

    def relay_copy(right, n, q):
        home, other, dz, _ = sides(right)
        src, dst = ends(right, n)
        begin, count = lanes_of(right, q)
        wide = pl.ds(MARGIN + 128 * begin, 128 * count)
        i = 1 if right else 0
        return pltpu.make_async_remote_copy(
            src_ref=relay.at[i, n, :, pl.ds(0, 128 * count)], dst_ref=fa.at[dst, :, wide],
            send_sem=r_ssem.at[i, n], recv_sem=z_rsem.at[i, q, n],
            device_id=(space, (z_at + dz) * LANES + other), device_id_type=MESH,
        )

    def send_far(right, n):
        home, _, _, inner = sides(right)

        @pl.when((y_at == home) & inner)
        def _():
            for q in sorted(range(LANES), key=lambda q: q == home):
                part_copy(right, n, q).start()

    def send_near():
        for right in (True, False):
            home, _, _, _ = sides(right)

            @pl.when(y_at != home)
            def _():
                for n in range(2):
                    near_copy(right, n).start()

    def pass_on():
        for step in range(2):
            for right in (True, False):
                n = step if right else 1 - step
                home, _, _, inner = sides(right)
                for q in range(LANES):
                    if q != home:

                        @pl.when((y_at == q) & inner)
                        def _():
                            part_copy(right, n, q).wait_recv()
                            relay_copy(right, n, q).start()

    def recv_planes(right, when):
        home, other, _, _ = sides(right)
        from_z = z_at > 0 if right else z_at < LANES - 1

        @pl.when((y_at != other) & when)
        def _():
            for n in range(2):
                near_copy(right, n).wait_recv()

        @pl.when((y_at == other) & from_z & when)
        def _():
            for n in range(2):
                for q in range(LANES):
                    if q == home:
                        part_copy(right, n, q).wait_recv()
                    else:
                        relay_copy(right, n, q).wait_recv()

    def end_planes():
        for right in (True, False):
            home, _, _, inner = sides(right)

            @pl.when(y_at != home)
            def _():
                for n in range(2):
                    near_copy(right, n).wait_send()

            @pl.when((y_at == home) & inner)
            def _():
                for n in range(2):
                    for q in range(LANES):
                        part_copy(right, n, q).wait_send()

            for q in range(LANES):
                if q != home:

                    @pl.when((y_at == q) & inner)
                    def _():
                        for n in range(2):
                            relay_copy(right, n, q).wait_send()

    def flow_plane(p):
        x = x_of(p)
        sx = [sb[s] * x for s in range(FACES)]
        scale = sb[30]

        def step(t, acc):
            off = pl.multiple_of(t * 256, 128)
            o = pl.ds(off, 256)
            ext = jnp.concatenate([distv[p, :, o], hr[0, p, :, o], hr[1, p, :, o], jnp.zeros((8, 256), F32)], axis=0)
            picked = jnp.dot(lhs[...], jnp.concatenate(split2(ext), axis=0), preferred_element_type=F32)
            for j in range(2):
                o = pl.ds(off + 128 * j, 128)
                dd, yy, zz = distv[p, :, o], yt[:, o], zt[:, o]
                out_sum, in_sum = None, None
                for s in range(FACES):
                    w = sx[s] + sb[6 + s] * yy + sb[12 + s] * zz
                    up = jnp.maximum(w, 0.0)
                    term = (w - up) * picked[16 * s : 16 * s + 16, 128 * j : 128 * j + 128]
                    out_sum = up if s == 0 else out_sum + up
                    in_sum = term if s == 0 else in_sum + term
                f = dd - scale * (out_sum * dd + in_sum)
                pb[p, :, o] = f
                for i, part in enumerate(split3(f)):
                    pm[pl.ds(pl.multiple_of((i * PLANES + p) * CELLS, CELLS), CELLS), o] = part
            return acc

        lax.fori_loop(0, FLAT // 256, step, 0, unroll=True)

    for step, p in enumerate(order):

        @pl.when(has_below)
        def _():
            halo(1, p, space + 1).wait_recv()

        @pl.when(has_above)
        def _():
            halo(0, p, space - 1).wait_recv()

        flow_plane(p)
        if step == 0:
            send_far(True, 0)
            send_far(False, 1)
        else:

            @pl.when(p == PLANES - 1)
            def _():
                send_far(True, 1)

            @pl.when(p == 0)
            def _():
                send_far(False, 0)

    rows = PLANES * CELLS
    flow = jnp.dot(pm[...], wts[...], preferred_element_type=F32)
    flow = flow[0:rows] + flow[rows : 2 * rows] + flow[2 * rows :]

    flux = total(fsend, frecv, f_ssem, f_rsem)
    ratio = spread(flux[:, 0:128] / jnp.where(flux[:, 128:256] > 0.0, flux[:, 128:256], 1.0), columns(mat, 0, 6))
    for s in range(FACES):
        sb[18 + s] = jnp.where(sb[24 + s] > 0.5, -sb[30] * ratio[:, 128 * s : 128 * s + 128], 0.0)

    def wall_planes(off, planes):
        o = pl.ds(off, 128)
        yy, zz, mm = yt[:, o], zt[:, o], mt[:, o]
        sums = [None] * len(planes)
        for s in range(FACES):
            along = sb[6 + s] * yy + sb[12 + s] * zz
            for i, p in enumerate(planes):
                term = jnp.minimum(sb[s] * xs[p] + along, 0.0) * sb[18 + s]
                sums[i] = term if s == 0 else sums[i] + term
        return [sums[i] * (mm * mx[p]) for i, p in enumerate(planes)]

    acc = []
    for p in range(PLANES):
        plane = flow[CELLS * p : CELLS * p + CELLS]
        for s in range(FACES):
            at = (s * PLANES + p) * CELLS
            plane = plane + sb[18 + s] * fq[at : at + CELLS, :]
        acc.append(plane)
    acc = jnp.concatenate(acc, axis=0)
    acc = acc + pltpu.roll(acc, 64, 1)
    kinds = mat[28 * 128 : 28 * 128 + 16, :].astype(F32)
    sent = None
    for p in range(PLANES):
        weight = kinds[0:1] + kinds[1:2] * xs[p] + kinds[2:3] * (xs[p] * xs[p])
        if p == 0:
            weight = weight + kinds[3:4] * jnp.where(has_left, 0.0, 1.0)
        if p == PLANES - 1:
            weight = weight + kinds[3:4] * jnp.where(has_right, 0.0, 1.0)
        term = weight * acc[CELLS * p : CELLS * p + CELLS]
        sent = term if p == 0 else sent + term

    lane8 = lax.broadcasted_iota(jnp.int32, (8, 128), 1)
    for half in range(2):
        own = jnp.where(lane8 < 16, sent[8 * half : 8 * half + 8], 0.0)
        asend[half : half + 1, :] = jnp.sum(pltpu.roll(own, 0, 1, stride=16, stride_axis=0), axis=0, keepdims=True)
    for d in FAR_FIRST:
        gather_copy(asend, arecv, m_ssem, m_rsem, d).start()

    def along_copy(buf, k, d, to):
        return pltpu.make_async_remote_copy(
            src_ref=buf.at[0], dst_ref=buf.at[d], send_sem=b_ssem.at[k, d], recv_sem=b_rsem.at[k, d],
            device_id=(space, to), device_id_type=MESH,
        )

    def y_copy(d):
        return along_copy(yrecv, 0, d, z_at * LANES + lax.rem(y_at + d, LANES))

    def z_copy(d):
        return along_copy(zrecv, 1, d, lax.rem(z_at + d, LANES) * LANES + y_at)

    yrecv[0] = jnp.where(lane8 < 64, sent[0:8], sent[8:16])
    for d in (2, 1, 3):
        y_copy(d).start()

    def add_walls(t, acc):
        off = pl.multiple_of(t * 128, 128)
        walls = wall_planes(off, range(PLANES))
        for p in range(PLANES):
            fa[p + 2, :, pl.ds(off + MARGIN, 128)] = pb[p, :, pl.ds(off, 128)] + walls[p]
        return acc


    halo_planes = (-2, -1, PLANES, PLANES + 1)

    def halo_walls(t, acc):
        off = pl.multiple_of(t * 128, 128)
        walls = wall_planes(off, halo_planes)
        for i in range(4):
            wb[i, :, pl.ds(off, 128)] = walls[i]
        return acc

    pass_on()
    send_near()
    for d in range(1, LANES):
        y_copy(d).wait_recv()
    zrecv[0] = (yrecv[0] + yrecv[1]) + (yrecv[2] + yrecv[3])
    for d in (2, 1, 3):
        z_copy(d).start()
    lax.fori_loop(0, FLAT // 128, add_walls, 0, unroll=3)
    lax.fori_loop(0, FLAT // 128, halo_walls, 0, unroll=3)

    def coefficients(allm):
        m = [allm[:, 128 * i : 128 * i + 128] for i in range(10)]
        inv = 1.0 / m[0]
        ux, uy, uz = m[1] * inv, m[2] * inv, m[3] * inv
        cxx, cyy, czz = m[4] * inv - ux * ux, m[5] * inv - uy * uy, m[6] * inv - uz * uz
        cxy, cxz, cyz = m[7] * inv - ux * uy, m[8] * inv - ux * uz, m[9] * inv - uy * uz
        theta = (cxx + cyy + czz) / 3.0
        a = (RATE * STEP**3) * m[0] * jnp.exp(0.19 * jnp.log(theta))
        lx, ly, lz = 0.5 * (theta + cxx), 0.5 * (theta + cyy), 0.5 * (theta + czz)
        terms = (a, -a * ux, -a * uy, -a * uz, a * lx, a * ly, a * lz, 0.5 * a * cxy, 0.5 * a * cxz, 0.5 * a * cyz)
        return terms, dict(
            ux=ux, a=a, k0=1.0 - 32.0 * a * (lx + ly + lz), lx=16.0 * a * lx,
            ys=a * (16.0 * ly + 0.5), a2=2.0 * a, a2uy=2.0 * a * uy, a2uz=2.0 * a * uz, zq=16.0 * a * lz,
            gxy=4.0 * a * cxy, gxz=4.0 * a * cxz, gyz=4.0 * a * cyz,
        )

    lane = lax.broadcasted_iota(jnp.int32, (CELLS, 128), 1)
    cell = lax.broadcasted_iota(jnp.int32, (CELLS, 128), 0)
    moments = total(asend, arecv, m_ssem, m_rsem)
    moments = jnp.concatenate([jnp.broadcast_to(moments[half : half + 1], (8, 128)) for half in range(2)], axis=0)
    moments = jnp.where((lane >> 4) == (cell & 7), moments, 0.0)
    terms, c1 = coefficients(times(moments, columns(mat, 6, 10)))

    def second_coefficients():
        for d in range(1, LANES):
            z_copy(d).wait_recv()
        packed = (zrecv[0] + zrecv[1]) + (zrecv[2] + zrecv[3])

        def unpack(x):
            return jnp.concatenate([x, pltpu.roll(x, 64, 1)], axis=0)

        on_face = (lane >= AT_FACE) & (lane < 64)
        least = unpack(zrecv[z_at])
        largest = unpack(zrecv[lax.rem(z_at + 1, LANES)])
        sums = jnp.where(lane < AT_FACE, unpack(packed), jnp.where(on_face, least, 0.0))
        sums = sums + pltpu.roll(jnp.where(on_face, largest, 0.0), len(X_FACE), 1)
        factor = jnp.where(lane < 110, 1.0, 0.0)
        for t in range(10):
            factor = jnp.where((lane >= 10 * t) & (lane < 10 * t + 10), terms[t], factor)
        stencil = times(sums, columns(mat, 26, 2))
        return coefficients(times(factor * (stencil[:, 0:128] + stencil[:, 128:256]), columns(mat, 16, 10)))[1]

    width = FLAT

    def lane_factors(k, c):
        a2, a2uy, a2uz, zq = (rep(c[q], FLAT // 128) for q in ("a2", "a2uy", "a2uz", "zq"))
        drift = a2 * zt[...] - a2uz
        lf[k, 0] = a2 * yt[...] - a2uy
        lf[k, 1] = zq + drift
        lf[k, 2] = zq - drift

    def relax_plane(src, at, dst, dst_at, p, c, k):
        n = width // 128
        margin = MARGIN if dst.shape[-1] == WIDE else 0
        x = x_of(p)
        drift_n = c["a2"] * (x + STEP - c["ux"]) + c["lx"]
        drift_p = c["lx"] - c["a2"] * (x - STEP - c["ux"])
        kn, kp, k0 = rep(drift_n, n), rep(drift_p, n), rep(c["k0"], n)
        ys, gxy, gxz, gyz = (rep(c[q], n) for q in ("ys", "gxy", "gxz", "gyz"))

        def step(t, acc):
            off = pl.multiple_of(t * width, 128)
            win = pl.ds(off, width + 2 * MARGIN)
            cen = pl.ds(off, width)
            cw, nw, pw = src[at, :, win], src[at + 1, :, win], src[at - 1, :, win]
            xw = nw - pw
            total_w = width + 2 * MARGIN

            def up(v):
                return pltpu.roll(v, total_w - NV, 1)[:, MARGIN : MARGIN + width]

            def down(v):
                return pltpu.roll(v, NV, 1)[:, MARGIN : MARGIN + width]

            cc, nn, pp = (v[:, MARGIN : MARGIN + width] for v in (cw, nw, pw))
            u, d = up(cw), down(cw)
            diff = u - d
            res = k0 * cc + kn * nn + kp * pp
            res = res + ys * (u + d) + lf[k, 0, :, cen] * diff + gxy * (up(xw) - down(xw))
            cross = gxz * (nn - pp) + gyz * diff
            plus = lf[k, 1, :, cen] * cc + cross
            minus = lf[k, 2, :, cen] * cc - cross
            res = res + kt[0, :, cen] * pltpu.roll(plus, width - 1, 1)
            res = res + kt[1, :, cen] * pltpu.roll(minus, 1, 1)
            dst[dst_at, :, pl.ds(off + margin, width)] = res
            return acc

        lax.fori_loop(0, FLAT // width, step, 0, unroll=True)

    lane_factors(0, c1)
    relax_plane(fa, 3, fb, 2, 1, c1, 0)

    def edge(right):
        return jnp.where(right, PLANES + 1, 2)

    def relax_side(right):
        left = jnp.logical_not(right)
        recv_planes(True, left)
        recv_planes(False, right)
        arrived = jnp.where(right, PLANES + 2, 0)
        walls = jnp.where(right, 2, 0)
        halo_at = jnp.where(right, PLANES + 2, 1)

        @pl.when((right & has_right) | (left & has_left))
        def _():
            for i in range(2):
                fa[arrived + i, :, MARGIN : MARGIN + FLAT] = fa[arrived + i, :, MARGIN : MARGIN + FLAT] + wb[walls + i]
            relax_plane(fa, halo_at, fb, halo_at - 1, halo_at - 2, c1, 0)

        relax_plane(fa, edge(right), fb, edge(right) - 1, edge(right) - 2, c1, 0)

    def relax_again(right):
        relax_plane(fb, edge(right) - 1, out, edge(right) - 2, edge(right) - 2, c2, 1)

    right_first = y_at == 0
    right_last = jnp.logical_not(right_first)
    relax_side(right_first)
    relax_side(right_last)
    c2 = second_coefficients()
    lane_factors(1, c2)
    relax_again(right_first)
    relax_again(right_last)
    relax_plane(fb, 2, out, 1, 1, c2, 1)

    @pl.when(has_above)
    def _():
        for p in range(PLANES):
            halo(1, p, space + 1).wait_send()

    @pl.when(has_below)
    def _():
        for p in range(PLANES):
            halo(0, p, space - 1).wait_send()

    for d in range(1, VELS):
        gather_copy(fsend, frecv, f_ssem, f_rsem, d).wait_send()
        gather_copy(asend, arecv, m_ssem, m_rsem, d).wait_send()
    for d in range(1, LANES):
        y_copy(d).wait_send()
        z_copy(d).wait_send()
    end_planes()


def body(distribution, freestream, face_area, cell_volume, neighbours, wall_flags, send_cells):
    dma = pltpu.SemaphoreType.DMA
    hbm = pl.BlockSpec(memory_space=pltpu.HBM)
    new = pl.pallas_call(
        kernel,
        out_shape=pltpu.VMEM((PLANES, CELLS, FLAT), F32),
        in_specs=[hbm] * 9,
        out_specs=pl.BlockSpec(memory_space=pltpu.VMEM),
        scratch_shapes=[
            pltpu.VMEM((PLANES, FLAT), F32),
            pltpu.VMEM((3, FACES, CELLS), F32),
            pltpu.VMEM((1, CELLS), F32),
            pltpu.VMEM((FACES, CELLS), jnp.int32),
            pltpu.VMEM((FACES, CELLS), jnp.int32),
            pltpu.SMEM((2, HALO), jnp.int32),
            pltpu.VMEM((PLANES, CELLS, FLAT), F32),
            pltpu.VMEM((2, PLANES, HALO, FLAT), F32),
            pltpu.VMEM((2, PLANES, HALO, FLAT), F32),
            pltpu.VMEM((FLAT, 128), BF16),
            pltpu.VMEM((28 * 128 + 16, 128), BF16),
            pltpu.VMEM((PLANES, CELLS, FLAT), F32),
            pltpu.VMEM((PLANES + 4, CELLS, WIDE), F32),
            pltpu.VMEM((4, CELLS, FLAT), F32),
            pltpu.VMEM((PLANES + 2, CELLS, WIDE), F32),
            pltpu.VMEM((2, 2, CELLS, 4 * 128), F32),
            pltpu.VMEM((2 * FACES * PLANES * CELLS, FLAT), BF16),
            pltpu.VMEM((FACES * PLANES * CELLS, 128), F32),
            pltpu.VMEM((3 * PLANES * CELLS, FLAT), BF16),
            pltpu.VMEM((CELLS, FLAT), F32),
            pltpu.VMEM((CELLS, FLAT), F32),
            pltpu.VMEM((CELLS, FLAT), F32),
            pltpu.VMEM((2, CELLS, FLAT), F32),
            pltpu.VMEM((2, 3, CELLS, FLAT), F32),
            pltpu.VMEM((32, 128), F32),
            pltpu.VMEM((32, CELLS, 128), F32),
            pltpu.VMEM((96, 64), BF16),
            pltpu.VMEM((1, 256), F32),
            pltpu.VMEM((VELS, 1, 256), F32),
            pltpu.VMEM((2, 128), F32),
            pltpu.VMEM((VELS, 2, 128), F32),
            pltpu.VMEM((LANES, 8, 128), F32),
            pltpu.VMEM((LANES, 8, 128), F32),
            dma((PLANES,)), dma((2, PLANES)), dma((2, PLANES)),
            dma((VELS,)), dma((VELS,)), dma((VELS,)), dma((VELS,)), dma((2, 2)), dma((2, 2)),
            dma((8,)), dma((2, LANES, 2)), dma((2, LANES, 2)), dma((2, 2)), dma((2, 2)),
            dma((2, LANES)), dma((2, LANES)),
        ],
        compiler_params=pltpu.CompilerParams(
            collective_id=0, has_side_effects=True, vmem_limit_bytes=56 * 1024 * 1024
        ),
    )(
        jnp.transpose(distribution, (1, 0, 2)), freestream, face_area, cell_volume.reshape(1, CELLS), neighbours,
        wall_flags, send_cells, jnp.asarray(sum_weights()), jnp.asarray(small_matrices()),
    )
    return jnp.transpose(new, (1, 0, 2))


def solution(mesh):
    in_specs = (
        P("space", "vel", None),
        P("vel", None),
        P(None, None, "space"),
        P("space"),
        P(None, "space"),
        P(None, "space"),
        P(None, "space"),
    )
    out_specs = P("space", "vel", None)
    return jax.shard_map(body, mesh=mesh, in_specs=in_specs, out_specs=out_specs, check_vma=False)
```
